32 devices in a mesh: gx: 8 (over z, x), st: 4 (over y, core).
Axes of the slice: x: 2, y: 2, z: 4, core: 2. Of those that a mesh axis runs over, the one named last changes fastest.
Arguments:
- checkpoint: float32 [26, 64, 32, 128], P(None, ('gx', 'st')), may hold values from -0.5 to 1, as said below
- adjoint_in: float32 [26, 64, 32, 128], P(None, 'gx', 'st'), may hold values from -6 to 6
- solid_mask: int32 [64, 32, 128], P('gx', 'st'), may hold values 0 or 1
- tile_map: int32 [64, 32], P('gx', 'st'), may hold values from 0 to 4095
- theta: float32 [4096], replicated, may hold values from 0.8 to 1.2
- first_moment: float32 [4096], replicated, may hold values from -6 to 6
- second_moment: float32 [4096], replicated, may hold values from 1 to 30
Outputs:
- adjoint_out: float32 [26, 64, 32, 128], P(None, 'gx', 'st')
- theta_new: float32 [4096], replicated
- first_new: float32 [4096], replicated
- second_new: float32 [4096], replicated
- nusselt: float32 [], replicated
The draws below stay inside these ranges and needn't reach their ends.
Inputs may be any that keep to these rules, and one draw needn't show every extreme that they name: `checkpoint`: populations near a local equilibrium; the flow populations of a cell sum to a density near 1.
All inputs are finite; a program needn't handle non-finite values. No bound on the sum of `solid_mask` on one device may be relied on, other than what follows from the above.
Results may differ from the reference program's by a relative error of at most 0.0001.
Values sent between devices are 32-bit elements; how exact they have to be, the bound alone decides.
A program may use at most 64 MiB of HBM per device.

```python
import math
import jax
import jax.numpy as jnp
import numpy as np
from jax import lax

NZ = 128
STEPS = 4
NTILE = 4096
ADAM_STEP = 100
NX = 64
NY = 32


VELOCITY = np.array([[0, 0, 0], [1, 0, 0], [-1, 0, 0], [0, 1, 0], [0, -1, 0], [0, 0, 1], [0, 0, -1], [1, 1, 0], [-1, -1, 0], [1, -1, 0], [-1, 1, 0], [1, 0, 1], [-1, 0, -1], [1, 0, -1], [-1, 0, 1], [0, 1, 1], [0, -1, -1], [0, 1, -1], [0, -1, 1], [0, 0, 0], [1, 0, 0], [-1, 0, 0], [0, 1, 0], [0, -1, 0], [0, 0, 1], [0, 0, -1]], dtype=np.int32)


WEIGHTS = np.array([1.0 / 3.0] + [1.0 / 18.0] * 6 + [1.0 / 36.0] * 12 + [0.25] + [0.125] * 6, dtype=np.float32)


def column_drawn(values):
    return jnp.asarray(values, jnp.float32).reshape(-1, 1, 1, 1)


def rough_noise(subkey, shape):
    return jax.random.truncated_normal(subkey, -3.0, 3.0, shape, jnp.float32)


def draw_checkpoint(key, part):
    keys = jax.random.split(key, 7)
    shape_cells = (NX, NY, NZ)
    position = jnp.arange(NX, dtype=jnp.float32) / max(NX - 1, 1)
    growth = 1.0 + 2.0 * position
    growth = growth[:, None, None]
    density = 1.0 + 0.02 * rough_noise(keys[0], shape_cells)
    speed_x = 0.03 * growth * rough_noise(keys[1], shape_cells)
    speed_y = 0.03 * growth * rough_noise(keys[2], shape_cells)
    base_z = rough_noise(keys[3], shape_cells)
    speed_z = 0.03 * growth * base_z
    temper = 0.5 + 0.03 * growth * (0.6 * base_z + 0.8 * rough_noise(keys[4], shape_cells))
    projected = column_drawn(VELOCITY[:19, 0]) * speed_x + column_drawn(VELOCITY[:19, 1]) * speed_y + column_drawn(VELOCITY[:19, 2]) * speed_z
    square_speed = speed_x * speed_x + speed_y * speed_y + speed_z * speed_z
    flow_part = column_drawn(WEIGHTS[:19]) * (density + 3.0 * projected + 4.5 * projected * projected - 1.5 * square_speed)
    flow_part = flow_part + column_drawn(WEIGHTS[:19]) * 0.02 * rough_noise(keys[5], (19,) + shape_cells)
    heat_proj = column_drawn(VELOCITY[19:, 0]) * speed_x + column_drawn(VELOCITY[19:, 1]) * speed_y + column_drawn(VELOCITY[19:, 2]) * speed_z
    heat_part = column_drawn(WEIGHTS[19:]) * temper * (1.0 + 4.0 * heat_proj)
    heat_part = heat_part + column_drawn(WEIGHTS[19:]) * 0.02 * rough_noise(keys[6], (7,) + shape_cells)
    return jnp.concatenate([flow_part, heat_part], 0).astype(jnp.float32)


def plant(values, stream_key, least, largest):
    shape = values.shape
    place = [jax.random.randint(jax.random.fold_in(stream_key, axis), (), 0, shape[axis]) for axis in range(len(shape))]
    values = values.at[tuple(place)].set(least)
    longest = shape.index(max(shape))
    place[longest] = (place[longest] + 1) % shape[longest]
    return values.at[tuple(place)].set(largest)


def level_of(key, extent, cuts, smallest, largest):
    gain = 1.0
    for dim, blocks in cuts:
        heights = jax.random.uniform(jax.random.fold_in(jax.random.fold_in(key, 6), dim), (blocks,), jnp.float32, smallest / len(cuts), largest / len(cuts))
        gain = gain * jnp.repeat(jnp.exp(heights), extent[dim] // blocks).reshape((-1,) + (1,) * (len(extent) - 1 - dim))
    return gain


def bell_draw(stream_key, dims, width, limit, shards=(), kind=jnp.bfloat16):
    values = width * jax.random.normal(stream_key, dims, jnp.float32)
    if shards:
        values = values * level_of(stream_key, dims, shards, -0.22, 0.18)
    return jnp.clip(values, -limit, limit).astype(kind)


def setup_inputs(seed: int = 0) -> dict:
    seeds = jax.random.split(jax.random.key(seed), 8)
    checkpoint = draw_checkpoint(jax.random.fold_in(seeds[7], 71), 0)
    adjoint_in = bell_draw(seeds[1], (26, NX, NY, NZ), 1.0, 6.0, ((1, 8), (2, 4)), jnp.float32)
    solid_mask = plant((jax.random.randint(seeds[2], (NX, NY, NZ), 0, 8) < 1).astype(jnp.int32), jax.random.fold_in(seeds[2], 1), 0, 1)
    tile_map = plant(jax.random.randint(seeds[3], (NX, NY), 0, NTILE), jax.random.fold_in(seeds[3], 1), 0, NTILE - 1).astype(jnp.int32)
    theta = jnp.clip(jax.random.uniform(seeds[4], (NTILE,), jnp.float32, 0.8, 1.2), 0.8, 1.2)
    first_moment = bell_draw(seeds[5], (NTILE,), 1.0, 6.0, (), jnp.float32)
    second_moment = jnp.clip(jnp.exp(jax.random.uniform(seeds[6], (NTILE,), jnp.float32, math.log(1.0), math.log(30.0))), 1.0, 30.0)
    return dict(checkpoint=checkpoint, adjoint_in=adjoint_in, solid_mask=solid_mask, tile_map=tile_map, theta=theta, first_moment=first_moment, second_moment=second_moment)


VELOCITY = np.array([[0, 0, 0], [1, 0, 0], [-1, 0, 0], [0, 1, 0], [0, -1, 0], [0, 0, 1], [0, 0, -1], [1, 1, 0], [-1, -1, 0], [1, -1, 0], [-1, 1, 0], [1, 0, 1], [-1, 0, -1], [1, 0, -1], [-1, 0, 1], [0, 1, 1], [0, -1, -1], [0, 1, -1], [0, -1, 1], [0, 0, 0], [1, 0, 0], [-1, 0, 0], [0, 1, 0], [0, -1, 0], [0, 0, 1], [0, 0, -1]], dtype=np.int32)
WEIGHTS = np.array([1.0 / 3.0] + [1.0 / 18.0] * 6 + [1.0 / 36.0] * 12 + [0.25] + [0.125] * 6, dtype=np.float32)
OPPOSITE = np.array([0, 2, 1, 4, 3, 6, 5, 8, 7, 10, 9, 12, 11, 14, 13, 16, 15, 18, 17, 19, 21, 20, 23, 22, 25, 24], dtype=np.int32)
TAU_FLOW = 0.8
TAU_HEAT = 0.8
BUOYANCY = 0.001
MEAN_TEMP = 0.5
KAPPA = 0.075
rising_heat = 24
LEARN_RATE = 0.05
BETA_ONE = 0.9
BETA_TWO = 0.99
ADAM_EPS = 1e-08

def column(values):
    return jnp.asarray(values, jnp.float32).reshape(-1, 1, 1, 1)

def collide(populations):
    flow_part = populations[:19]
    heat_part = populations[19:]
    density = lax.optimization_barrier(jnp.sum(flow_part, 0))
    speed_x = lax.optimization_barrier(jnp.sum(flow_part * column(VELOCITY[:19, 0]), 0))
    speed_y = lax.optimization_barrier(jnp.sum(flow_part * column(VELOCITY[:19, 1]), 0))
    speed_z = lax.optimization_barrier(jnp.sum(flow_part * column(VELOCITY[:19, 2]), 0))
    temper = lax.optimization_barrier(jnp.sum(heat_part, 0))
    forced_z = speed_z + TAU_FLOW * BUOYANCY * (temper - MEAN_TEMP)
    projected = column(VELOCITY[:19, 0]) * speed_x + column(VELOCITY[:19, 1]) * speed_y + column(VELOCITY[:19, 2]) * forced_z
    square_speed = speed_x * speed_x + speed_y * speed_y + forced_z * forced_z
    equilibrium = column(WEIGHTS[:19]) * (density + 3.0 * projected + 4.5 * projected * projected - 1.5 * square_speed)
    flow_post = flow_part - (flow_part - equilibrium) / TAU_FLOW
    heat_proj = column(VELOCITY[19:, 0]) * speed_x + column(VELOCITY[19:, 1]) * speed_y + column(VELOCITY[19:, 2]) * speed_z
    heat_equil = column(WEIGHTS[19:]) * temper * (1.0 + 4.0 * heat_proj)
    heat_post = heat_part - (heat_part - heat_equil) / TAU_HEAT
    return jnp.concatenate([flow_post, heat_post], 0)

def shift_depth(field, step_z):
    if step_z == 1:
        return jnp.concatenate([jnp.zeros_like(field[..., :1]), field[..., :-1]], -1)
    if step_z == -1:
        return jnp.concatenate([field[..., 1:], jnp.zeros_like(field[..., :1])], -1)
    return field

def bounce_table(solid_mask):
    solid_cells = solid_mask.astype(jnp.float32)
    padded = jnp.pad(solid_cells, ((0, 0), (0, 0), (1, 1)), constant_values=1.0)
    wall_layer = jnp.pad(jnp.zeros_like(solid_cells), ((0, 0), (0, 0), (1, 1)), constant_values=1.0)
    depth_cells = solid_cells.shape[2]
    sources = []
    for component in range(26):
        step_x = int(VELOCITY[component, 0])
        step_y = int(VELOCITY[component, 1])
        step_z = int(VELOCITY[component, 2])
        source = jnp.roll(padded, (step_x, step_y), axis=(0, 1))[:, :, 1 - step_z:1 - step_z + depth_cells]
        if component >= 19:
            source = source - 2.0 * wall_layer[:, :, 1 - step_z:1 - step_z + depth_cells]
        sources.append(source)
    return jnp.stack(sources)

def pull_all(field, velocity):
    pieces = []
    for component in range(26):
        step_x = int(velocity[component, 0])
        step_y = int(velocity[component, 1])
        step_z = int(velocity[component, 2])
        shifted = jnp.roll(field[component], (step_x, step_y), axis=(0, 1))
        pieces.append(shift_depth(shifted, step_z))
    return jnp.stack(pieces)

def propagate(collided, bounce, plate_temp):
    kept_share = 1.0 - jnp.abs(bounce)
    result = kept_share * pull_all(collided, VELOCITY) + bounce * collided[OPPOSITE]
    return result.at[rising_heat, :, :, 0].add(0.25 * plate_temp)

def propagate_adjoint(adjoint, bounce):
    kept_share = 1.0 - jnp.abs(bounce)
    return pull_all(kept_share * adjoint, -VELOCITY) + (bounce * adjoint)[OPPOSITE]

def flux_seed(populations, fluid):
    speed_z = lax.optimization_barrier(jnp.sum(populations[:19] * column(VELOCITY[:19, 2]), 0))
    temper = lax.optimization_barrier(jnp.sum(populations[19:], 0))
    flow_seed = fluid * column(VELOCITY[:19, 2]) * temper
    heat_seed = jnp.broadcast_to(fluid * speed_z, (7,) + speed_z.shape)
    return (speed_z, temper, jnp.concatenate([flow_seed, heat_seed], 0))

def adam_update(theta, first_moment, second_moment, tile_grad):
    first_new = BETA_ONE * first_moment + (1.0 - BETA_ONE) * tile_grad
    second_new = BETA_TWO * second_moment + (1.0 - BETA_TWO) * tile_grad * tile_grad
    first_hat = first_new / (1.0 - BETA_ONE ** ADAM_STEP)
    second_hat = second_new / (1.0 - BETA_TWO ** ADAM_STEP)
    theta_new = theta - LEARN_RATE * first_hat / (jnp.sqrt(second_hat) + ADAM_EPS)
    return (theta_new, first_new, second_new)

def reference(checkpoint, adjoint_in, solid_mask, tile_map, theta, first_moment, second_moment):
    bounce = bounce_table(solid_mask)
    plate_temp = theta[tile_map]
    fluid = 1.0 - solid_mask.astype(jnp.float32)
    current = checkpoint
    stored = []
    for counter in range(STEPS):
        stored.append(current)
        current = propagate(collide(current), bounce, plate_temp)
    speed_z, temper, seed_field = flux_seed(current, fluid)
    heat_sum = jnp.sum(fluid * speed_z * temper)
    nusselt = 1.0 + heat_sum / (KAPPA * solid_mask.shape[0] * solid_mask.shape[1])
    adjoint = adjoint_in + (nusselt - 1.0) * seed_field
    plate_grad = jnp.zeros(plate_temp.shape, jnp.float32)
    for counter in range(STEPS - 1, -1, -1):
        plate_grad = plate_grad + 0.25 * adjoint[rising_heat, :, :, 0]
        spread = propagate_adjoint(adjoint, bounce)
        adjoint = jax.vjp(collide, stored[counter])[1](spread)[0]
    tile_grad = jax.ops.segment_sum(plate_grad.reshape(-1), tile_map.reshape(-1), num_segments=NTILE)
    theta_new, first_new, second_new = adam_update(theta, first_moment, second_moment, tile_grad)
    return (adjoint, theta_new, first_new, second_new, nusselt)
```

```python
import functools

import jax
import jax.numpy as jnp
import numpy as np
from jax import lax
from jax.experimental import pallas as pl
from jax.experimental.pallas import tpu as pltpu
from jax.sharding import PartitionSpec as P

STEPS = 4
ADAM_STEP = 100

VELOCITY = [
    (0, 0, 0), (1, 0, 0), (-1, 0, 0), (0, 1, 0), (0, -1, 0), (0, 0, 1), (0, 0, -1),
    (1, 1, 0), (-1, -1, 0), (1, -1, 0), (-1, 1, 0), (1, 0, 1), (-1, 0, -1), (1, 0, -1),
    (-1, 0, 1), (0, 1, 1), (0, -1, -1), (0, 1, -1), (0, -1, 1),
    (0, 0, 0), (1, 0, 0), (-1, 0, 0), (0, 1, 0), (0, -1, 0), (0, 0, 1), (0, 0, -1),
]
WEIGHTS = [1.0 / 3.0] + [1.0 / 18.0] * 6 + [1.0 / 36.0] * 12 + [0.25] + [0.125] * 6
OPPOSITE = [0, 2, 1, 4, 3, 6, 5, 8, 7, 10, 9, 12, 11, 14, 13, 16, 15, 18, 17,
            19, 21, 20, 23, 22, 25, 24]
OMEGA = 1.25
LIFT = 0.8 * 0.001
MEAN_TEMP = 0.5
KAPPA = 0.075
RISING = 24
LEARN_RATE = 0.05
BETA_ONE = 0.9
BETA_TWO = 0.99
ADAM_EPS = 1e-08
MESH = pl.DeviceIdType.MESH

X_UP = [i for i in range(26) if VELOCITY[i][0] == 1]
X_DOWN = [i for i in range(26) if VELOCITY[i][0] == -1]
Y_UP = [i for i in range(26) if VELOCITY[i][1] == 1]
Y_DOWN = [i for i in range(26) if VELOCITY[i][1] == -1]
FULL = [(1, 0, 0, 6), (-1, 0, 6, 6), (0, 1, 12, 6), (0, -1, 18, 6),
        (1, 1, 24, 1), (-1, -1, 25, 1), (1, -1, 26, 1), (-1, 1, 27, 1)]
SINGLE = [(1, 0, 0, 1), (-1, 0, 1, 1), (0, 1, 2, 1), (0, -1, 3, 1),
          (1, 1, 4, 1), (-1, -1, 5, 1), (1, -1, 6, 1), (-1, 1, 7, 1)]
FACES = [(1, 0, 0, 2), (-1, 0, 2, 2), (0, 1, 4, 2), (0, -1, 6, 2)]
ROUND_ADJ = STEPS
ROUNDS = 2 * STEPS


def same(i):
    return i


def opposite(i):
    return OPPOSITE[i]


def kernel(n_gx, n_st, planes,
           check_ref, adj_ref, solid_ref, map_ref, theta_ref, first_ref, second_ref,
           out_ref, theta_out, first_out, second_out, nu_out,
           start, adj, pop_a, pop_b, rim_a, rim_b, moments, table, plate, bed,
           msg_out, msg_in, flag_out, flag_in, seed_out, seed_in, seed,
           mask_x, mask_lo, mask_hi, tiles, heat, grads, low_hot, high_hot,
           msg_sent, msg_got, flag_sent, flag_got, seed_sent, seed_got,
           all_sent, all_got, check_sent, check_got, own_sem, adj_sem):
    bx, by, nz = solid_ref.shape
    gx = lax.axis_index("gx")
    st = lax.axis_index("st")
    n = n_gx * n_st
    me = gx * n_st + st
    pops = (pop_a, pop_b)
    rims = (rim_a, rim_b)
    sub = lax.broadcasted_iota(jnp.int32, (by, nz), 0)
    lane = lax.broadcasted_iota(jnp.int32, (by, nz), 1)

    own = pltpu.make_async_copy(
        check_ref.at[:, :, pl.ds(pl.multiple_of(st * by, by), by), :],
        start.at[:, pl.ds(st * planes, planes)], own_sem)
    own.start()
    adj_copy = pltpu.make_async_copy(adj_ref, adj, adj_sem)
    adj_copy.start()

    def device(offset):
        other = lax.rem(me + offset, n)
        return (other // n_st, lax.rem(other, n_st))

    barrier = pltpu.get_barrier_semaphore()

    @pl.loop(1, n)
    def _(offset):
        pl.semaphore_signal(barrier, inc=1, device_id=device(offset), device_id_type=MESH)

    pl.semaphore_wait(barrier, n - 1)

    def check_copy(step):
        other = lax.rem(st + step, n_st)
        return pltpu.make_async_remote_copy(
            src_ref=check_ref.at[:, :, pl.ds(pl.multiple_of(other * by, by), by), :],
            dst_ref=start.at[:, pl.ds(st * planes, planes)],
            send_sem=check_sent, recv_sem=check_got,
            device_id=(gx, other), device_id_type=MESH)

    for step in range(1, n_st):
        check_copy(step).start()

    def send(messages, out, into, sent, got):
        for dx, dy, first, count in messages:
            pltpu.make_async_remote_copy(
                src_ref=out.at[pl.ds(first, count)], dst_ref=into.at[pl.ds(first, count)],
                send_sem=sent, recv_sem=got,
                device_id=(lax.rem(gx + dx + n_gx, n_gx), lax.rem(st + dy + n_st, n_st)),
                device_id_type=MESH).start()

    def send_all(buf, k):
        @pl.loop(1, n)
        def _(offset):
            pltpu.make_async_remote_copy(
                src_ref=buf.at[0], dst_ref=buf.at[offset],
                send_sem=all_sent.at[k], recv_sem=all_got.at[k],
                device_id=device(offset), device_id_type=MESH).start()

    def wait_for(ref, sem):
        pltpu.make_async_copy(ref, ref, sem).wait()

    def flags(x, carry):
        value = solid_ref[x].astype(jnp.float32)
        mask_x[x + 1] = value
        flag_out[2, pl.ds(x, 1), :] = value[by - 1:by]
        flag_out[3, pl.ds(x, 1), :] = value[0:1]
        return carry

    lax.fori_loop(0, bx, flags, 0)
    flag_out[0] = mask_x[bx]
    flag_out[1] = mask_x[1]
    flag_out[4] = mask_x[bx]
    flag_out[5] = mask_x[1]
    flag_out[6] = mask_x[bx]
    flag_out[7] = mask_x[1]
    send(SINGLE, flag_out, flag_in, flag_sent, flag_got)

    cell_x = lax.broadcasted_iota(jnp.int32, (bx, nz), 0)
    cell_lane = lax.broadcasted_iota(jnp.int32, (bx, nz), 1)
    numbers = map_ref[...].astype(jnp.float32)
    row = jnp.zeros((bx, nz), jnp.float32)
    for y in range(by):
        row = row + jnp.where(cell_lane == bx * y + cell_x, numbers[:, y:y + 1] + 1.0, 0.0)
    tiles[0] = jnp.sum(row, 0, keepdims=True) - 1.0
    send_all(tiles, 0)

    def hot(index):
        number = tiles[index]
        high = jnp.floor(number * (1.0 / nz))
        low = number - high * nz
        rows = theta_ref.shape[0]
        high_eq = lax.broadcasted_iota(jnp.int32, (rows, nz), 0).astype(jnp.float32) == high
        low_eq = lax.broadcasted_iota(jnp.int32, (nz, nz), 0).astype(jnp.float32) == low
        return (jnp.where(high_eq, 1.0, 0.0), jnp.where(low_eq, 1.0, 0.0).astype(jnp.bfloat16))

    def split(value):
        one = value.astype(jnp.bfloat16)
        rest = value - one.astype(jnp.float32)
        two = rest.astype(jnp.bfloat16)
        three = (rest - two.astype(jnp.float32)).astype(jnp.bfloat16)
        return jnp.concatenate([one, two, three], 0)

    def add_up(value):
        third = value.shape[0] // 3
        return value[:third] + value[third:2 * third] + value[2 * third:]

    high, low = hot(0)
    high_hot[0] = high
    low_hot[0] = low
    picked = lax.dot_general(split(theta_ref[...]), low, (((1,), (0,)), ((), ())),
                             preferred_element_type=jnp.float32)
    temperature = jnp.sum(add_up(picked) * high, 0, keepdims=True)

    def lay_plate(x, carry):
        chosen = jnp.where(lane == bx * sub + x, temperature, 0.0)
        total = jnp.sum(chosen, 1, keepdims=True)
        plate[x] = jnp.where(lane == 0, 0.25 * total, 0.0)
        return carry

    lax.fori_loop(0, bx, lay_plate, 0)

    def pack_rows(r, which, values, x):
        for k, i in enumerate(Y_UP):
            msg_out[r, 12 + k, pl.ds(x, 1), :] = values(which(i))[by - 1:by]
        for k, i in enumerate(Y_DOWN):
            msg_out[r, 18 + k, pl.ds(x, 1), :] = values(which(i))[0:1]

    def pack_planes(r, which, last, first):
        for k, i in enumerate(X_UP):
            msg_out[r, k] = last(which(i))
        for k, i in enumerate(X_DOWN):
            msg_out[r, 6 + k] = first(which(i))
        msg_out[r, 24] = last(which(7))
        msg_out[r, 25] = first(which(8))
        msg_out[r, 26] = last(which(9))
        msg_out[r, 27] = first(which(10))

    def send_round(r):
        send(FULL, msg_out.at[r], msg_in.at[r], msg_sent.at[r], msg_got.at[r])

    def unpack(r, which, pop, rim, extra=None):
        def arrived(slot, i, side):
            value = msg_in[r, slot]
            return value if extra is None else value + extra(which(i), side)

        for k, i in enumerate(X_UP):
            pop[which(i), 0] = arrived(k, i, 0)
        for k, i in enumerate(X_DOWN):
            pop[which(i), bx + 1] = arrived(6 + k, i, 1)
        for k, i in enumerate(Y_UP):
            rim[which(i), 1:bx + 1, :] = arrived(12 + k, i, 2)
        for k, i in enumerate(Y_DOWN):
            rim[which(i), 1:bx + 1, :] = arrived(18 + k, i, 3)
        rim[which(7), 0:1, :] = msg_in[r, 24, by - 1:by, :]
        rim[which(8), bx + 1:bx + 2, :] = msg_in[r, 25, 0:1, :]
        rim[which(9), 0:1, :] = msg_in[r, 26, 0:1, :]
        rim[which(10), bx + 1:bx + 2, :] = msg_in[r, 27, by - 1:by, :]

    def turn(value, edge, step_y, step_z):
        if step_y == 1:
            value = jnp.where(sub == 0, edge, pltpu.roll(value, 1, 0))
        elif step_y == -1:
            value = jnp.where(sub == by - 1, edge, pltpu.roll(value, by - 1, 0))
        if step_z == 1:
            value = pltpu.roll(value, 1, 1)
        elif step_z == -1:
            value = pltpu.roll(value, nz - 1, 1)
        return value

    def pull(pop, rim, source, i, x):
        step_x, step_y, step_z = VELOCITY[i]
        edge = rim[source, pl.ds(x + 1 - step_x, 1), :] if step_y else None
        return turn(pop[source, x + 1 - step_x], edge, step_y, step_z)

    adj_copy.wait()

    def adj_rows(x, carry):
        pack_rows(ROUND_ADJ, opposite, lambda j: adj[j, x], x)
        return carry

    lax.fori_loop(0, bx, adj_rows, 0)
    pack_planes(ROUND_ADJ, opposite, lambda j: adj[j, bx - 1], lambda j: adj[j, 0])
    send_round(ROUND_ADJ)

    wait_for(flag_in, flag_got)
    mask_x[0] = flag_in[0]
    mask_x[bx + 1] = flag_in[1]
    mask_lo[1:bx + 1, :] = flag_in[2]
    mask_hi[1:bx + 1, :] = flag_in[3]
    mask_lo[0:1, :] = flag_in[4, by - 1:by, :]
    mask_hi[bx + 1:bx + 2, :] = flag_in[5, 0:1, :]
    mask_hi[0:1, :] = flag_in[6, 0:1, :]
    mask_lo[bx + 1:bx + 2, :] = flag_in[7, by - 1:by, :]

    def fill_table(x, carry):
        for i in range(1, 19):
            step_x, step_y, step_z = VELOCITY[i]
            edge = None
            if step_y:
                edge = (mask_lo if step_y == 1 else mask_hi)[pl.ds(x + 1 - step_x, 1), :]
            value = turn(mask_x[x + 1 - step_x], edge, step_y, step_z)
            if step_z:
                value = jnp.where(lane == (0 if step_z == 1 else nz - 1), 1.0, value)
            table[i, x] = value
        return carry

    lax.fori_loop(0, bx, fill_table, 0)

    def moments_of(s):
        def pairs(i):
            return s[i] + s[i + 1], s[i] - s[i + 1]

        p = {}
        m = {}
        for i in range(1, 19, 2):
            p[i], m[i] = pairs(i)
        density = s[0] + ((p[1] + p[3]) + (p[5] + p[7])) + ((p[9] + p[11]) + (p[13] + p[15])) + p[17]
        speed_x = (m[1] + m[7]) + (m[9] + m[11]) + m[13]
        speed_y = (m[3] + m[7]) + (m[15] + m[17]) - m[9]
        speed_z = (m[5] + m[11]) + (m[15] - m[17]) - m[13]
        temper = (s[19] + s[20]) + (s[21] + s[22]) + (s[23] + s[24]) + s[25]
        return density, speed_x, speed_y, speed_z, temper

    def along(c, a, b, d):
        total = None
        for step, value in zip(c, (a, b, d)):
            if step == 0:
                continue
            if total is None:
                total = value if step == 1 else -value
            else:
                total = total + value if step == 1 else total - value
        return total

    def collide(s, k, x):
        density, ux, uy, uz, temper = moments_of(s)
        moments[k, 0, x] = ux
        moments[k, 1, x] = uy
        moments[k, 2, x] = uz
        moments[k, 3, x] = temper
        vz = uz + LIFT * (temper - MEAN_TEMP)
        base = density - 1.5 * (ux * ux + uy * uy + vz * vz)
        post = [None] * 26
        post[0] = (1.0 - OMEGA) * s[0] + (OMEGA * WEIGHTS[0]) * base
        for i in range(1, 19, 2):
            cv = along(VELOCITY[i], ux, uy, vz)
            even = base + (4.5 * cv) * cv
            odd = 3.0 * cv
            weight = OMEGA * WEIGHTS[i]
            post[i] = (1.0 - OMEGA) * s[i] + weight * (even + odd)
            post[i + 1] = (1.0 - OMEGA) * s[i + 1] + weight * (even - odd)
        post[19] = (1.0 - OMEGA) * s[19] + (OMEGA * WEIGHTS[19]) * temper
        share = (OMEGA * WEIGHTS[20]) * temper
        for i, u in ((20, ux), (22, uy), (24, uz)):
            odd = (4.0 * u) * share
            post[i] = (1.0 - OMEGA) * s[i] + (share + odd)
            post[i + 1] = (1.0 - OMEGA) * s[i + 1] + (share - odd)
        return post

    def keep(pop, r, which, values, x):
        for i in range(26):
            pop[i, x + 1] = values[i]
        pack_rows(r, which, lambda j: values[j], x)

    def ship(pop, r, which):
        pack_planes(r, which, lambda j: pop[j, bx], lambda j: pop[j, 1])
        send_round(r)

    def propagated(pop, rim, x):
        result = [pop[0, x + 1]] + [None] * 25
        result[19] = pop[19, x + 1]
        for i in range(1, 26):
            if i == 19:
                continue
            solid = table[i if i < 19 else i - 19, x] > 0.5
            back = pop[OPPOSITE[i], x + 1]
            if i == 24:
                back = jnp.where(lane == 0, -back, back)
            elif i == 25:
                back = jnp.where(lane == nz - 1, -back, back)
            result[i] = jnp.where(solid, back, pull(pop, rim, i, i, x))
        result[RISING] = result[RISING] + plate[x]
        return result

    own.wait()
    wait_for(start.at[:, pl.ds(0, (n_st - 1) * planes)], check_got)

    def begin(x, carry):
        keep(pop_a, 0, same, collide([start[i, x] for i in range(26)], 0, x), x)
        return carry

    lax.fori_loop(0, bx, begin, 0)
    ship(pop_a, 0, same)

    wait_for(tiles.at[pl.ds(1, n - 1)], all_got.at[0])

    def fill_hot(index, carry):
        high, low = hot(index)
        high_hot[index] = high
        low_hot[index] = low
        return carry

    lax.fori_loop(1, n, fill_hot, 0)

    for k in range(1, STEPS):
        old, new = pops[(k - 1) % 2], pops[k % 2]
        rim = rims[(k - 1) % 2]
        wait_for(msg_in.at[k - 1], msg_got.at[k - 1])
        unpack(k - 1, same, old, rim)

        def advance(x, carry, old=old, new=new, rim=rim, k=k):
            keep(new, k, same, collide(propagated(old, rim, x), k, x), x)
            return carry

        lax.fori_loop(0, bx, advance, 0)
        ship(new, k, same)

    last, rim = pops[(STEPS - 1) % 2], rims[(STEPS - 1) % 2]
    wait_for(msg_in.at[STEPS - 1], msg_got.at[STEPS - 1])
    unpack(STEPS - 1, same, last, rim)

    def finish(x, total):
        _, _, _, uz, temper = moments_of(propagated(last, rim, x))
        fluid = 1.0 - mask_x[x + 1]
        warm = fluid * temper
        rise = fluid * uz
        seed[0, x] = warm
        seed[1, x] = rise
        seed_out[4, pl.ds(x, 1), :] = warm[by - 1:by]
        seed_out[5, pl.ds(x, 1), :] = rise[by - 1:by]
        seed_out[6, pl.ds(x, 1), :] = warm[0:1]
        seed_out[7, pl.ds(x, 1), :] = rise[0:1]
        return total + warm * uz

    flux = lax.fori_loop(0, bx, finish, jnp.zeros((by, nz), jnp.float32))
    heat[0] = jnp.sum(flux, 0, keepdims=True)
    send_all(heat, 1)
    seed_out[0] = seed[0, bx - 1]
    seed_out[1] = seed[1, bx - 1]
    seed_out[2] = seed[0, 0]
    seed_out[3] = seed[1, 0]
    send(FACES, seed_out, seed_in, seed_sent, seed_got)
    wait_for(msg_in.at[ROUND_ADJ], msg_got.at[ROUND_ADJ])
    wait_for(seed_in, seed_got)
    wait_for(heat.at[pl.ds(1, n - 1)], all_got.at[1])
    heat_sum = jnp.sum(jnp.sum(heat[...], 0), 1, keepdims=True)
    nusselt = 1.0 + heat_sum / (KAPPA * (bx * n_gx * by * n_st))
    nu_out[...] = nusselt
    gain = jnp.broadcast_to(nusselt - 1.0, (by, nz))

    def seeded(j, warm, rise):
        if j >= 19:
            return gain * rise
        if VELOCITY[j][2] == 0:
            return jnp.zeros((by, nz), jnp.float32)
        return gain * warm if VELOCITY[j][2] == 1 else -(gain * warm)

    def bed_of(value, x):
        return jnp.where(lane == bx * sub + x, 0.25 * value[:, 0:1], 0.0)

    def seed_adjoint(x, total):
        warm = seed[0, x]
        rise = seed[1, x]
        for j in range(26):
            value = adj[j, x] + seeded(j, warm, rise)
            pop_a[j, x + 1] = value
            if j == RISING:
                total = total + bed_of(value, x)
        return total

    total = lax.fori_loop(0, bx, seed_adjoint, jnp.zeros((by, nz), jnp.float32))
    unpack(ROUND_ADJ, opposite, pop_a, rim_a,
           lambda j, side: seeded(j, seed_in[2 * side], seed_in[2 * side + 1]))

    def pulled_back(pop, rim, x):
        fluid = 1.0 - mask_x[x + 1]
        above = jnp.where(lane == 0, 0.0, fluid)
        below = jnp.where(lane == nz - 1, 0.0, fluid)
        mu = [None] * 26
        mu[0] = pop[0, x + 1]
        mu[19] = pop[19, x + 1]
        for i in range(1, 26):
            if i == 19:
                continue
            step_z = VELOCITY[i][2]
            share = fluid if step_z == 0 else (above if step_z == 1 else below)
            bounce = table[i if i < 19 else i - 19, x]
            if i == 24:
                bounce = jnp.where(lane == 0, -1.0, bounce)
            elif i == 25:
                bounce = jnp.where(lane == nz - 1, -1.0, bounce)
            mu[OPPOSITE[i]] = share * pull(pop, rim, OPPOSITE[i], i, x) + bounce * pop[i, x + 1]
        return mu

    def collide_back(mu, k, x):
        ux = moments[k, 0, x]
        uy = moments[k, 1, x]
        uz = moments[k, 2, x]
        temper = moments[k, 3, x]
        vz = uz + LIFT * (temper - MEAN_TEMP)
        even = {}
        odd = {}
        for i in range(1, 19, 2):
            even[i] = mu[i] + mu[i + 1]
            odd[i] = mu[i] - mu[i + 1]
        axis = OMEGA * WEIGHTS[1]
        diag = OMEGA * WEIGHTS[7]
        xy = diag * (even[7] + even[9])
        xz = diag * (even[11] + even[13])
        yz = diag * (even[15] + even[17])
        ex, ey, ez = axis * even[1], axis * even[3], axis * even[5]
        zero = (OMEGA * WEIGHTS[0]) * mu[0] + ((ex + ey) + (ez + xy)) + (xz + yz)
        sxx = ex + (xy + xz)
        syy = ey + (xy + yz)
        szz = ez + (xz + yz)
        sxy = diag * (even[7] - even[9])
        sxz = diag * (even[11] - even[13])
        syz = diag * (even[15] - even[17])
        one_x = axis * odd[1] + diag * ((odd[7] + odd[9]) + (odd[11] + odd[13]))
        one_y = axis * odd[3] + diag * ((odd[7] - odd[9]) + (odd[15] + odd[17]))
        one_z = axis * odd[5] + diag * ((odd[11] - odd[13]) + (odd[15] - odd[17]))
        bar_x = 3.0 * (one_x - zero * ux) + 9.0 * (sxx * ux + sxy * uy + sxz * vz)
        bar_y = 3.0 * (one_y - zero * uy) + 9.0 * (sxy * ux + syy * uy + syz * vz)
        bar_z = 3.0 * (one_z - zero * vz) + 9.0 * (sxz * ux + syz * uy + szz * vz)
        share = OMEGA * WEIGHTS[20]
        hx = (4.0 * share) * (mu[20] - mu[21])
        hy = (4.0 * share) * (mu[22] - mu[23])
        hz = (4.0 * share) * (mu[24] - mu[25])
        warm = (OMEGA * WEIGHTS[19]) * mu[19] + share * (
            ((mu[20] + mu[21]) + (mu[22] + mu[23])) + (mu[24] + mu[25]))
        bar_t = warm + (hx * ux + hy * uy + hz * uz) + LIFT * bar_z
        bar_x = bar_x + temper * hx
        bar_y = bar_y + temper * hy
        bar_z = bar_z + temper * hz
        lam = [None] * 26
        lam[0] = (1.0 - OMEGA) * mu[0] + zero
        for i in range(1, 19, 2):
            cb = along(VELOCITY[i], bar_x, bar_y, bar_z)
            lam[i] = (1.0 - OMEGA) * mu[i] + (zero + cb)
            lam[i + 1] = (1.0 - OMEGA) * mu[i + 1] + (zero - cb)
        for i in range(19, 26):
            lam[i] = (1.0 - OMEGA) * mu[i] + bar_t
        return lam

    for step in range(STEPS - 1):
        old, new = pops[step % 2], pops[(step + 1) % 2]
        rim = rims[step % 2]
        k = STEPS - 1 - step
        r = ROUND_ADJ + step
        if step:
            wait_for(msg_in.at[r], msg_got.at[r])
            unpack(r, opposite, old, rim)

        def retreat(x, total, old=old, new=new, rim=rim, k=k, r=r):
            lam = collide_back(pulled_back(old, rim, x), k, x)
            keep(new, r + 1, opposite, lam, x)
            return total + bed_of(lam[RISING], x)

        total = lax.fori_loop(0, bx, retreat, total)
        ship(new, r + 1, opposite)

    grads[0] = jnp.sum(total, 0, keepdims=True)
    send_all(grads, 2)

    old, rim = pops[(STEPS - 1) % 2], rims[(STEPS - 1) % 2]
    r = ROUND_ADJ + STEPS - 1
    wait_for(msg_in.at[r], msg_got.at[r])
    unpack(r, opposite, old, rim)

    def end(x, carry):
        lam = collide_back(pulled_back(old, rim, x), 0, x)
        for i in range(26):
            out_ref[i, x] = lam[i]
        return carry

    lax.fori_loop(0, bx, end, 0)

    wait_for(grads.at[pl.ds(1, n - 1)], all_got.at[2])
    rows = theta_ref.shape[0]
    unroll = 8 if n % 8 == 0 else 1

    def gather_tiles(chunk, total):
        for part in range(unroll):
            index = chunk * unroll + part
            weighted = split(high_hot[index] * grads[index])
            total = total + lax.dot_general(weighted, low_hot[index], (((1,), (1,)), ((), ())),
                                            preferred_element_type=jnp.float32)
        return total

    tile_grad = add_up(lax.fori_loop(0, n // unroll, gather_tiles,
                                     jnp.zeros((3 * rows, nz), jnp.float32)))
    first_new = BETA_ONE * first_ref[...] + (1.0 - BETA_ONE) * tile_grad
    second_new = BETA_TWO * second_ref[...] + (1.0 - BETA_TWO) * tile_grad * tile_grad
    first_hat = first_new / (1.0 - BETA_ONE**ADAM_STEP)
    second_hat = second_new / (1.0 - BETA_TWO**ADAM_STEP)
    first_out[...] = first_new
    second_out[...] = second_new
    theta_out[...] = theta_ref[...] - LEARN_RATE * first_hat / (jnp.sqrt(second_hat) + ADAM_EPS)

    wait_for(start.at[:, pl.ds(0, (n_st - 1) * planes)], check_sent)
    wait_for(flag_out, flag_sent)
    wait_for(seed_out, seed_sent)
    for r in range(ROUNDS):
        wait_for(msg_out.at[r], msg_sent.at[r])
    wait_for(tiles.at[pl.ds(1, n - 1)], all_sent.at[0])
    wait_for(heat.at[pl.ds(1, n - 1)], all_sent.at[1])
    wait_for(grads.at[pl.ds(1, n - 1)], all_sent.at[2])


def body(n_gx, n_st, checkpoint, adjoint_in, solid_mask, tile_map, theta, first_moment, second_moment):
    bx, by, nz = solid_mask.shape
    planes = checkpoint.shape[1]
    n = n_gx * n_st
    rows = theta.shape[0] // nz
    f32 = jnp.float32
    wide = 16
    vmem = pl.BlockSpec(memory_space=pltpu.VMEM)
    hbm = pl.BlockSpec(memory_space=pl.ANY)
    dma = pltpu.SemaphoreType.DMA
    out, theta_new, first_new, second_new, nusselt = pl.pallas_call(
        functools.partial(kernel, n_gx, n_st, planes),
        out_shape=(
            jax.ShapeDtypeStruct((26, bx, by, nz), f32),
            jax.ShapeDtypeStruct((rows, nz), f32),
            jax.ShapeDtypeStruct((rows, nz), f32),
            jax.ShapeDtypeStruct((rows, nz), f32),
            jax.ShapeDtypeStruct((1, 1), f32),
        ),
        in_specs=[hbm, hbm] + [vmem] * 5,
        out_specs=(vmem,) * 5,
        scratch_shapes=[
            pltpu.VMEM((26, bx, by, nz), f32),
            pltpu.VMEM((26, bx, by, nz), f32),
            pltpu.VMEM((26, bx + 2, by, nz), f32),
            pltpu.VMEM((26, bx + 2, by, nz), f32),
            pltpu.VMEM((26, wide, nz), f32),
            pltpu.VMEM((26, wide, nz), f32),
            pltpu.VMEM((STEPS, 4, bx, by, nz), f32),
            pltpu.VMEM((19, bx, by, nz), f32),
            pltpu.VMEM((bx, by, nz), f32),
            pltpu.VMEM((by, nz), f32),
            pltpu.VMEM((ROUNDS, 28, by, nz), f32),
            pltpu.VMEM((ROUNDS, 28, by, nz), f32),
            pltpu.VMEM((8, by, nz), f32),
            pltpu.VMEM((8, by, nz), f32),
            pltpu.VMEM((8, by, nz), f32),
            pltpu.VMEM((8, by, nz), f32),
            pltpu.VMEM((2, bx, by, nz), f32),
            pltpu.VMEM((bx + 2, by, nz), f32),
            pltpu.VMEM((wide, nz), f32),
            pltpu.VMEM((wide, nz), f32),
            pltpu.VMEM((n, 1, nz), f32),
            pltpu.VMEM((n, 1, nz), f32),
            pltpu.VMEM((n, 1, nz), f32),
            pltpu.VMEM((n, nz, nz), jnp.bfloat16),
            pltpu.VMEM((n, rows, nz), f32),
            dma((ROUNDS,)),
            dma((ROUNDS,)),
            dma,
            dma,
            dma,
            dma,
            dma((3,)),
            dma((3,)),
            dma,
            dma,
            dma,
            dma,
        ],
        compiler_params=pltpu.CompilerParams(
            collective_id=0, has_side_effects=True, vmem_limit_bytes=40 * 1024 * 1024),
        name="window",
    )(checkpoint, adjoint_in, solid_mask, tile_map, theta.reshape(rows, nz),
      first_moment.reshape(rows, nz), second_moment.reshape(rows, nz))
    flat = theta.shape
    return (out, theta_new.reshape(flat), first_new.reshape(flat), second_new.reshape(flat),
            nusselt.reshape(()))


def solution(mesh):
    return jax.shard_map(
        functools.partial(body, mesh.shape["gx"], mesh.shape["st"]),
        mesh=mesh,
        in_specs=(
            P(None, ("gx", "st"), None, None),
            P(None, "gx", "st", None),
            P("gx", "st", None),
            P("gx", "st"),
            P(),
            P(),
            P(),
        ),
        out_specs=(P(None, "gx", "st", None), P(), P(), P(), P()),
        check_vma=False,
    )
```

```python
import functools

import jax
import jax.numpy as jnp
import numpy as np
from jax import lax
from jax.experimental import pallas as pl
from jax.experimental.pallas import tpu as pltpu
from jax.sharding import PartitionSpec as P

STEPS = 4
ADAM_STEP = 100

VELOCITY = [
    (0, 0, 0), (1, 0, 0), (-1, 0, 0), (0, 1, 0), (0, -1, 0), (0, 0, 1), (0, 0, -1),
    (1, 1, 0), (-1, -1, 0), (1, -1, 0), (-1, 1, 0), (1, 0, 1), (-1, 0, -1), (1, 0, -1),
    (-1, 0, 1), (0, 1, 1), (0, -1, -1), (0, 1, -1), (0, -1, 1),
    (0, 0, 0), (1, 0, 0), (-1, 0, 0), (0, 1, 0), (0, -1, 0), (0, 0, 1), (0, 0, -1),
]
WEIGHTS = [1.0 / 3.0] + [1.0 / 18.0] * 6 + [1.0 / 36.0] * 12 + [0.25] + [0.125] * 6
OPPOSITE = [0, 2, 1, 4, 3, 6, 5, 8, 7, 10, 9, 12, 11, 14, 13, 16, 15, 18, 17,
            19, 21, 20, 23, 22, 25, 24]
OMEGA = 1.25
LIFT = 0.8 * 0.001
MEAN_TEMP = 0.5
KAPPA = 0.075
RISING = 24
LEARN_RATE = 0.05
BETA_ONE = 0.9
BETA_TWO = 0.99
ADAM_EPS = 1e-08
MESH = pl.DeviceIdType.MESH

X_UP = [i for i in range(26) if VELOCITY[i][0] == 1]
X_DOWN = [i for i in range(26) if VELOCITY[i][0] == -1]
Y_UP = [i for i in range(26) if VELOCITY[i][1] == 1]
Y_DOWN = [i for i in range(26) if VELOCITY[i][1] == -1]
FULL = [(1, 0, 0, 6), (-1, 0, 6, 6), (0, 1, 12, 6), (0, -1, 18, 6),
        (1, 1, 24, 1), (-1, -1, 25, 1), (1, -1, 26, 1), (-1, 1, 27, 1)]
SINGLE = [(1, 0, 0, 1), (-1, 0, 1, 1), (0, 1, 2, 1), (0, -1, 3, 1),
          (1, 1, 4, 1), (-1, -1, 5, 1), (1, -1, 6, 1), (-1, 1, 7, 1)]
FACES = [(1, 0, 0, 2), (-1, 0, 2, 2), (0, 1, 4, 2), (0, -1, 6, 2)]
ROUND_ADJ = STEPS
ROUNDS = 2 * STEPS


def same(i):
    return i


def opposite(i):
    return OPPOSITE[i]


def kernel(n_gx, n_st, planes,
           check_ref, adj_ref, solid_hbm, map_hbm, theta_hbm,
           out_ref, grad_out, nu_out,
           solid_ref, map_ref, theta_ref, start, adj, pop_a, pop_b, rim_a, rim_b, moments, table, plate,
           msg_out, msg_in, flag_out, flag_in, seed_out, seed_in, seed,
           mask_x, mask_lo, mask_hi, tiles, heat, grads, low_hot, high_hot,
           msg_sent, msg_got, flag_sent, flag_got, seed_sent, seed_got,
           all_sent, all_got, check_sent, check_got, own_sem, adj_sem, small_sem):
    bx, by, nz = solid_ref.shape
    gx = lax.axis_index("gx")
    st = lax.axis_index("st")
    n = n_gx * n_st
    me = gx * n_st + st
    pops = (pop_a, pop_b)
    rims = (rim_a, rim_b)
    sub = lax.broadcasted_iota(jnp.int32, (by, nz), 0)
    lane = lax.broadcasted_iota(jnp.int32, (by, nz), 1)

    own = pltpu.make_async_copy(
        check_ref.at[:, :, pl.ds(pl.multiple_of(st * by, by), by), :],
        start.at[:, pl.ds(st * planes, planes)], own_sem)
    own.start()
    adj_copy = pltpu.make_async_copy(adj_ref, adj, adj_sem)
    adj_copy.start()
    small = [pltpu.make_async_copy(source, into, small_sem.at[k]) for k, (source, into) in enumerate(
        ((solid_hbm, solid_ref), (map_hbm, map_ref), (theta_hbm, theta_ref)))]
    for copy in small:
        copy.start()

    def device(offset):
        other = lax.rem(me + offset, n)
        return (other // n_st, lax.rem(other, n_st))

    barrier = pltpu.get_barrier_semaphore()

    @pl.loop(1, n)
    def _(offset):
        pl.semaphore_signal(barrier, inc=1, device_id=device(offset), device_id_type=MESH)

    pl.semaphore_wait(barrier, n - 1)

    def check_copy(step):
        other = lax.rem(st + step, n_st)
        return pltpu.make_async_remote_copy(
            src_ref=check_ref.at[:, :, pl.ds(pl.multiple_of(other * by, by), by), :],
            dst_ref=start.at[:, pl.ds(st * planes, planes)],
            send_sem=check_sent, recv_sem=check_got,
            device_id=(gx, other), device_id_type=MESH)

    for step in range(1, n_st):
        check_copy(step).start()

    def send(messages, out, into, sent, got):
        for dx, dy, first, count in messages:
            pltpu.make_async_remote_copy(
                src_ref=out.at[pl.ds(first, count)], dst_ref=into.at[pl.ds(first, count)],
                send_sem=sent, recv_sem=got,
                device_id=(lax.rem(gx + dx + n_gx, n_gx), lax.rem(st + dy + n_st, n_st)),
                device_id_type=MESH).start()

    def send_all(buf, k):
        @pl.loop(1, n)
        def _(offset):
            pltpu.make_async_remote_copy(
                src_ref=buf.at[0], dst_ref=buf.at[offset],
                send_sem=all_sent.at[k], recv_sem=all_got.at[k],
                device_id=device(offset), device_id_type=MESH).start()

    def wait_for(ref, sem):
        pltpu.make_async_copy(ref, ref, sem).wait()

    for copy in small:
        copy.wait()

    def flags(x, carry):
        value = solid_ref[x].astype(jnp.float32)
        mask_x[x + 1] = value
        flag_out[2, pl.ds(x, 1), :] = value[by - 1:by]
        flag_out[3, pl.ds(x, 1), :] = value[0:1]
        return carry

    lax.fori_loop(0, bx, flags, 0)
    flag_out[0] = mask_x[bx]
    flag_out[1] = mask_x[1]
    flag_out[4] = mask_x[bx]
    flag_out[5] = mask_x[1]
    flag_out[6] = mask_x[bx]
    flag_out[7] = mask_x[1]
    send(SINGLE, flag_out, flag_in, flag_sent, flag_got)

    cell_x = lax.broadcasted_iota(jnp.int32, (bx, nz), 0)
    cell_lane = lax.broadcasted_iota(jnp.int32, (bx, nz), 1)
    numbers = map_ref[...].astype(jnp.float32)
    row = jnp.zeros((bx, nz), jnp.float32)
    for y in range(by):
        row = row + jnp.where(cell_lane == bx * y + cell_x, numbers[:, y:y + 1] + 1.0, 0.0)
    tiles[0] = jnp.sum(row, 0, keepdims=True)
    send_all(tiles, 0)

    def joined(buf, pair):
        return buf[2 * pair] + pltpu.roll(buf[2 * pair + 1], nz // 2, 1)

    def hot(number):
        number = number - 1.0
        high = jnp.floor(number * (1.0 / nz))
        low = number - high * nz
        rows = theta_ref.shape[0]
        high_eq = lax.broadcasted_iota(jnp.int32, (rows, nz), 0).astype(jnp.float32) == high
        low_eq = lax.broadcasted_iota(jnp.int32, (nz, nz), 0).astype(jnp.float32) == low
        return jnp.where(high_eq, 1.0, 0.0), jnp.where(low_eq, 1.0, 0.0)

    def split(value):
        one = value.astype(jnp.bfloat16)
        rest = value - one.astype(jnp.float32)
        two = rest.astype(jnp.bfloat16)
        three = (rest - two.astype(jnp.float32)).astype(jnp.bfloat16)
        return jnp.concatenate([one, two, three], 0)

    def add_up(value):
        third = value.shape[0] // 3
        return value[:third] + value[third:2 * third] + value[2 * third:]

    high, low = hot(tiles[0])
    picked = lax.dot_general(split(theta_ref[...]), low.astype(jnp.bfloat16), (((1,), (0,)), ((), ())),
                             preferred_element_type=jnp.float32)
    temperature = jnp.sum(add_up(picked) * high, 0, keepdims=True)

    def lay_plate(x, carry):
        chosen = jnp.where(lane == bx * sub + x, temperature, 0.0)
        total = jnp.sum(chosen, 1, keepdims=True)
        plate[x] = jnp.where(lane == 0, 0.25 * total, 0.0)
        return carry

    lax.fori_loop(0, bx, lay_plate, 0)

    def pack_rows(r, which, values, x):
        for k, i in enumerate(Y_UP):
            msg_out[r, 12 + k, pl.ds(x, 1), :] = values(which(i))[by - 1:by]
        for k, i in enumerate(Y_DOWN):
            msg_out[r, 18 + k, pl.ds(x, 1), :] = values(which(i))[0:1]

    def pack_planes(r, which, last, first):
        for k, i in enumerate(X_UP):
            msg_out[r, k] = last(which(i))
        for k, i in enumerate(X_DOWN):
            msg_out[r, 6 + k] = first(which(i))
        msg_out[r, 24] = last(which(7))
        msg_out[r, 25] = first(which(8))
        msg_out[r, 26] = last(which(9))
        msg_out[r, 27] = first(which(10))

    def send_round(r):
        send(FULL, msg_out.at[r], msg_in.at[r], msg_sent.at[r], msg_got.at[r])

    def unpack(r, which, pop, rim, extra=None):
        def arrived(slot, i, side):
            value = msg_in[r, slot]
            return value if extra is None else value + extra(which(i), side)

        for k, i in enumerate(X_UP):
            pop[which(i), 0] = arrived(k, i, 0)
        for k, i in enumerate(X_DOWN):
            pop[which(i), bx + 1] = arrived(6 + k, i, 1)
        for k, i in enumerate(Y_UP):
            rim[which(i), 1:bx + 1, :] = arrived(12 + k, i, 2)
        for k, i in enumerate(Y_DOWN):
            rim[which(i), 1:bx + 1, :] = arrived(18 + k, i, 3)
        rim[which(7), 0:1, :] = msg_in[r, 24, by - 1:by, :]
        rim[which(8), bx + 1:bx + 2, :] = msg_in[r, 25, 0:1, :]
        rim[which(9), 0:1, :] = msg_in[r, 26, 0:1, :]
        rim[which(10), bx + 1:bx + 2, :] = msg_in[r, 27, by - 1:by, :]

    def turn(value, edge, step_y, step_z):
        if step_y == 1:
            value = jnp.where(sub == 0, edge, pltpu.roll(value, 1, 0))
        elif step_y == -1:
            value = jnp.where(sub == by - 1, edge, pltpu.roll(value, by - 1, 0))
        if step_z == 1:
            value = pltpu.roll(value, 1, 1)
        elif step_z == -1:
            value = pltpu.roll(value, nz - 1, 1)
        return value

    def pull(pop, rim, source, i, x):
        step_x, step_y, step_z = VELOCITY[i]
        edge = rim[source, pl.ds(x + 1 - step_x, 1), :] if step_y else None
        return turn(pop[source, x + 1 - step_x], edge, step_y, step_z)

    adj_copy.wait()

    def adj_rows(x, carry):
        pack_rows(ROUND_ADJ, opposite, lambda j: adj[j, x], x)
        return carry

    lax.fori_loop(0, bx, adj_rows, 0)
    pack_planes(ROUND_ADJ, opposite, lambda j: adj[j, bx - 1], lambda j: adj[j, 0])
    send_round(ROUND_ADJ)

    wait_for(flag_in, flag_got)
    mask_x[0] = flag_in[0]
    mask_x[bx + 1] = flag_in[1]
    mask_lo[1:bx + 1, :] = flag_in[2]
    mask_hi[1:bx + 1, :] = flag_in[3]
    mask_lo[0:1, :] = flag_in[4, by - 1:by, :]
    mask_hi[bx + 1:bx + 2, :] = flag_in[5, 0:1, :]
    mask_hi[0:1, :] = flag_in[6, 0:1, :]
    mask_lo[bx + 1:bx + 2, :] = flag_in[7, by - 1:by, :]

    def fill_table(x, carry):
        for i in range(1, 19):
            step_x, step_y, step_z = VELOCITY[i]
            edge = None
            if step_y:
                edge = (mask_lo if step_y == 1 else mask_hi)[pl.ds(x + 1 - step_x, 1), :]
            value = turn(mask_x[x + 1 - step_x], edge, step_y, step_z)
            if step_z:
                value = jnp.where(lane == (0 if step_z == 1 else nz - 1), 1.0, value)
            table[i, x] = value
        return carry

    lax.fori_loop(0, bx, fill_table, 0)

    def moments_of(s):
        def pairs(i):
            return s[i] + s[i + 1], s[i] - s[i + 1]

        p = {}
        m = {}
        for i in range(1, 19, 2):
            p[i], m[i] = pairs(i)
        density = s[0] + ((p[1] + p[3]) + (p[5] + p[7])) + ((p[9] + p[11]) + (p[13] + p[15])) + p[17]
        speed_x = (m[1] + m[7]) + (m[9] + m[11]) + m[13]
        speed_y = (m[3] + m[7]) + (m[15] + m[17]) - m[9]
        speed_z = (m[5] + m[11]) + (m[15] - m[17]) - m[13]
        temper = (s[19] + s[20]) + (s[21] + s[22]) + (s[23] + s[24]) + s[25]
        return density, speed_x, speed_y, speed_z, temper

    def along(c, a, b, d):
        total = None
        for step, value in zip(c, (a, b, d)):
            if step == 0:
                continue
            if total is None:
                total = value if step == 1 else -value
            else:
                total = total + value if step == 1 else total - value
        return total

    def collide(s, k, x):
        density, ux, uy, uz, temper = moments_of(s)
        moments[k, 0, x] = ux
        moments[k, 1, x] = uy
        moments[k, 2, x] = uz
        moments[k, 3, x] = temper
        vz = uz + LIFT * (temper - MEAN_TEMP)
        base = density - 1.5 * (ux * ux + uy * uy + vz * vz)
        post = [None] * 26
        post[0] = (1.0 - OMEGA) * s[0] + (OMEGA * WEIGHTS[0]) * base
        for i in range(1, 19, 2):
            cv = along(VELOCITY[i], ux, uy, vz)
            even = base + (4.5 * cv) * cv
            odd = 3.0 * cv
            weight = OMEGA * WEIGHTS[i]
            post[i] = (1.0 - OMEGA) * s[i] + weight * (even + odd)
            post[i + 1] = (1.0 - OMEGA) * s[i + 1] + weight * (even - odd)
        post[19] = (1.0 - OMEGA) * s[19] + (OMEGA * WEIGHTS[19]) * temper
        share = (OMEGA * WEIGHTS[20]) * temper
        for i, u in ((20, ux), (22, uy), (24, uz)):
            odd = (4.0 * u) * share
            post[i] = (1.0 - OMEGA) * s[i] + (share + odd)
            post[i + 1] = (1.0 - OMEGA) * s[i + 1] + (share - odd)
        return post

    def keep(pop, r, which, values, x):
        for i in range(26):
            pop[i, x + 1] = values[i]
        pack_rows(r, which, lambda j: values[j], x)

    def ship(pop, r, which):
        pack_planes(r, which, lambda j: pop[j, bx], lambda j: pop[j, 1])
        send_round(r)

    def propagated(pop, rim, x):
        result = [pop[0, x + 1]] + [None] * 25
        result[19] = pop[19, x + 1]
        for i in range(1, 26):
            if i == 19:
                continue
            solid = table[i if i < 19 else i - 19, x] > 0.5
            back = pop[OPPOSITE[i], x + 1]
            if i == 24:
                back = jnp.where(lane == 0, -back, back)
            elif i == 25:
                back = jnp.where(lane == nz - 1, -back, back)
            result[i] = jnp.where(solid, back, pull(pop, rim, i, i, x))
        result[RISING] = result[RISING] + plate[x]
        return result

    wait_for(tiles.at[pl.ds(1, n - 1)], all_got.at[0])

    def fill_hot(pair, carry):
        high, low = hot(joined(tiles, pair))
        high_hot[pair] = high
        low_hot[pl.ds(pl.multiple_of(pair * nz, nz), nz), :] = low.T.astype(jnp.bfloat16)
        return carry

    lax.fori_loop(0, n // 2, fill_hot, 0)


    own.wait()
    wait_for(start.at[:, pl.ds(0, (n_st - 1) * planes)], check_got)

    def begin(x, carry):
        keep(pop_a, 0, same, collide([start[i, x] for i in range(26)], 0, x), x)
        return carry

    lax.fori_loop(0, bx, begin, 0)
    ship(pop_a, 0, same)

    for k in range(1, STEPS):
        old, new = pops[(k - 1) % 2], pops[k % 2]
        rim = rims[(k - 1) % 2]
        wait_for(msg_in.at[k - 1], msg_got.at[k - 1])
        unpack(k - 1, same, old, rim)

        def advance(x, carry, old=old, new=new, rim=rim, k=k):
            keep(new, k, same, collide(propagated(old, rim, x), k, x), x)
            return carry

        lax.fori_loop(0, bx, advance, 0)
        ship(new, k, same)

    last, rim = pops[(STEPS - 1) % 2], rims[(STEPS - 1) % 2]
    wait_for(msg_in.at[STEPS - 1], msg_got.at[STEPS - 1])
    unpack(STEPS - 1, same, last, rim)

    def finish(x, total):
        _, _, _, uz, temper = moments_of(propagated(last, rim, x))
        fluid = 1.0 - mask_x[x + 1]
        warm = fluid * temper
        rise = fluid * uz
        seed[0, x] = warm
        seed[1, x] = rise
        seed_out[4, pl.ds(x, 1), :] = warm[by - 1:by]
        seed_out[5, pl.ds(x, 1), :] = rise[by - 1:by]
        seed_out[6, pl.ds(x, 1), :] = warm[0:1]
        seed_out[7, pl.ds(x, 1), :] = rise[0:1]
        return total + warm * uz

    flux = lax.fori_loop(0, bx, finish, jnp.zeros((by, nz), jnp.float32))
    heat[0] = jnp.sum(flux, 0, keepdims=True)
    send_all(heat, 1)
    seed_out[0] = seed[0, bx - 1]
    seed_out[1] = seed[1, bx - 1]
    seed_out[2] = seed[0, 0]
    seed_out[3] = seed[1, 0]
    send(FACES, seed_out, seed_in, seed_sent, seed_got)
    wait_for(msg_in.at[ROUND_ADJ], msg_got.at[ROUND_ADJ])
    wait_for(seed_in, seed_got)
    wait_for(heat.at[pl.ds(1, n - 1)], all_got.at[1])
    heat_sum = jnp.sum(jnp.sum(heat[...], 0), 1, keepdims=True)
    nusselt = 1.0 + heat_sum / (KAPPA * (bx * n_gx * by * n_st))
    nu_out[...] = nusselt
    gain = jnp.broadcast_to(nusselt - 1.0, (by, nz))

    def seeded(j, warm, rise):
        if j >= 19:
            return gain * rise
        if VELOCITY[j][2] == 0:
            return jnp.zeros((by, nz), jnp.float32)
        return gain * warm if VELOCITY[j][2] == 1 else -(gain * warm)

    def bed_of(value, x):
        return jnp.where(lane == bx * sub + x, 0.25 * value[:, 0:1], 0.0)

    def seed_adjoint(x, total):
        warm = seed[0, x]
        rise = seed[1, x]
        for j in range(26):
            value = adj[j, x] + seeded(j, warm, rise)
            pop_a[j, x + 1] = value
            if j == RISING:
                total = total + bed_of(value, x)
        return total

    total = lax.fori_loop(0, bx, seed_adjoint, jnp.zeros((by, nz), jnp.float32))
    unpack(ROUND_ADJ, opposite, pop_a, rim_a,
           lambda j, side: seeded(j, seed_in[2 * side], seed_in[2 * side + 1]))

    def pulled_back(pop, rim, x):
        fluid = 1.0 - mask_x[x + 1]
        above = jnp.where(lane == 0, 0.0, fluid)
        below = jnp.where(lane == nz - 1, 0.0, fluid)
        mu = [None] * 26
        mu[0] = pop[0, x + 1]
        mu[19] = pop[19, x + 1]
        for i in range(1, 26):
            if i == 19:
                continue
            step_z = VELOCITY[i][2]
            share = fluid if step_z == 0 else (above if step_z == 1 else below)
            bounce = table[i if i < 19 else i - 19, x]
            if i == 24:
                bounce = jnp.where(lane == 0, -1.0, bounce)
            elif i == 25:
                bounce = jnp.where(lane == nz - 1, -1.0, bounce)
            mu[OPPOSITE[i]] = share * pull(pop, rim, OPPOSITE[i], i, x) + bounce * pop[i, x + 1]
        return mu

    def collide_back(mu, k, x):
        ux = moments[k, 0, x]
        uy = moments[k, 1, x]
        uz = moments[k, 2, x]
        temper = moments[k, 3, x]
        vz = uz + LIFT * (temper - MEAN_TEMP)
        even = {}
        odd = {}
        for i in range(1, 19, 2):
            even[i] = mu[i] + mu[i + 1]
            odd[i] = mu[i] - mu[i + 1]
        axis = OMEGA * WEIGHTS[1]
        diag = OMEGA * WEIGHTS[7]
        xy = diag * (even[7] + even[9])
        xz = diag * (even[11] + even[13])
        yz = diag * (even[15] + even[17])
        ex, ey, ez = axis * even[1], axis * even[3], axis * even[5]
        zero = (OMEGA * WEIGHTS[0]) * mu[0] + ((ex + ey) + (ez + xy)) + (xz + yz)
        sxx = ex + (xy + xz)
        syy = ey + (xy + yz)
        szz = ez + (xz + yz)
        sxy = diag * (even[7] - even[9])
        sxz = diag * (even[11] - even[13])
        syz = diag * (even[15] - even[17])
        one_x = axis * odd[1] + diag * ((odd[7] + odd[9]) + (odd[11] + odd[13]))
        one_y = axis * odd[3] + diag * ((odd[7] - odd[9]) + (odd[15] + odd[17]))
        one_z = axis * odd[5] + diag * ((odd[11] - odd[13]) + (odd[15] - odd[17]))
        bar_x = 3.0 * (one_x - zero * ux) + 9.0 * (sxx * ux + sxy * uy + sxz * vz)
        bar_y = 3.0 * (one_y - zero * uy) + 9.0 * (sxy * ux + syy * uy + syz * vz)
        bar_z = 3.0 * (one_z - zero * vz) + 9.0 * (sxz * ux + syz * uy + szz * vz)
        share = OMEGA * WEIGHTS[20]
        hx = (4.0 * share) * (mu[20] - mu[21])
        hy = (4.0 * share) * (mu[22] - mu[23])
        hz = (4.0 * share) * (mu[24] - mu[25])
        warm = (OMEGA * WEIGHTS[19]) * mu[19] + share * (
            ((mu[20] + mu[21]) + (mu[22] + mu[23])) + (mu[24] + mu[25]))
        bar_t = warm + (hx * ux + hy * uy + hz * uz) + LIFT * bar_z
        bar_x = bar_x + temper * hx
        bar_y = bar_y + temper * hy
        bar_z = bar_z + temper * hz
        lam = [None] * 26
        lam[0] = (1.0 - OMEGA) * mu[0] + zero
        for i in range(1, 19, 2):
            cb = along(VELOCITY[i], bar_x, bar_y, bar_z)
            lam[i] = (1.0 - OMEGA) * mu[i] + (zero + cb)
            lam[i + 1] = (1.0 - OMEGA) * mu[i + 1] + (zero - cb)
        for i in range(19, 26):
            lam[i] = (1.0 - OMEGA) * mu[i] + bar_t
        return lam

    for step in range(STEPS - 1):
        old, new = pops[step % 2], pops[(step + 1) % 2]
        rim = rims[step % 2]
        k = STEPS - 1 - step
        r = ROUND_ADJ + step
        if step:
            wait_for(msg_in.at[r], msg_got.at[r])
            unpack(r, opposite, old, rim)

        def retreat(x, total, old=old, new=new, rim=rim, k=k, r=r):
            lam = collide_back(pulled_back(old, rim, x), k, x)
            keep(new, r + 1, opposite, lam, x)
            return total + bed_of(lam[RISING], x)

        total = lax.fori_loop(0, bx, retreat, total)
        ship(new, r + 1, opposite)

    grads[0] = jnp.sum(total, 0, keepdims=True)
    send_all(grads, 2)

    old, rim = pops[(STEPS - 1) % 2], rims[(STEPS - 1) % 2]
    r = ROUND_ADJ + STEPS - 1
    wait_for(msg_in.at[r], msg_got.at[r])
    unpack(r, opposite, old, rim)

    def end(x, carry):
        lam = collide_back(pulled_back(old, rim, x), 0, x)
        for i in range(26):
            out_ref[i, x] = lam[i]
        return carry

    lax.fori_loop(0, bx, end, 0)

    wait_for(grads.at[pl.ds(1, n - 1)], all_got.at[2])
    rows = theta_ref.shape[0]
    pairs = n // 2
    part = 16 if pairs % 16 == 0 else pairs

    def gather_tiles(chunk, total):
        weighted = [split(high_hot[chunk * part + p] * joined(grads, chunk * part + p))
                    for p in range(part)]
        low = low_hot[pl.ds(pl.multiple_of(chunk * (part * nz), nz), part * nz), :]
        return total + jnp.dot(jnp.concatenate(weighted, 1), low,
                               preferred_element_type=jnp.float32)

    grad_out[...] = add_up(lax.fori_loop(0, pairs // part, gather_tiles,
                                         jnp.zeros((3 * rows, nz), jnp.float32)))

    wait_for(start.at[:, pl.ds(0, (n_st - 1) * planes)], check_sent)
    wait_for(flag_out, flag_sent)
    wait_for(seed_out, seed_sent)
    for r in range(ROUNDS):
        wait_for(msg_out.at[r], msg_sent.at[r])
    wait_for(tiles.at[pl.ds(1, n - 1)], all_sent.at[0])
    wait_for(heat.at[pl.ds(1, n - 1)], all_sent.at[1])
    wait_for(grads.at[pl.ds(1, n - 1)], all_sent.at[2])


def update(lam_ref, grad_ref, nu_ref, theta_ref, first_ref, second_ref,
           out_ref, theta_out, first_out, second_out, nu_out, sem):
    copy = pltpu.make_async_copy(lam_ref, out_ref, sem)
    copy.start()
    tile_grad = grad_ref[...]
    first_new = BETA_ONE * first_ref[...] + (1.0 - BETA_ONE) * tile_grad
    second_new = BETA_TWO * second_ref[...] + (1.0 - BETA_TWO) * tile_grad * tile_grad
    first_hat = first_new / (1.0 - BETA_ONE**ADAM_STEP)
    second_hat = second_new / (1.0 - BETA_TWO**ADAM_STEP)
    first_out[...] = first_new
    second_out[...] = second_new
    theta_out[...] = theta_ref[...] - LEARN_RATE * first_hat / (jnp.sqrt(second_hat) + ADAM_EPS)
    nu_out[...] = nu_ref[...]
    copy.wait()


def body(n_gx, n_st, checkpoint, adjoint_in, solid_mask, tile_map, theta, first_moment, second_moment):
    bx, by, nz = solid_mask.shape
    planes = checkpoint.shape[1]
    n = n_gx * n_st
    rows = theta.shape[0] // nz
    f32 = jnp.float32
    wide = 16
    vmem = pl.BlockSpec(memory_space=pltpu.VMEM)
    hbm = pl.BlockSpec(memory_space=pltpu.HBM)
    dma = pltpu.SemaphoreType.DMA
    out, tile_grad, nusselt = pl.pallas_call(
        functools.partial(kernel, n_gx, n_st, planes),
        out_shape=(
            jax.ShapeDtypeStruct((26, bx, by, nz), f32),
            jax.ShapeDtypeStruct((rows, nz), f32),
            jax.ShapeDtypeStruct((1, 1), f32),
        ),
        in_specs=[hbm] * 5,
        out_specs=(vmem,) * 3,
        scratch_shapes=[
            pltpu.VMEM((bx, by, nz), jnp.int32),
            pltpu.VMEM((bx, by), jnp.int32),
            pltpu.VMEM((rows, nz), f32),
            pltpu.VMEM((26, bx, by, nz), f32),
            pltpu.VMEM((26, bx, by, nz), f32),
            pltpu.VMEM((26, bx + 2, by, nz), f32),
            pltpu.VMEM((26, bx + 2, by, nz), f32),
            pltpu.VMEM((26, wide, nz), f32),
            pltpu.VMEM((26, wide, nz), f32),
            pltpu.VMEM((STEPS, 4, bx, by, nz), f32),
            pltpu.VMEM((19, bx, by, nz), f32),
            pltpu.VMEM((bx, by, nz), f32),
            pltpu.VMEM((ROUNDS, 28, by, nz), f32),
            pltpu.VMEM((ROUNDS, 28, by, nz), f32),
            pltpu.VMEM((8, by, nz), f32),
            pltpu.VMEM((8, by, nz), f32),
            pltpu.VMEM((8, by, nz), f32),
            pltpu.VMEM((8, by, nz), f32),
            pltpu.VMEM((2, bx, by, nz), f32),
            pltpu.VMEM((bx + 2, by, nz), f32),
            pltpu.VMEM((wide, nz), f32),
            pltpu.VMEM((wide, nz), f32),
            pltpu.VMEM((n, 1, nz), f32),
            pltpu.VMEM((n, 1, nz), f32),
            pltpu.VMEM((n, 1, nz), f32),
            pltpu.VMEM((n // 2 * nz, nz), jnp.bfloat16),
            pltpu.VMEM((n // 2, rows, nz), f32),
            dma((ROUNDS,)),
            dma((ROUNDS,)),
            dma,
            dma,
            dma,
            dma,
            dma((3,)),
            dma((3,)),
            dma,
            dma,
            dma,
            dma,
            dma((3,)),
        ],
        compiler_params=pltpu.CompilerParams(
            collective_id=0, has_side_effects=True, vmem_limit_bytes=40 * 1024 * 1024),
        name="window",
    )(*(pltpu.with_memory_space_constraint(value, pltpu.HBM) for value in (
        checkpoint, adjoint_in, solid_mask, tile_map, theta.reshape(rows, nz))))
    small = jax.ShapeDtypeStruct((rows, nz), f32)
    adjoint_out, theta_new, first_new, second_new, nusselt = pl.pallas_call(
        update,
        out_shape=(jax.ShapeDtypeStruct((26, bx, by, nz), f32), small, small, small,
                   jax.ShapeDtypeStruct((1, 1), f32)),
        in_specs=[vmem] * 6,
        out_specs=(hbm, vmem, vmem, vmem, vmem),
        scratch_shapes=[dma],
        name="update",
    )(out, tile_grad, nusselt, theta.reshape(rows, nz), first_moment.reshape(rows, nz),
      second_moment.reshape(rows, nz))
    flat = theta.shape
    return (adjoint_out, theta_new.reshape(flat), first_new.reshape(flat),
            second_new.reshape(flat), nusselt.reshape(()))


def solution(mesh):
    return jax.shard_map(
        functools.partial(body, mesh.shape["gx"], mesh.shape["st"]),
        mesh=mesh,
        in_specs=(
            P(None, ("gx", "st"), None, None),
            P(None, "gx", "st", None),
            P("gx", "st", None),
            P("gx", "st"),
            P(),
            P(),
            P(),
        ),
        out_specs=(P(None, "gx", "st", None), P(), P(), P(), P()),
        check_vma=False,
    )
```

```python
import functools

import jax
import jax.numpy as jnp
import numpy as np
from jax import lax
from jax.experimental import pallas as pl
from jax.experimental.pallas import tpu as pltpu
from jax.sharding import PartitionSpec as P

STEPS = 4
ADAM_STEP = 100

VELOCITY = [
    (0, 0, 0), (1, 0, 0), (-1, 0, 0), (0, 1, 0), (0, -1, 0), (0, 0, 1), (0, 0, -1),
    (1, 1, 0), (-1, -1, 0), (1, -1, 0), (-1, 1, 0), (1, 0, 1), (-1, 0, -1), (1, 0, -1),
    (-1, 0, 1), (0, 1, 1), (0, -1, -1), (0, 1, -1), (0, -1, 1),
    (0, 0, 0), (1, 0, 0), (-1, 0, 0), (0, 1, 0), (0, -1, 0), (0, 0, 1), (0, 0, -1),
]
WEIGHTS = [1.0 / 3.0] + [1.0 / 18.0] * 6 + [1.0 / 36.0] * 12 + [0.25] + [0.125] * 6
OPPOSITE = [0, 2, 1, 4, 3, 6, 5, 8, 7, 10, 9, 12, 11, 14, 13, 16, 15, 18, 17,
            19, 21, 20, 23, 22, 25, 24]
OMEGA = 1.25
LIFT = 0.8 * 0.001
MEAN_TEMP = 0.5
KAPPA = 0.075
RISING = 24
LEARN_RATE = 0.05
BETA_ONE = 0.9
BETA_TWO = 0.99
ADAM_EPS = 1e-08
MESH = pl.DeviceIdType.MESH

X_UP = [i for i in range(26) if VELOCITY[i][0] == 1]
X_DOWN = [i for i in range(26) if VELOCITY[i][0] == -1]
Y_UP = [i for i in range(26) if VELOCITY[i][1] == 1]
Y_DOWN = [i for i in range(26) if VELOCITY[i][1] == -1]
FAR = [(1, 0, 0, 6), (-1, 0, 6, 6), (1, 1, 12, 1), (-1, -1, 13, 1), (1, -1, 14, 1), (-1, 1, 15, 1)]
INNER = [(0, 1, 16, 6), (0, -1, 22, 6)]
EDGE = [(0, 1, 28, 6), (0, -1, 34, 6)]
GROUPS = [(FAR, 0, 16), (INNER, 16, 12), (EDGE, 28, 12)]
SINGLE = [(1, 0, 0, 1), (-1, 0, 1, 1), (0, 1, 2, 1), (0, -1, 3, 1),
          (1, 1, 4, 1), (-1, -1, 5, 1), (1, -1, 6, 1), (-1, 1, 7, 1)]
FACES = [(1, 0, 0, 2), (-1, 0, 2, 2), (0, 1, 4, 2), (0, -1, 6, 2)]
ROUND_ADJ = STEPS
ROUNDS = 2 * STEPS


def same(i):
    return i


def opposite(i):
    return OPPOSITE[i]


def kernel(n_gx, n_st, planes,
           check_ref, adj_ref, solid_hbm, map_hbm, theta_hbm, first_hbm, second_hbm,
           out_ref, theta_out, first_out, second_out, nu_out,
           solid_ref, map_ref, theta_ref, first_ref, second_ref, start, adj, pop_a, pop_b, rim_a, rim_b, moments, table, plate,
           msg_out, msg_in, flag_out, flag_in, seed_out, seed_in, seed,
           mask_x, mask_lo, mask_hi, tiles, heat, grads, low_hot, high_hot,
           msg_sent, msg_got, flag_sent, flag_got, seed_sent, seed_got,
           all_sent, all_got, check_sent, check_got, own_sem, adj_sem, small_sem):
    bx, by, nz = solid_ref.shape
    gx = lax.axis_index("gx")
    st = lax.axis_index("st")
    n = n_gx * n_st
    me = gx * n_st + st
    pops = (pop_a, pop_b)
    rims = (rim_a, rim_b)
    sub = lax.broadcasted_iota(jnp.int32, (by, nz), 0)
    lane = lax.broadcasted_iota(jnp.int32, (by, nz), 1)

    own = pltpu.make_async_copy(
        check_ref.at[:, :, pl.ds(pl.multiple_of(st * by, by), by), :],
        start.at[:, pl.ds(st * planes, planes)], own_sem)
    own.start()
    adj_copy = pltpu.make_async_copy(adj_ref, adj, adj_sem)
    adj_copy.start()
    small = [pltpu.make_async_copy(source, into, small_sem.at[k]) for k, (source, into) in enumerate(
        ((solid_hbm, solid_ref), (map_hbm, map_ref), (theta_hbm, theta_ref),
         (first_hbm, first_ref), (second_hbm, second_ref)))]
    for copy in small:
        copy.start()

    def device(offset):
        other = lax.rem(me + offset, n)
        return (other // n_st, lax.rem(other, n_st))

    barrier = pltpu.get_barrier_semaphore()

    @pl.loop(1, n)
    def _(offset):
        pl.semaphore_signal(barrier, inc=1, device_id=device(offset), device_id_type=MESH)

    pl.semaphore_wait(barrier, n - 1)

    def check_copy(step):
        other = lax.rem(st + step, n_st)
        return pltpu.make_async_remote_copy(
            src_ref=check_ref.at[:, :, pl.ds(pl.multiple_of(other * by, by), by), :],
            dst_ref=start.at[:, pl.ds(st * planes, planes)],
            send_sem=check_sent, recv_sem=check_got,
            device_id=(gx, other), device_id_type=MESH)

    for step in range(1, n_st):
        check_copy(step).start()

    def send(messages, out, into, sent, got):
        for dx, dy, first, count in messages:
            pltpu.make_async_remote_copy(
                src_ref=out.at[pl.ds(first, count)], dst_ref=into.at[pl.ds(first, count)],
                send_sem=sent, recv_sem=got,
                device_id=(lax.rem(gx + dx + n_gx, n_gx), lax.rem(st + dy + n_st, n_st)),
                device_id_type=MESH).start()

    def send_all(buf, k):
        @pl.loop(1, n)
        def _(offset):
            pltpu.make_async_remote_copy(
                src_ref=buf.at[0], dst_ref=buf.at[offset],
                send_sem=all_sent.at[k], recv_sem=all_got.at[k],
                device_id=device(offset), device_id_type=MESH).start()

    def wait_for(ref, sem):
        pltpu.make_async_copy(ref, ref, sem).wait()

    for copy in small:
        copy.wait()

    def flags(x, carry):
        value = solid_ref[x].astype(jnp.float32)
        mask_x[x + 1] = value
        flag_out[2, pl.ds(x, 1), :] = value[by - 1:by]
        flag_out[3, pl.ds(x, 1), :] = value[0:1]
        return carry

    lax.fori_loop(0, bx, flags, 0)
    flag_out[0] = mask_x[bx]
    flag_out[1] = mask_x[1]
    flag_out[4] = mask_x[bx]
    flag_out[5] = mask_x[1]
    flag_out[6] = mask_x[bx]
    flag_out[7] = mask_x[1]
    send(SINGLE, flag_out, flag_in, flag_sent, flag_got)

    cell_x = lax.broadcasted_iota(jnp.int32, (bx, nz), 0)
    cell_lane = lax.broadcasted_iota(jnp.int32, (bx, nz), 1)
    numbers = map_ref[...].astype(jnp.float32)
    row = jnp.zeros((bx, nz), jnp.float32)
    for y in range(by):
        row = row + jnp.where(cell_lane == bx * y + cell_x, numbers[:, y:y + 1] + 1.0, 0.0)
    tiles[0] = jnp.sum(row, 0, keepdims=True)
    send_all(tiles, 0)

    def joined(buf, pair):
        return buf[2 * pair] + pltpu.roll(buf[2 * pair + 1], nz // 2, 1)

    def hot(number):
        number = number - 1.0
        high = jnp.floor(number * (1.0 / nz))
        low = number - high * nz
        rows = theta_ref.shape[0]
        high_eq = lax.broadcasted_iota(jnp.int32, (rows, nz), 0).astype(jnp.float32) == high
        low_eq = lax.broadcasted_iota(jnp.int32, (nz, nz), 0).astype(jnp.float32) == low
        return jnp.where(high_eq, 1.0, 0.0), jnp.where(low_eq, 1.0, 0.0)

    def split(value):
        one = value.astype(jnp.bfloat16)
        rest = value - one.astype(jnp.float32)
        two = rest.astype(jnp.bfloat16)
        three = (rest - two.astype(jnp.float32)).astype(jnp.bfloat16)
        return jnp.concatenate([one, two, three], 0)

    def add_up(value):
        third = value.shape[0] // 3
        return value[:third] + value[third:2 * third] + value[2 * third:]

    high, low = hot(tiles[0])
    picked = lax.dot_general(split(theta_ref[...]), low.astype(jnp.bfloat16), (((1,), (0,)), ((), ())),
                             preferred_element_type=jnp.float32)
    temperature = jnp.sum(add_up(picked) * high, 0, keepdims=True)

    def lay_plate(x, carry):
        chosen = jnp.where(lane == bx * sub + x, temperature, 0.0)
        total = jnp.sum(chosen, 1, keepdims=True)
        plate[x] = jnp.where(lane == 0, 0.25 * total, 0.0)
        return carry

    lax.fori_loop(0, bx, lay_plate, 0)

    def pack_rows(r, which, values, x, base):
        for k, i in enumerate(Y_UP):
            msg_out[r, base + k, pl.ds(x, 1), :] = values(which(i))[by - 1:by]
        for k, i in enumerate(Y_DOWN):
            msg_out[r, base + 6 + k, pl.ds(x, 1), :] = values(which(i))[0:1]

    def pack_planes(r, which, last, first):
        for k, i in enumerate(X_UP):
            msg_out[r, k] = last(which(i))
        for k, i in enumerate(X_DOWN):
            msg_out[r, 6 + k] = first(which(i))
        msg_out[r, 12] = last(which(7))
        msg_out[r, 13] = first(which(8))
        msg_out[r, 14] = last(which(9))
        msg_out[r, 15] = first(which(10))

    def send_group(r, group):
        send(GROUPS[group][0], msg_out.at[r], msg_in.at[r], msg_sent.at[r], msg_got.at[r, group])

    def wait_group(r, group):
        _, first, count = GROUPS[group]
        wait_for(msg_in.at[r, pl.ds(first, count)], msg_got.at[r, group])

    def unpack_far(r, which, pop, rim, extra=None):
        def arrived(slot, i, side):
            value = msg_in[r, slot]
            return value if extra is None else value + extra(which(i), side)

        for k, i in enumerate(X_UP):
            pop[which(i), 0] = arrived(k, i, 0)
        for k, i in enumerate(X_DOWN):
            pop[which(i), bx + 1] = arrived(6 + k, i, 1)
        rim[which(7), 0:1, :] = msg_in[r, 12, by - 1:by, :]
        rim[which(8), bx + 1:bx + 2, :] = msg_in[r, 13, 0:1, :]
        rim[which(9), 0:1, :] = msg_in[r, 14, 0:1, :]
        rim[which(10), bx + 1:bx + 2, :] = msg_in[r, 15, by - 1:by, :]

    def unpack_inner(r, which, rim, extra=None):
        for side, rows_of, base in ((2, Y_UP, 16), (3, Y_DOWN, 22)):
            for k, i in enumerate(rows_of):
                value = msg_in[r, base + k]
                if extra is not None:
                    value = value + extra(which(i), side)
                rim[which(i), 2:bx, :] = value[1:bx - 1]

    def unpack_edge(r, which, rim, extra=None):
        for side, rows_of, base in ((2, Y_UP, 28), (3, Y_DOWN, 34)):
            for k, i in enumerate(rows_of):
                value = msg_in[r, base + k]
                if extra is not None:
                    value = value + extra(which(i), side)
                rim[which(i), 1:2, :] = value[0:1]
                rim[which(i), bx:bx + 1, :] = value[bx - 1:bx]

    def turn(value, edge, step_y, step_z):
        if step_y == 1:
            value = jnp.where(sub == 0, edge, pltpu.roll(value, 1, 0))
        elif step_y == -1:
            value = jnp.where(sub == by - 1, edge, pltpu.roll(value, by - 1, 0))
        if step_z == 1:
            value = pltpu.roll(value, 1, 1)
        elif step_z == -1:
            value = pltpu.roll(value, nz - 1, 1)
        return value

    def pull(pop, rim, source, i, x):
        step_x, step_y, step_z = VELOCITY[i]
        edge = rim[source, pl.ds(x + 1 - step_x, 1), :] if step_y else None
        return turn(pop[source, x + 1 - step_x], edge, step_y, step_z)

    adj_copy.wait()

    def adj_rows(x, carry):
        pack_rows(ROUND_ADJ, opposite, lambda j: adj[j, x], x, 16)
        return carry

    lax.fori_loop(1, bx - 1, adj_rows, 0)
    for x in (0, bx - 1):
        pack_rows(ROUND_ADJ, opposite, lambda j, x=x: adj[j, x], x, 28)
    pack_planes(ROUND_ADJ, opposite, lambda j: adj[j, bx - 1], lambda j: adj[j, 0])
    for group in range(3):
        send_group(ROUND_ADJ, group)

    wait_for(flag_in, flag_got)
    mask_x[0] = flag_in[0]
    mask_x[bx + 1] = flag_in[1]
    mask_lo[1:bx + 1, :] = flag_in[2]
    mask_hi[1:bx + 1, :] = flag_in[3]
    mask_lo[0:1, :] = flag_in[4, by - 1:by, :]
    mask_hi[bx + 1:bx + 2, :] = flag_in[5, 0:1, :]
    mask_hi[0:1, :] = flag_in[6, 0:1, :]
    mask_lo[bx + 1:bx + 2, :] = flag_in[7, by - 1:by, :]

    def fill_table(x, carry):
        for i in range(1, 19):
            step_x, step_y, step_z = VELOCITY[i]
            edge = None
            if step_y:
                edge = (mask_lo if step_y == 1 else mask_hi)[pl.ds(x + 1 - step_x, 1), :]
            value = turn(mask_x[x + 1 - step_x], edge, step_y, step_z)
            if step_z:
                value = jnp.where(lane == (0 if step_z == 1 else nz - 1), 1.0, value)
            table[i, x] = value
        return carry

    lax.fori_loop(0, bx, fill_table, 0)

    def moments_of(s):
        def pairs(i):
            return s[i] + s[i + 1], s[i] - s[i + 1]

        p = {}
        m = {}
        for i in range(1, 19, 2):
            p[i], m[i] = pairs(i)
        density = s[0] + ((p[1] + p[3]) + (p[5] + p[7])) + ((p[9] + p[11]) + (p[13] + p[15])) + p[17]
        speed_x = (m[1] + m[7]) + (m[9] + m[11]) + m[13]
        speed_y = (m[3] + m[7]) + (m[15] + m[17]) - m[9]
        speed_z = (m[5] + m[11]) + (m[15] - m[17]) - m[13]
        temper = (s[19] + s[20]) + (s[21] + s[22]) + (s[23] + s[24]) + s[25]
        return density, speed_x, speed_y, speed_z, temper

    def along(c, a, b, d):
        total = None
        for step, value in zip(c, (a, b, d)):
            if step == 0:
                continue
            if total is None:
                total = value if step == 1 else -value
            else:
                total = total + value if step == 1 else total - value
        return total

    def collide(s, k, x):
        density, ux, uy, uz, temper = moments_of(s)
        moments[k, 0, x] = ux
        moments[k, 1, x] = uy
        moments[k, 2, x] = uz
        moments[k, 3, x] = temper
        vz = uz + LIFT * (temper - MEAN_TEMP)
        base = density - 1.5 * (ux * ux + uy * uy + vz * vz)
        post = [None] * 26
        post[0] = (1.0 - OMEGA) * s[0] + (OMEGA * WEIGHTS[0]) * base
        for i in range(1, 19, 2):
            cv = along(VELOCITY[i], ux, uy, vz)
            even = base + (4.5 * cv) * cv
            odd = 3.0 * cv
            weight = OMEGA * WEIGHTS[i]
            post[i] = (1.0 - OMEGA) * s[i] + weight * (even + odd)
            post[i + 1] = (1.0 - OMEGA) * s[i + 1] + weight * (even - odd)
        post[19] = (1.0 - OMEGA) * s[19] + (OMEGA * WEIGHTS[19]) * temper
        share = (OMEGA * WEIGHTS[20]) * temper
        for i, u in ((20, ux), (22, uy), (24, uz)):
            odd = (4.0 * u) * share
            post[i] = (1.0 - OMEGA) * s[i] + (share + odd)
            post[i + 1] = (1.0 - OMEGA) * s[i + 1] + (share - odd)
        return post

    def keep(pop, r, which, values, x, base):
        for i in range(26):
            pop[i, x + 1] = values[i]
        pack_rows(r, which, lambda j: values[j], x, base)

    def ship_edges(pop, r, which):
        pack_planes(r, which, lambda j: pop[j, bx], lambda j: pop[j, 1])
        send_group(r, 0)
        send_group(r, 2)

    def outer(it):
        return it * (bx - 1)

    def next_to(it):
        return 1 + it * (bx - 3)

    def over(place, count, work, carry):
        return lax.fori_loop(0, count, lambda it, total: work(place(it), total), carry)

    def whole_step(work, carry, pop, r, which):
        carry = over(outer, 2, functools.partial(work, base=28), carry)
        ship_edges(pop, r, which)
        carry = over(lambda it: it + 1, bx - 2, functools.partial(work, base=16), carry)
        send_group(r, 1)
        return carry

    def fed_step(work, carry, old, rim, r, which, new=None, between=None):
        wait_group(r, 1)
        unpack_inner(r, which, rim)
        carry = over(lambda it: it + 2, bx - 4, functools.partial(work, base=16), carry)
        wait_group(r, 2)
        unpack_edge(r, which, rim)
        carry = over(next_to, 2, functools.partial(work, base=16), carry)
        if new is not None:
            send_group(r + 1, 1)
        if between is not None:
            between()
        wait_group(r, 0)
        unpack_far(r, which, old, rim)
        carry = over(outer, 2, functools.partial(work, base=28), carry)
        if new is not None:
            ship_edges(new, r + 1, which)
        return carry

    def propagated(pop, rim, x):
        result = [pop[0, x + 1]] + [None] * 25
        result[19] = pop[19, x + 1]
        for i in range(1, 26):
            if i == 19:
                continue
            solid = table[i if i < 19 else i - 19, x] > 0.5
            back = pop[OPPOSITE[i], x + 1]
            if i == 24:
                back = jnp.where(lane == 0, -back, back)
            elif i == 25:
                back = jnp.where(lane == nz - 1, -back, back)
            result[i] = jnp.where(solid, back, pull(pop, rim, i, i, x))
        result[RISING] = result[RISING] + plate[x]
        return result

    wait_for(tiles.at[pl.ds(1, n - 1)], all_got.at[0])

    def fill_hot(pair, carry):
        high, low = hot(joined(tiles, pair))
        high_hot[pair] = high
        low_hot[pl.ds(pl.multiple_of(pair * nz, nz), nz), :] = low.T.astype(jnp.bfloat16)
        return carry

    lax.fori_loop(0, n // 2, fill_hot, 0)


    own.wait()
    wait_for(start.at[:, pl.ds(0, (n_st - 1) * planes)], check_got)

    def begin(x, carry, base):
        keep(pop_a, 0, same, collide([start[i, x] for i in range(26)], 0, x), x, base)
        return carry

    whole_step(begin, 0, pop_a, 0, same)

    for k in range(1, STEPS):
        old, new = pops[(k - 1) % 2], pops[k % 2]
        rim = rims[(k - 1) % 2]

        def advance(x, carry, base, old=old, new=new, rim=rim, k=k):
            keep(new, k, same, collide(propagated(old, rim, x), k, x), x, base)
            return carry

        fed_step(advance, 0, old, rim, k - 1, same, new)

    last, rim = pops[(STEPS - 1) % 2], rims[(STEPS - 1) % 2]

    def finish(x, total, base, last=last, rim=rim):
        _, _, _, uz, temper = moments_of(propagated(last, rim, x))
        fluid = 1.0 - mask_x[x + 1]
        warm = fluid * temper
        rise = fluid * uz
        seed[0, x] = warm
        seed[1, x] = rise
        seed_out[4, pl.ds(x, 1), :] = warm[by - 1:by]
        seed_out[5, pl.ds(x, 1), :] = rise[by - 1:by]
        seed_out[6, pl.ds(x, 1), :] = warm[0:1]
        seed_out[7, pl.ds(x, 1), :] = rise[0:1]
        return total + warm * uz

    flux = fed_step(finish, jnp.zeros((by, nz), jnp.float32), last, rim, STEPS - 1, same)
    heat[0] = jnp.sum(flux, 0, keepdims=True)
    send_all(heat, 1)
    seed_out[0] = seed[0, bx - 1]
    seed_out[1] = seed[1, bx - 1]
    seed_out[2] = seed[0, 0]
    seed_out[3] = seed[1, 0]
    send(FACES, seed_out, seed_in, seed_sent, seed_got)
    for group in range(3):
        wait_group(ROUND_ADJ, group)
    wait_for(seed_in, seed_got)
    wait_for(heat.at[pl.ds(1, n - 1)], all_got.at[1])
    heat_sum = jnp.sum(jnp.sum(heat[...], 0), 1, keepdims=True)
    nusselt = 1.0 + heat_sum / (KAPPA * (bx * n_gx * by * n_st))
    nu_out[...] = nusselt
    gain = jnp.broadcast_to(nusselt - 1.0, (by, nz))

    def seeded(j, warm, rise):
        if j >= 19:
            return gain * rise
        if VELOCITY[j][2] == 0:
            return jnp.zeros((by, nz), jnp.float32)
        return gain * warm if VELOCITY[j][2] == 1 else -(gain * warm)

    def bed_of(value, x):
        return jnp.where(lane == bx * sub + x, 0.25 * value[:, 0:1], 0.0)

    def seed_adjoint(x, total):
        warm = seed[0, x]
        rise = seed[1, x]
        for j in range(26):
            value = adj[j, x] + seeded(j, warm, rise)
            pop_a[j, x + 1] = value
            if j == RISING:
                total = total + bed_of(value, x)
        return total

    total = lax.fori_loop(0, bx, seed_adjoint, jnp.zeros((by, nz), jnp.float32))

    def arrived_seed(j, side):
        return seeded(j, seed_in[2 * side], seed_in[2 * side + 1])

    unpack_far(ROUND_ADJ, opposite, pop_a, rim_a, arrived_seed)
    unpack_inner(ROUND_ADJ, opposite, rim_a, arrived_seed)
    unpack_edge(ROUND_ADJ, opposite, rim_a, arrived_seed)

    def pulled_back(pop, rim, x):
        fluid = 1.0 - mask_x[x + 1]
        above = jnp.where(lane == 0, 0.0, fluid)
        below = jnp.where(lane == nz - 1, 0.0, fluid)
        mu = [None] * 26
        mu[0] = pop[0, x + 1]
        mu[19] = pop[19, x + 1]
        for i in range(1, 26):
            if i == 19:
                continue
            step_z = VELOCITY[i][2]
            share = fluid if step_z == 0 else (above if step_z == 1 else below)
            bounce = table[i if i < 19 else i - 19, x]
            if i == 24:
                bounce = jnp.where(lane == 0, -1.0, bounce)
            elif i == 25:
                bounce = jnp.where(lane == nz - 1, -1.0, bounce)
            mu[OPPOSITE[i]] = share * pull(pop, rim, OPPOSITE[i], i, x) + bounce * pop[i, x + 1]
        return mu

    def collide_back(mu, k, x):
        ux = moments[k, 0, x]
        uy = moments[k, 1, x]
        uz = moments[k, 2, x]
        temper = moments[k, 3, x]
        vz = uz + LIFT * (temper - MEAN_TEMP)
        even = {}
        odd = {}
        for i in range(1, 19, 2):
            even[i] = mu[i] + mu[i + 1]
            odd[i] = mu[i] - mu[i + 1]
        axis = OMEGA * WEIGHTS[1]
        diag = OMEGA * WEIGHTS[7]
        xy = diag * (even[7] + even[9])
        xz = diag * (even[11] + even[13])
        yz = diag * (even[15] + even[17])
        ex, ey, ez = axis * even[1], axis * even[3], axis * even[5]
        zero = (OMEGA * WEIGHTS[0]) * mu[0] + ((ex + ey) + (ez + xy)) + (xz + yz)
        sxx = ex + (xy + xz)
        syy = ey + (xy + yz)
        szz = ez + (xz + yz)
        sxy = diag * (even[7] - even[9])
        sxz = diag * (even[11] - even[13])
        syz = diag * (even[15] - even[17])
        one_x = axis * odd[1] + diag * ((odd[7] + odd[9]) + (odd[11] + odd[13]))
        one_y = axis * odd[3] + diag * ((odd[7] - odd[9]) + (odd[15] + odd[17]))
        one_z = axis * odd[5] + diag * ((odd[11] - odd[13]) + (odd[15] - odd[17]))
        bar_x = 3.0 * (one_x - zero * ux) + 9.0 * (sxx * ux + sxy * uy + sxz * vz)
        bar_y = 3.0 * (one_y - zero * uy) + 9.0 * (sxy * ux + syy * uy + syz * vz)
        bar_z = 3.0 * (one_z - zero * vz) + 9.0 * (sxz * ux + syz * uy + szz * vz)
        share = OMEGA * WEIGHTS[20]
        hx = (4.0 * share) * (mu[20] - mu[21])
        hy = (4.0 * share) * (mu[22] - mu[23])
        hz = (4.0 * share) * (mu[24] - mu[25])
        warm = (OMEGA * WEIGHTS[19]) * mu[19] + share * (
            ((mu[20] + mu[21]) + (mu[22] + mu[23])) + (mu[24] + mu[25]))
        bar_t = warm + (hx * ux + hy * uy + hz * uz) + LIFT * bar_z
        bar_x = bar_x + temper * hx
        bar_y = bar_y + temper * hy
        bar_z = bar_z + temper * hz
        lam = [None] * 26
        lam[0] = (1.0 - OMEGA) * mu[0] + zero
        for i in range(1, 19, 2):
            cb = along(VELOCITY[i], bar_x, bar_y, bar_z)
            lam[i] = (1.0 - OMEGA) * mu[i] + (zero + cb)
            lam[i + 1] = (1.0 - OMEGA) * mu[i + 1] + (zero - cb)
        for i in range(19, 26):
            lam[i] = (1.0 - OMEGA) * mu[i] + bar_t
        return lam

    for step in range(STEPS - 1):
        old, new = pops[step % 2], pops[(step + 1) % 2]
        rim = rims[step % 2]
        k = STEPS - 1 - step
        r = ROUND_ADJ + step

        def retreat(x, total, base, old=old, new=new, rim=rim, k=k, r=r):
            lam = collide_back(pulled_back(old, rim, x), k, x)
            keep(new, r + 1, opposite, lam, x, base)
            return total + bed_of(lam[RISING], x)

        if step == 0:
            total = whole_step(retreat, total, new, r + 1, opposite)
        else:
            total = fed_step(retreat, total, old, rim, r, opposite, new)

    grads[0] = jnp.sum(total, 0, keepdims=True)
    send_all(grads, 2)

    old, rim = pops[(STEPS - 1) % 2], rims[(STEPS - 1) % 2]

    def end(x, carry, base):
        lam = collide_back(pulled_back(old, rim, x), 0, x)
        for i in range(26):
            out_ref[i, x] = lam[i]
        return carry

    fed_step(end, 0, old, rim, ROUND_ADJ + STEPS - 1, opposite)

    wait_for(grads.at[pl.ds(1, n - 1)], all_got.at[2])
    rows = theta_ref.shape[0]
    pairs = n // 2
    part = 16 if pairs % 16 == 0 else pairs

    def gather_tiles(chunk, total):
        weighted = [split(high_hot[chunk * part + p] * joined(grads, chunk * part + p))
                    for p in range(part)]
        low = low_hot[pl.ds(pl.multiple_of(chunk * (part * nz), nz), part * nz), :]
        return total + jnp.dot(jnp.concatenate(weighted, 1), low,
                               preferred_element_type=jnp.float32)

    tile_grad = add_up(lax.fori_loop(0, pairs // part, gather_tiles,
                                        jnp.zeros((3 * rows, nz), jnp.float32)))
    first_new = BETA_ONE * first_ref[...] + (1.0 - BETA_ONE) * tile_grad
    second_new = BETA_TWO * second_ref[...] + (1.0 - BETA_TWO) * tile_grad * tile_grad
    first_hat = first_new / (1.0 - BETA_ONE**ADAM_STEP)
    second_hat = second_new / (1.0 - BETA_TWO**ADAM_STEP)
    first_out[...] = first_new
    second_out[...] = second_new
    theta_out[...] = theta_ref[...] - LEARN_RATE * first_hat / (jnp.sqrt(second_hat) + ADAM_EPS)

    wait_for(start.at[:, pl.ds(0, (n_st - 1) * planes)], check_sent)
    wait_for(flag_out, flag_sent)
    wait_for(seed_out, seed_sent)
    for r in range(ROUNDS):
        wait_for(msg_out.at[r], msg_sent.at[r])
    wait_for(tiles.at[pl.ds(1, n - 1)], all_sent.at[0])
    wait_for(heat.at[pl.ds(1, n - 1)], all_sent.at[1])
    wait_for(grads.at[pl.ds(1, n - 1)], all_sent.at[2])


def deliver(*refs):
    sem = refs[-1]
    half = (len(refs) - 1) // 2
    copies = [pltpu.make_async_copy(refs[k], refs[half + k], sem.at[k]) for k in range(half)]
    for copy in copies:
        copy.start()
    for copy in copies:
        copy.wait()


def body(n_gx, n_st, checkpoint, adjoint_in, solid_mask, tile_map, theta, first_moment, second_moment):
    bx, by, nz = solid_mask.shape
    planes = checkpoint.shape[1]
    n = n_gx * n_st
    rows = theta.shape[0] // nz
    f32 = jnp.float32
    wide = 16
    vmem = pl.BlockSpec(memory_space=pltpu.VMEM)
    hbm = pl.BlockSpec(memory_space=pltpu.HBM)
    dma = pltpu.SemaphoreType.DMA
    small = jax.ShapeDtypeStruct((rows, nz), f32)
    shapes = (jax.ShapeDtypeStruct((26, bx, by, nz), f32), small, small, small,
              jax.ShapeDtypeStruct((1, 1), f32))
    results = pl.pallas_call(
        functools.partial(kernel, n_gx, n_st, planes),
        out_shape=shapes,
        in_specs=[hbm] * 7,
        out_specs=(vmem,) * 5,
        scratch_shapes=[
            pltpu.VMEM((bx, by, nz), jnp.int32),
            pltpu.VMEM((bx, by), jnp.int32),
            pltpu.VMEM((rows, nz), f32),
            pltpu.VMEM((rows, nz), f32),
            pltpu.VMEM((rows, nz), f32),
            pltpu.VMEM((26, bx, by, nz), f32),
            pltpu.VMEM((26, bx, by, nz), f32),
            pltpu.VMEM((26, bx + 2, by, nz), f32),
            pltpu.VMEM((26, bx + 2, by, nz), f32),
            pltpu.VMEM((26, wide, nz), f32),
            pltpu.VMEM((26, wide, nz), f32),
            pltpu.VMEM((STEPS, 4, bx, by, nz), f32),
            pltpu.VMEM((19, bx, by, nz), f32),
            pltpu.VMEM((bx, by, nz), f32),
            pltpu.VMEM((ROUNDS, 40, by, nz), f32),
            pltpu.VMEM((ROUNDS, 40, by, nz), f32),
            pltpu.VMEM((8, by, nz), f32),
            pltpu.VMEM((8, by, nz), f32),
            pltpu.VMEM((8, by, nz), f32),
            pltpu.VMEM((8, by, nz), f32),
            pltpu.VMEM((2, bx, by, nz), f32),
            pltpu.VMEM((bx + 2, by, nz), f32),
            pltpu.VMEM((wide, nz), f32),
            pltpu.VMEM((wide, nz), f32),
            pltpu.VMEM((n, 1, nz), f32),
            pltpu.VMEM((n, 1, nz), f32),
            pltpu.VMEM((n, 1, nz), f32),
            pltpu.VMEM((n // 2 * nz, nz), jnp.bfloat16),
            pltpu.VMEM((n // 2, rows, nz), f32),
            dma((ROUNDS,)),
            dma((ROUNDS, 3)),
            dma,
            dma,
            dma,
            dma,
            dma((3,)),
            dma((3,)),
            dma,
            dma,
            dma,
            dma,
            dma((5,)),
        ],
        compiler_params=pltpu.CompilerParams(
            collective_id=0, has_side_effects=True, vmem_limit_bytes=40 * 1024 * 1024),
        name="window",
    )(*(pltpu.with_memory_space_constraint(value, pltpu.HBM) for value in (
        checkpoint, adjoint_in, solid_mask, tile_map, theta.reshape(rows, nz),
        first_moment.reshape(rows, nz), second_moment.reshape(rows, nz))))
    adjoint_out, theta_new, first_new, second_new, nusselt = pl.pallas_call(
        deliver,
        out_shape=shapes,
        in_specs=[vmem] * 5,
        out_specs=(hbm,) * 5,
        scratch_shapes=[dma((5,))],
        name="deliver",
    )(*results)
    flat = theta.shape
    return (adjoint_out, theta_new.reshape(flat), first_new.reshape(flat),
            second_new.reshape(flat), nusselt.reshape(()))


def solution(mesh):
    return jax.shard_map(
        functools.partial(body, mesh.shape["gx"], mesh.shape["st"]),
        mesh=mesh,
        in_specs=(
            P(None, ("gx", "st"), None, None),
            P(None, "gx", "st", None),
            P("gx", "st", None),
            P("gx", "st"),
            P(),
            P(),
            P(),
        ),
        out_specs=(P(None, "gx", "st", None), P(), P(), P(), P()),
        check_vma=False,
    )
```

```python
import functools

import jax
import jax.numpy as jnp
import numpy as np
from jax import lax
from jax.experimental import pallas as pl
from jax.experimental.pallas import tpu as pltpu
from jax.sharding import PartitionSpec as P

STEPS = 4
ADAM_STEP = 100

VELOCITY = [
    (0, 0, 0), (1, 0, 0), (-1, 0, 0), (0, 1, 0), (0, -1, 0), (0, 0, 1), (0, 0, -1),
    (1, 1, 0), (-1, -1, 0), (1, -1, 0), (-1, 1, 0), (1, 0, 1), (-1, 0, -1), (1, 0, -1),
    (-1, 0, 1), (0, 1, 1), (0, -1, -1), (0, 1, -1), (0, -1, 1),
    (0, 0, 0), (1, 0, 0), (-1, 0, 0), (0, 1, 0), (0, -1, 0), (0, 0, 1), (0, 0, -1),
]
WEIGHTS = [1.0 / 3.0] + [1.0 / 18.0] * 6 + [1.0 / 36.0] * 12 + [0.25] + [0.125] * 6
OPPOSITE = [0, 2, 1, 4, 3, 6, 5, 8, 7, 10, 9, 12, 11, 14, 13, 16, 15, 18, 17,
            19, 21, 20, 23, 22, 25, 24]
OMEGA = 1.25
LIFT = 0.8 * 0.001
MEAN_TEMP = 0.5
KAPPA = 0.075
RISING = 24
LEARN_RATE = 0.05
BETA_ONE = 0.9
BETA_TWO = 0.99
ADAM_EPS = 1e-08
MESH = pl.DeviceIdType.MESH

X_UP = [i for i in range(26) if VELOCITY[i][0] == 1]
X_DOWN = [i for i in range(26) if VELOCITY[i][0] == -1]
Y_UP = [i for i in range(26) if VELOCITY[i][1] == 1]
Y_DOWN = [i for i in range(26) if VELOCITY[i][1] == -1]
FAR = [(1, 0, 0, 6), (-1, 0, 6, 6), (1, 1, 12, 1), (-1, -1, 13, 1), (1, -1, 14, 1), (-1, 1, 15, 1)]
INNER = [(0, 1, 16, 6), (0, -1, 22, 6)]
EDGE = [(0, 1, 28, 6), (0, -1, 34, 6)]
GROUPS = [(FAR, 0, 16), (INNER, 16, 12), (EDGE, 28, 12)]
SINGLE = [(1, 0, 0, 1), (-1, 0, 1, 1), (0, 1, 2, 1), (0, -1, 3, 1),
          (1, 1, 4, 1), (-1, -1, 5, 1), (1, -1, 6, 1), (-1, 1, 7, 1)]
FACES = [(1, 0, 0, 2), (-1, 0, 2, 2), (0, 1, 4, 2), (0, -1, 6, 2)]
ROUND_ADJ = STEPS
ROUNDS = 2 * STEPS


def same(i):
    return i


def opposite(i):
    return OPPOSITE[i]


def kernel(n_gx, n_st, planes,
           check_ref, adj_ref, solid_hbm, map_hbm, theta_hbm, first_hbm, second_hbm,
           out_ref, theta_out, first_out, second_out, nu_out,
           solid_ref, map_ref, theta_ref, first_ref, second_ref, lam, nu, theta_new, first_new, second_new, start, adj, pops, rims, moments, table, plate,
           msg_out, msg_in, flag_out, flag_in, seed_out, seed_in, seed,
           mask_x, mask_lo, mask_hi, tiles, heat, grads, low_hot, high_hot,
           msg_sent, msg_got, flag_sent, flag_got, seed_sent, seed_got,
           all_sent, all_got, check_sent, check_got, own_sem, adj_sem, small_sem, out_sem):
    bx, by, nz = solid_ref.shape
    gx = lax.axis_index("gx")
    st = lax.axis_index("st")
    n = n_gx * n_st
    me = gx * n_st + st
    sub = lax.broadcasted_iota(jnp.int32, (by, nz), 0)
    lane = lax.broadcasted_iota(jnp.int32, (by, nz), 1)

    own = pltpu.make_async_copy(
        check_ref.at[:, :, pl.ds(pl.multiple_of(st * by, by), by), :],
        start.at[:, pl.ds(st * planes, planes)], own_sem)
    own.start()
    adj_copy = pltpu.make_async_copy(adj_ref, adj, adj_sem)
    adj_copy.start()
    small = [pltpu.make_async_copy(source, into, small_sem.at[k]) for k, (source, into) in enumerate(
        ((solid_hbm, solid_ref), (map_hbm, map_ref), (theta_hbm, theta_ref),
         (first_hbm, first_ref), (second_hbm, second_ref)))]
    for copy in small:
        copy.start()

    def device(offset):
        other = lax.rem(me + offset, n)
        return (other // n_st, lax.rem(other, n_st))

    barrier = pltpu.get_barrier_semaphore()

    @pl.loop(1, n)
    def _(offset):
        pl.semaphore_signal(barrier, inc=1, device_id=device(offset), device_id_type=MESH)

    pl.semaphore_wait(barrier, n - 1)

    def check_copy(step):
        other = lax.rem(st + step, n_st)
        return pltpu.make_async_remote_copy(
            src_ref=check_ref.at[:, :, pl.ds(pl.multiple_of(other * by, by), by), :],
            dst_ref=start.at[:, pl.ds(st * planes, planes)],
            send_sem=check_sent, recv_sem=check_got,
            device_id=(gx, other), device_id_type=MESH)

    for step in range(1, n_st):
        check_copy(step).start()

    def send(messages, out, into, sent, got):
        for dx, dy, first, count in messages:
            pltpu.make_async_remote_copy(
                src_ref=out.at[pl.ds(first, count)], dst_ref=into.at[pl.ds(first, count)],
                send_sem=sent, recv_sem=got,
                device_id=(lax.rem(gx + dx + n_gx, n_gx), lax.rem(st + dy + n_st, n_st)),
                device_id_type=MESH).start()

    def send_all(buf, k):
        @pl.loop(1, n)
        def _(offset):
            pltpu.make_async_remote_copy(
                src_ref=buf.at[0], dst_ref=buf.at[offset],
                send_sem=all_sent.at[k], recv_sem=all_got.at[k],
                device_id=device(offset), device_id_type=MESH).start()

    def wait_for(ref, sem):
        pltpu.make_async_copy(ref, ref, sem).wait()

    for copy in small:
        copy.wait()

    def flags(x, carry):
        value = solid_ref[x].astype(jnp.float32)
        mask_x[x + 1] = value
        flag_out[2, pl.ds(x, 1), :] = value[by - 1:by]
        flag_out[3, pl.ds(x, 1), :] = value[0:1]
        return carry

    lax.fori_loop(0, bx, flags, 0)
    flag_out[0] = mask_x[bx]
    flag_out[1] = mask_x[1]
    flag_out[4] = mask_x[bx]
    flag_out[5] = mask_x[1]
    flag_out[6] = mask_x[bx]
    flag_out[7] = mask_x[1]
    send(SINGLE, flag_out, flag_in, flag_sent, flag_got)

    cell_x = lax.broadcasted_iota(jnp.int32, (bx, nz), 0)
    cell_lane = lax.broadcasted_iota(jnp.int32, (bx, nz), 1)
    numbers = map_ref[...].astype(jnp.float32)
    row = jnp.zeros((bx, nz), jnp.float32)
    for y in range(by):
        row = row + jnp.where(cell_lane == bx * y + cell_x, numbers[:, y:y + 1] + 1.0, 0.0)
    tiles[0] = jnp.sum(row, 0, keepdims=True)
    send_all(tiles, 0)

    def joined(buf, pair):
        return buf[2 * pair] + pltpu.roll(buf[2 * pair + 1], nz // 2, 1)

    def hot(number):
        number = number - 1.0
        high = jnp.floor(number * (1.0 / nz))
        low = number - high * nz
        rows = theta_ref.shape[0]
        high_eq = lax.broadcasted_iota(jnp.int32, (rows, nz), 0).astype(jnp.float32) == high
        low_eq = lax.broadcasted_iota(jnp.int32, (nz, nz), 0).astype(jnp.float32) == low
        return jnp.where(high_eq, 1.0, 0.0), jnp.where(low_eq, 1.0, 0.0)

    def split(value):
        one = value.astype(jnp.bfloat16)
        rest = value - one.astype(jnp.float32)
        two = rest.astype(jnp.bfloat16)
        three = (rest - two.astype(jnp.float32)).astype(jnp.bfloat16)
        return jnp.concatenate([one, two, three], 0)

    def add_up(value):
        third = value.shape[0] // 3
        return value[:third] + value[third:2 * third] + value[2 * third:]

    high, low = hot(tiles[0])
    picked = lax.dot_general(split(theta_ref[...]), low.astype(jnp.bfloat16), (((1,), (0,)), ((), ())),
                             preferred_element_type=jnp.float32)
    temperature = jnp.sum(add_up(picked) * high, 0, keepdims=True)

    def lay_plate(x, carry):
        chosen = jnp.where(lane == bx * sub + x, temperature, 0.0)
        total = jnp.sum(chosen, 1, keepdims=True)
        plate[x] = jnp.where(lane == 0, 0.25 * total, 0.0)
        return carry

    lax.fori_loop(0, bx, lay_plate, 0)

    def pack_rows(r, which, values, x, base):
        for k, i in enumerate(Y_UP):
            msg_out[r, base + k, pl.ds(x, 1), :] = values(which(i))[by - 1:by]
        for k, i in enumerate(Y_DOWN):
            msg_out[r, base + 6 + k, pl.ds(x, 1), :] = values(which(i))[0:1]

    def pack_planes(r, which, last, first):
        for k, i in enumerate(X_UP):
            msg_out[r, k] = last(which(i))
        for k, i in enumerate(X_DOWN):
            msg_out[r, 6 + k] = first(which(i))
        msg_out[r, 12] = last(which(7))
        msg_out[r, 13] = first(which(8))
        msg_out[r, 14] = last(which(9))
        msg_out[r, 15] = first(which(10))

    def send_group(r, group):
        send(GROUPS[group][0], msg_out.at[r], msg_in.at[r], msg_sent.at[r], msg_got.at[r, group])

    def wait_group(r, group):
        _, first, count = GROUPS[group]
        wait_for(msg_in.at[r, pl.ds(first, count)], msg_got.at[r, group])

    def unpack_far(r, which, pop, rim, extra=None):
        def arrived(slot, i, side):
            value = msg_in[r, slot]
            return value if extra is None else value + extra(which(i), side)

        for k, i in enumerate(X_UP):
            pop[which(i), 0] = arrived(k, i, 0)
        for k, i in enumerate(X_DOWN):
            pop[which(i), bx + 1] = arrived(6 + k, i, 1)
        rim[which(7), 0:1, :] = msg_in[r, 12, by - 1:by, :]
        rim[which(8), bx + 1:bx + 2, :] = msg_in[r, 13, 0:1, :]
        rim[which(9), 0:1, :] = msg_in[r, 14, 0:1, :]
        rim[which(10), bx + 1:bx + 2, :] = msg_in[r, 15, by - 1:by, :]

    def unpack_inner(r, which, rim, extra=None):
        for side, rows_of, base in ((2, Y_UP, 16), (3, Y_DOWN, 22)):
            for k, i in enumerate(rows_of):
                value = msg_in[r, base + k]
                if extra is not None:
                    value = value + extra(which(i), side)
                rim[which(i), 2:bx, :] = value[1:bx - 1]

    def unpack_edge(r, which, rim, extra=None):
        for side, rows_of, base in ((2, Y_UP, 28), (3, Y_DOWN, 34)):
            for k, i in enumerate(rows_of):
                value = msg_in[r, base + k]
                if extra is not None:
                    value = value + extra(which(i), side)
                rim[which(i), 1:2, :] = value[0:1]
                rim[which(i), bx:bx + 1, :] = value[bx - 1:bx]

    def turn(value, edge, step_y, step_z):
        if step_y == 1:
            value = jnp.where(sub == 0, edge, pltpu.roll(value, 1, 0))
        elif step_y == -1:
            value = jnp.where(sub == by - 1, edge, pltpu.roll(value, by - 1, 0))
        if step_z == 1:
            value = pltpu.roll(value, 1, 1)
        elif step_z == -1:
            value = pltpu.roll(value, nz - 1, 1)
        return value

    def pull(pop, rim, source, i, x):
        step_x, step_y, step_z = VELOCITY[i]
        edge = rim[source, pl.ds(x + 1 - step_x, 1), :] if step_y else None
        return turn(pop[source, x + 1 - step_x], edge, step_y, step_z)

    wait_for(flag_in, flag_got)
    mask_x[0] = flag_in[0]
    mask_x[bx + 1] = flag_in[1]
    mask_lo[1:bx + 1, :] = flag_in[2]
    mask_hi[1:bx + 1, :] = flag_in[3]
    mask_lo[0:1, :] = flag_in[4, by - 1:by, :]
    mask_hi[bx + 1:bx + 2, :] = flag_in[5, 0:1, :]
    mask_hi[0:1, :] = flag_in[6, 0:1, :]
    mask_lo[bx + 1:bx + 2, :] = flag_in[7, by - 1:by, :]

    def fill_table(x, carry):
        for i in range(1, 19):
            step_x, step_y, step_z = VELOCITY[i]
            edge = None
            if step_y:
                edge = (mask_lo if step_y == 1 else mask_hi)[pl.ds(x + 1 - step_x, 1), :]
            value = turn(mask_x[x + 1 - step_x], edge, step_y, step_z)
            if step_z:
                value = jnp.where(lane == (0 if step_z == 1 else nz - 1), 1.0, value)
            table[i, x] = value
        return carry

    lax.fori_loop(0, bx, fill_table, 0)

    def moments_of(s):
        def pairs(i):
            return s[i] + s[i + 1], s[i] - s[i + 1]

        p = {}
        m = {}
        for i in range(1, 19, 2):
            p[i], m[i] = pairs(i)
        density = s[0] + ((p[1] + p[3]) + (p[5] + p[7])) + ((p[9] + p[11]) + (p[13] + p[15])) + p[17]
        speed_x = (m[1] + m[7]) + (m[9] + m[11]) + m[13]
        speed_y = (m[3] + m[7]) + (m[15] + m[17]) - m[9]
        speed_z = (m[5] + m[11]) + (m[15] - m[17]) - m[13]
        temper = (s[19] + s[20]) + (s[21] + s[22]) + (s[23] + s[24]) + s[25]
        return density, speed_x, speed_y, speed_z, temper

    def along(c, a, b, d):
        total = None
        for step, value in zip(c, (a, b, d)):
            if step == 0:
                continue
            if total is None:
                total = value if step == 1 else -value
            else:
                total = total + value if step == 1 else total - value
        return total

    def collide(s):
        density, ux, uy, uz, temper = moments_of(s)
        vz = uz + LIFT * (temper - MEAN_TEMP)
        base = density - 1.5 * (ux * ux + uy * uy + vz * vz)
        post = [None] * 26
        post[0] = (1.0 - OMEGA) * s[0] + (OMEGA * WEIGHTS[0]) * base
        for i in range(1, 19, 2):
            cv = along(VELOCITY[i], ux, uy, vz)
            even = base + (4.5 * cv) * cv
            odd = 3.0 * cv
            weight = OMEGA * WEIGHTS[i]
            post[i] = (1.0 - OMEGA) * s[i] + weight * (even + odd)
            post[i + 1] = (1.0 - OMEGA) * s[i + 1] + weight * (even - odd)
        post[19] = (1.0 - OMEGA) * s[19] + (OMEGA * WEIGHTS[19]) * temper
        share = (OMEGA * WEIGHTS[20]) * temper
        for i, u in ((20, ux), (22, uy), (24, uz)):
            odd = (4.0 * u) * share
            post[i] = (1.0 - OMEGA) * s[i] + (share + odd)
            post[i + 1] = (1.0 - OMEGA) * s[i + 1] + (share - odd)
        return post, (ux, uy, uz, temper)

    def keep(pop, r, which, values, x, base):
        for i in range(26):
            pop[i, x + 1] = values[i]
        pack_rows(r, which, lambda j: values[j], x, base)

    def ship_edges(pop, r, which):
        pack_planes(r, which, lambda j: pop[j, bx], lambda j: pop[j, 1])
        send_group(r, 0)
        send_group(r, 2)

    def remember(k, x, values):
        for part in range(4):
            moments[k, part, x] = values[part]

    inner_pairs = (bx - 4) // 2
    pairs_x = bx // 2

    def place(it):
        inner = it < inner_pairs
        away = pairs_x - 1 - it
        return (jnp.where(inner, 2 + 2 * it, away),
                jnp.where(inner, 3 + 2 * it, bx - 1 - away))

    def whole_step(work, carry, pop, r, which):
        carry = work(0, bx - 1, carry, 28)
        ship_edges(pop, r, which)
        carry = lax.fori_loop(
            0, pairs_x - 1, lambda it, c: work(1 + 2 * it, 2 + 2 * it, c, 16), carry)
        send_group(r, 1)
        return carry

    def fed_step(work, carry, old, rim, r, which, new=None, between=None):
        def pair(it, total):
            @pl.when(it == 0)
            def _():
                wait_group(r, 1)
                unpack_inner(r, which, rim)

            @pl.when(it == inner_pairs)
            def _():
                wait_group(r, 2)
                unpack_edge(r, which, rim)

            @pl.when(it == pairs_x - 1)
            def _():
                if new is not None:
                    send_group(r + 1, 1)
                if between is not None:
                    between()
                wait_group(r, 0)
                unpack_far(r, which, old, rim)

            first, second = place(it)
            return work(first, second, total, jnp.where(it == pairs_x - 1, 28, 16))

        carry = lax.fori_loop(0, pairs_x, pair, carry)
        if new is not None:
            ship_edges(new, r + 1, which)
        return carry

    def propagated(pop, rim, x):
        result = [pop[0, x + 1]] + [None] * 25
        result[19] = pop[19, x + 1]
        for i in range(1, 26):
            if i == 19:
                continue
            solid = table[i if i < 19 else i - 19, x] > 0.5
            back = pop[OPPOSITE[i], x + 1]
            if i == 24:
                back = jnp.where(lane == 0, -back, back)
            elif i == 25:
                back = jnp.where(lane == nz - 1, -back, back)
            result[i] = jnp.where(solid, back, pull(pop, rim, i, i, x))
        result[RISING] = result[RISING] + plate[x]
        return result

    wait_for(tiles.at[pl.ds(1, n - 1)], all_got.at[0])

    def fill_hot(pair, carry):
        high, low = hot(joined(tiles, pair))
        high_hot[pair] = high
        low_hot[pl.ds(pl.multiple_of(pair * nz, nz), nz), :] = low.T.astype(jnp.bfloat16)
        return carry

    lax.fori_loop(0, n // 2, fill_hot, 0)


    own.wait()
    wait_for(start.at[:, pl.ds(0, (n_st - 1) * planes)], check_got)

    def begin(first, second, carry, base):
        done = [collide([start[i, x] for i in range(26)]) for x in (first, second)]
        for x, (post, values) in zip((first, second), done):
            keep(pops.at[0], 0, same, post, x, base)
            remember(0, x, values)
        return carry

    whole_step(begin, 0, pops.at[0], 0, same)

    adj_copy.wait()

    def adj_rows(x, carry):
        pack_rows(ROUND_ADJ, opposite, lambda j: adj[j, x], x, 16)
        return carry

    lax.fori_loop(1, bx - 1, adj_rows, 0)
    for x in (0, bx - 1):
        pack_rows(ROUND_ADJ, opposite, lambda j, x=x: adj[j, x], x, 28)
    pack_planes(ROUND_ADJ, opposite, lambda j: adj[j, bx - 1], lambda j: adj[j, 0])
    for group in range(3):
        send_group(ROUND_ADJ, group)

    def forward(k, carry):
        now = lax.rem(k, 2)
        old, new, rim = pops.at[1 - now], pops.at[now], rims.at[1 - now]

        def advance(first, second, carry, base):
            done = [collide(propagated(old, rim, x)) for x in (first, second)]
            for x, (post, values) in zip((first, second), done):
                keep(new, k, same, post, x, base)
                remember(k, x, values)
            return carry

        return fed_step(advance, carry, old, rim, k - 1, same, new)

    lax.fori_loop(1, STEPS, forward, 0)

    last, rim = pops.at[(STEPS - 1) % 2], rims.at[(STEPS - 1) % 2]

    def finish(first, second, total, base):
        return finish_plane(second, finish_plane(first, total))

    def finish_plane(x, total):
        _, _, _, uz, temper = moments_of(propagated(last, rim, x))
        fluid = 1.0 - mask_x[x + 1]
        warm = fluid * temper
        rise = fluid * uz
        seed[0, x] = warm
        seed[1, x] = rise
        seed_out[4, pl.ds(x, 1), :] = warm[by - 1:by]
        seed_out[5, pl.ds(x, 1), :] = rise[by - 1:by]
        seed_out[6, pl.ds(x, 1), :] = warm[0:1]
        seed_out[7, pl.ds(x, 1), :] = rise[0:1]
        return total + warm * uz

    flux = fed_step(finish, jnp.zeros((by, nz), jnp.float32), last, rim, STEPS - 1, same)
    heat[0] = jnp.sum(flux, 0, keepdims=True)
    send_all(heat, 1)
    seed_out[0] = seed[0, bx - 1]
    seed_out[1] = seed[1, bx - 1]
    seed_out[2] = seed[0, 0]
    seed_out[3] = seed[1, 0]
    send(FACES, seed_out, seed_in, seed_sent, seed_got)
    for group in range(3):
        wait_group(ROUND_ADJ, group)
    wait_for(seed_in, seed_got)
    wait_for(heat.at[pl.ds(1, n - 1)], all_got.at[1])
    heat_sum = jnp.sum(jnp.sum(heat[...], 0), 1, keepdims=True)
    nusselt = 1.0 + heat_sum / (KAPPA * (bx * n_gx * by * n_st))
    nu[...] = nusselt
    gain = jnp.broadcast_to(nusselt - 1.0, (by, nz))

    def seeded(j, warm, rise):
        if j >= 19:
            return gain * rise
        if VELOCITY[j][2] == 0:
            return jnp.zeros((by, nz), jnp.float32)
        return gain * warm if VELOCITY[j][2] == 1 else -(gain * warm)

    def bed_of(value, x):
        return jnp.where(lane == bx * sub + x, 0.25 * value[:, 0:1], 0.0)

    def seed_adjoint(x, total):
        warm = seed[0, x]
        rise = seed[1, x]
        for j in range(26):
            value = adj[j, x] + seeded(j, warm, rise)
            pops[0, j, x + 1] = value
            if j == RISING:
                total = total + bed_of(value, x)
        return total

    total = lax.fori_loop(0, bx, seed_adjoint, jnp.zeros((by, nz), jnp.float32))

    def arrived_seed(j, side):
        return seeded(j, seed_in[2 * side], seed_in[2 * side + 1])

    unpack_far(ROUND_ADJ, opposite, pops.at[0], rims.at[0], arrived_seed)
    unpack_inner(ROUND_ADJ, opposite, rims.at[0], arrived_seed)
    unpack_edge(ROUND_ADJ, opposite, rims.at[0], arrived_seed)

    def pulled_back(pop, rim, x):
        fluid = 1.0 - mask_x[x + 1]
        above = jnp.where(lane == 0, 0.0, fluid)
        below = jnp.where(lane == nz - 1, 0.0, fluid)
        mu = [None] * 26
        mu[0] = pop[0, x + 1]
        mu[19] = pop[19, x + 1]
        for i in range(1, 26):
            if i == 19:
                continue
            step_z = VELOCITY[i][2]
            share = fluid if step_z == 0 else (above if step_z == 1 else below)
            bounce = table[i if i < 19 else i - 19, x]
            if i == 24:
                bounce = jnp.where(lane == 0, -1.0, bounce)
            elif i == 25:
                bounce = jnp.where(lane == nz - 1, -1.0, bounce)
            mu[OPPOSITE[i]] = share * pull(pop, rim, OPPOSITE[i], i, x) + bounce * pop[i, x + 1]
        return mu

    def collide_back(mu, k, x):
        ux = moments[k, 0, x]
        uy = moments[k, 1, x]
        uz = moments[k, 2, x]
        temper = moments[k, 3, x]
        vz = uz + LIFT * (temper - MEAN_TEMP)
        even = {}
        odd = {}
        for i in range(1, 19, 2):
            even[i] = mu[i] + mu[i + 1]
            odd[i] = mu[i] - mu[i + 1]
        axis = OMEGA * WEIGHTS[1]
        diag = OMEGA * WEIGHTS[7]
        xy = diag * (even[7] + even[9])
        xz = diag * (even[11] + even[13])
        yz = diag * (even[15] + even[17])
        ex, ey, ez = axis * even[1], axis * even[3], axis * even[5]
        zero = (OMEGA * WEIGHTS[0]) * mu[0] + ((ex + ey) + (ez + xy)) + (xz + yz)
        sxx = ex + (xy + xz)
        syy = ey + (xy + yz)
        szz = ez + (xz + yz)
        sxy = diag * (even[7] - even[9])
        sxz = diag * (even[11] - even[13])
        syz = diag * (even[15] - even[17])
        one_x = axis * odd[1] + diag * ((odd[7] + odd[9]) + (odd[11] + odd[13]))
        one_y = axis * odd[3] + diag * ((odd[7] - odd[9]) + (odd[15] + odd[17]))
        one_z = axis * odd[5] + diag * ((odd[11] - odd[13]) + (odd[15] - odd[17]))
        bar_x = 3.0 * (one_x - zero * ux) + 9.0 * (sxx * ux + sxy * uy + sxz * vz)
        bar_y = 3.0 * (one_y - zero * uy) + 9.0 * (sxy * ux + syy * uy + syz * vz)
        bar_z = 3.0 * (one_z - zero * vz) + 9.0 * (sxz * ux + syz * uy + szz * vz)
        share = OMEGA * WEIGHTS[20]
        hx = (4.0 * share) * (mu[20] - mu[21])
        hy = (4.0 * share) * (mu[22] - mu[23])
        hz = (4.0 * share) * (mu[24] - mu[25])
        warm = (OMEGA * WEIGHTS[19]) * mu[19] + share * (
            ((mu[20] + mu[21]) + (mu[22] + mu[23])) + (mu[24] + mu[25]))
        bar_t = warm + (hx * ux + hy * uy + hz * uz) + LIFT * bar_z
        bar_x = bar_x + temper * hx
        bar_y = bar_y + temper * hy
        bar_z = bar_z + temper * hz
        lam = [None] * 26
        lam[0] = (1.0 - OMEGA) * mu[0] + zero
        for i in range(1, 19, 2):
            cb = along(VELOCITY[i], bar_x, bar_y, bar_z)
            lam[i] = (1.0 - OMEGA) * mu[i] + (zero + cb)
            lam[i + 1] = (1.0 - OMEGA) * mu[i + 1] + (zero - cb)
        for i in range(19, 26):
            lam[i] = (1.0 - OMEGA) * mu[i] + bar_t
        return lam

    def backward(step, total, fed=True):
        now = lax.rem(step, 2)
        old, new, rim = pops.at[now], pops.at[1 - now], rims.at[now]
        k = STEPS - 1 - step
        r = ROUND_ADJ + step

        def retreat(first, second, total, base):
            done = [collide_back(pulled_back(old, rim, x), k, x) for x in (first, second)]
            for x, values in zip((first, second), done):
                keep(new, r + 1, opposite, values, x, base)
                total = total + bed_of(values[RISING], x)
            return total

        if fed:
            return fed_step(retreat, total, old, rim, r, opposite, new)
        return whole_step(retreat, total, new, r + 1, opposite)

    total = backward(0, total, False)
    total = lax.fori_loop(1, STEPS - 1, backward, total)

    grads[0] = jnp.sum(total, 0, keepdims=True)
    send_all(grads, 2)

    small_out = [pltpu.make_async_copy(source, into, out_sem.at[k]) for k, (source, into) in enumerate(
        ((theta_new, theta_out), (first_new, first_out), (second_new, second_out), (nu, nu_out)))]

    def inner_out():
        return pltpu.make_async_copy(lam.at[:, pl.ds(1, bx - 2)], out_ref.at[:, pl.ds(1, bx - 2)],
                                     out_sem.at[4])

    def edge_out(x, k):
        return pltpu.make_async_copy(lam.at[:, pl.ds(x, 1)], out_ref.at[:, pl.ds(x, 1)],
                                     out_sem.at[k])

    def update_tiles():
        inner_out().start()
        wait_for(grads.at[pl.ds(1, n - 1)], all_got.at[2])
        rows = theta_ref.shape[0]
        pairs = n // 2
        part = 16 if pairs % 16 == 0 else pairs

        def gather_tiles(chunk, total):
            weighted = [split(high_hot[chunk * part + p] * joined(grads, chunk * part + p))
                        for p in range(part)]
            low = low_hot[pl.ds(pl.multiple_of(chunk * (part * nz), nz), part * nz), :]
            return total + jnp.dot(jnp.concatenate(weighted, 1), low,
                                   preferred_element_type=jnp.float32)

        tile_grad = add_up(lax.fori_loop(0, pairs // part, gather_tiles,
                                            jnp.zeros((3 * rows, nz), jnp.float32)))
        first = BETA_ONE * first_ref[...] + (1.0 - BETA_ONE) * tile_grad
        second = BETA_TWO * second_ref[...] + (1.0 - BETA_TWO) * tile_grad * tile_grad
        first_hat = first / (1.0 - BETA_ONE**ADAM_STEP)
        second_hat = second / (1.0 - BETA_TWO**ADAM_STEP)
        first_new[...] = first
        second_new[...] = second
        theta_new[...] = theta_ref[...] - LEARN_RATE * first_hat / (jnp.sqrt(second_hat) + ADAM_EPS)
        for copy in small_out:
            copy.start()

    old, rim = pops.at[(STEPS - 1) % 2], rims.at[(STEPS - 1) % 2]

    def end(first, second, carry, base):
        done = [collide_back(pulled_back(old, rim, x), 0, x) for x in (first, second)]
        for x, values in zip((first, second), done):
            for i in range(26):
                lam[i, x] = values[i]
        return carry

    fed_step(end, 0, old, rim, ROUND_ADJ + STEPS - 1, opposite, between=update_tiles)
    edge_out(0, 5).start()
    edge_out(bx - 1, 6).start()

    wait_for(start.at[:, pl.ds(0, (n_st - 1) * planes)], check_sent)
    wait_for(flag_out, flag_sent)
    wait_for(seed_out, seed_sent)
    for r in range(ROUNDS):
        wait_for(msg_out.at[r], msg_sent.at[r])
    wait_for(tiles.at[pl.ds(1, n - 1)], all_sent.at[0])
    wait_for(heat.at[pl.ds(1, n - 1)], all_sent.at[1])
    wait_for(grads.at[pl.ds(1, n - 1)], all_sent.at[2])
    for copy in small_out:
        copy.wait()
    inner_out().wait()
    edge_out(0, 5).wait()
    edge_out(bx - 1, 6).wait()


def deliver(*refs):
    sem = refs[-1]
    half = (len(refs) - 1) // 2
    copies = [pltpu.make_async_copy(refs[k], refs[half + k], sem.at[k]) for k in range(half)]
    for copy in copies:
        copy.start()
    for copy in copies:
        copy.wait()


def body(n_gx, n_st, checkpoint, adjoint_in, solid_mask, tile_map, theta, first_moment, second_moment):
    bx, by, nz = solid_mask.shape
    planes = checkpoint.shape[1]
    n = n_gx * n_st
    rows = theta.shape[0] // nz
    f32 = jnp.float32
    wide = 16
    vmem = pl.BlockSpec(memory_space=pltpu.VMEM)
    hbm = pl.BlockSpec(memory_space=pltpu.HBM)
    dma = pltpu.SemaphoreType.DMA
    small = jax.ShapeDtypeStruct((rows, nz), f32)
    shapes = (jax.ShapeDtypeStruct((26, bx, by, nz), f32), small, small, small,
              jax.ShapeDtypeStruct((1, 1), f32))
    results = pl.pallas_call(
        functools.partial(kernel, n_gx, n_st, planes),
        out_shape=tuple(pltpu.HBM(value.shape, f32) for value in shapes),
        in_specs=[hbm] * 7,
        out_specs=(hbm,) * 5,
        scratch_shapes=[
            pltpu.VMEM((bx, by, nz), jnp.int32),
            pltpu.VMEM((bx, by), jnp.int32),
            pltpu.VMEM((rows, nz), f32),
            pltpu.VMEM((rows, nz), f32),
            pltpu.VMEM((rows, nz), f32),
            pltpu.VMEM((26, bx, by, nz), f32),
            pltpu.VMEM((1, 1), f32),
            pltpu.VMEM((rows, nz), f32),
            pltpu.VMEM((rows, nz), f32),
            pltpu.VMEM((rows, nz), f32),
            pltpu.VMEM((26, bx, by, nz), f32),
            pltpu.VMEM((26, bx, by, nz), f32),
            pltpu.VMEM((2, 26, bx + 2, by, nz), f32),
            pltpu.VMEM((2, 26, wide, nz), f32),
            pltpu.VMEM((STEPS, 4, bx, by, nz), f32),
            pltpu.VMEM((19, bx, by, nz), f32),
            pltpu.VMEM((bx, by, nz), f32),
            pltpu.VMEM((ROUNDS, 40, by, nz), f32),
            pltpu.VMEM((ROUNDS, 40, by, nz), f32),
            pltpu.VMEM((8, by, nz), f32),
            pltpu.VMEM((8, by, nz), f32),
            pltpu.VMEM((8, by, nz), f32),
            pltpu.VMEM((8, by, nz), f32),
            pltpu.VMEM((2, bx, by, nz), f32),
            pltpu.VMEM((bx + 2, by, nz), f32),
            pltpu.VMEM((wide, nz), f32),
            pltpu.VMEM((wide, nz), f32),
            pltpu.VMEM((n, 1, nz), f32),
            pltpu.VMEM((n, 1, nz), f32),
            pltpu.VMEM((n, 1, nz), f32),
            pltpu.VMEM((n // 2 * nz, nz), jnp.bfloat16),
            pltpu.VMEM((n // 2, rows, nz), f32),
            dma((ROUNDS,)),
            dma((ROUNDS, 3)),
            dma,
            dma,
            dma,
            dma,
            dma((3,)),
            dma((3,)),
            dma,
            dma,
            dma,
            dma,
            dma((5,)),
            dma((7,)),
        ],
        compiler_params=pltpu.CompilerParams(
            collective_id=0, has_side_effects=True, vmem_limit_bytes=40 * 1024 * 1024),
        name="window",
    )(*(pltpu.with_memory_space_constraint(value, pltpu.HBM) for value in (
        checkpoint, adjoint_in, solid_mask, tile_map, theta.reshape(rows, nz),
        first_moment.reshape(rows, nz), second_moment.reshape(rows, nz))))
    adjoint_out, theta_new, first_new, second_new, nusselt = pl.pallas_call(
        deliver,
        out_shape=shapes,
        in_specs=[hbm] * 5,
        out_specs=(hbm,) * 5,
        scratch_shapes=[dma((5,))],
        name="deliver",
    )(*(pltpu.with_memory_space_constraint(value, pltpu.HBM) for value in results))
    flat = theta.shape
    return (adjoint_out, theta_new.reshape(flat), first_new.reshape(flat),
            second_new.reshape(flat), nusselt.reshape(()))


def solution(mesh):
    return jax.shard_map(
        functools.partial(body, mesh.shape["gx"], mesh.shape["st"]),
        mesh=mesh,
        in_specs=(
            P(None, ("gx", "st"), None, None),
            P(None, "gx", "st", None),
            P("gx", "st", None),
            P("gx", "st"),
            P(),
            P(),
            P(),
        ),
        out_specs=(P(None, "gx", "st", None), P(), P(), P(), P()),
        check_vma=False,
    )
```

```python
import functools

import jax
import jax.numpy as jnp
import numpy as np
from jax import lax
from jax.experimental import pallas as pl
from jax.experimental.pallas import tpu as pltpu
from jax.sharding import PartitionSpec as P

STEPS = 4
ADAM_STEP = 100

VELOCITY = [
    (0, 0, 0), (1, 0, 0), (-1, 0, 0), (0, 1, 0), (0, -1, 0), (0, 0, 1), (0, 0, -1),
    (1, 1, 0), (-1, -1, 0), (1, -1, 0), (-1, 1, 0), (1, 0, 1), (-1, 0, -1), (1, 0, -1),
    (-1, 0, 1), (0, 1, 1), (0, -1, -1), (0, 1, -1), (0, -1, 1),
    (0, 0, 0), (1, 0, 0), (-1, 0, 0), (0, 1, 0), (0, -1, 0), (0, 0, 1), (0, 0, -1),
]
WEIGHTS = [1.0 / 3.0] + [1.0 / 18.0] * 6 + [1.0 / 36.0] * 12 + [0.25] + [0.125] * 6
OPPOSITE = [0, 2, 1, 4, 3, 6, 5, 8, 7, 10, 9, 12, 11, 14, 13, 16, 15, 18, 17,
            19, 21, 20, 23, 22, 25, 24]
OMEGA = 1.25
LIFT = 0.8 * 0.001
MEAN_TEMP = 0.5
KAPPA = 0.075
RISING = 24
LEARN_RATE = 0.05
BETA_ONE = 0.9
BETA_TWO = 0.99
ADAM_EPS = 1e-08
MESH = pl.DeviceIdType.MESH

X_UP = [i for i in range(26) if VELOCITY[i][0] == 1]
X_DOWN = [i for i in range(26) if VELOCITY[i][0] == -1]
Y_UP = [i for i in range(26) if VELOCITY[i][1] == 1]
Y_DOWN = [i for i in range(26) if VELOCITY[i][1] == -1]
FAR = [(1, 0, 0, 6), (-1, 0, 6, 6), (1, 1, 12, 1), (-1, -1, 13, 1), (1, -1, 14, 1), (-1, 1, 15, 1)]
INNER = [(0, 1, 16, 6), (0, -1, 22, 6)]
EDGE = [(0, 1, 28, 6), (0, -1, 34, 6)]
GROUPS = [(FAR, 0, 16), (INNER, 16, 12), (EDGE, 28, 12)]
SINGLE = [(1, 0, 0, 1), (-1, 0, 1, 1), (0, 1, 2, 1), (0, -1, 3, 1),
          (1, 1, 4, 1), (-1, -1, 5, 1), (1, -1, 6, 1), (-1, 1, 7, 1)]
FACES = [(1, 0, 0, 2), (-1, 0, 2, 2), (0, 1, 4, 2), (0, -1, 6, 2)]
ROUND_ADJ = STEPS
ROUNDS = 2 * STEPS


def same(i):
    return i


def opposite(i):
    return OPPOSITE[i]


def kernel(n_gx, n_st, planes,
           check_ref, adj_ref, solid_hbm, map_hbm, theta_hbm, first_hbm, second_hbm,
           lam, theta_new, first_new, second_new, nu,
           solid_ref, map_ref, theta_ref, first_ref, second_ref, start, adj, pops, rims, moments, table, plate,
           msg_out, msg_in, flag_out, flag_in, seed_out, seed_in, seed,
           mask_x, mask_lo, mask_hi, tiles, heat, grads, low_hot, high_hot,
           msg_sent, msg_got, flag_sent, flag_got, seed_sent, seed_got,
           all_sent, all_got, check_sent, check_got, own_sem, adj_sem, small_sem):
    bx, by, nz = solid_ref.shape
    gx = lax.axis_index("gx")
    st = lax.axis_index("st")
    n = n_gx * n_st
    me = gx * n_st + st
    sub = lax.broadcasted_iota(jnp.int32, (by, nz), 0)
    lane = lax.broadcasted_iota(jnp.int32, (by, nz), 1)

    own = pltpu.make_async_copy(
        check_ref.at[:, :, pl.ds(pl.multiple_of(st * by, by), by), :],
        start.at[:, pl.ds(st * planes, planes)], own_sem)
    own.start()
    adj_copy = pltpu.make_async_copy(adj_ref, adj, adj_sem)
    adj_copy.start()
    small = [pltpu.make_async_copy(source, into, small_sem.at[k]) for k, (source, into) in enumerate(
        ((solid_hbm, solid_ref), (map_hbm, map_ref), (theta_hbm, theta_ref),
         (first_hbm, first_ref), (second_hbm, second_ref)))]
    for copy in small:
        copy.start()

    def device(offset):
        other = lax.rem(me + offset, n)
        return (other // n_st, lax.rem(other, n_st))

    barrier = pltpu.get_barrier_semaphore()

    @pl.loop(1, n)
    def _(offset):
        pl.semaphore_signal(barrier, inc=1, device_id=device(offset), device_id_type=MESH)

    pl.semaphore_wait(barrier, n - 1)

    def check_copy(step):
        other = lax.rem(st + step, n_st)
        return pltpu.make_async_remote_copy(
            src_ref=check_ref.at[:, :, pl.ds(pl.multiple_of(other * by, by), by), :],
            dst_ref=start.at[:, pl.ds(st * planes, planes)],
            send_sem=check_sent, recv_sem=check_got,
            device_id=(gx, other), device_id_type=MESH)

    for step in range(1, n_st):
        check_copy(step).start()

    def send(messages, out, into, sent, got):
        for dx, dy, first, count in messages:
            pltpu.make_async_remote_copy(
                src_ref=out.at[pl.ds(first, count)], dst_ref=into.at[pl.ds(first, count)],
                send_sem=sent, recv_sem=got,
                device_id=(lax.rem(gx + dx + n_gx, n_gx), lax.rem(st + dy + n_st, n_st)),
                device_id_type=MESH).start()

    def send_all(buf, k):
        @pl.loop(1, n)
        def _(offset):
            pltpu.make_async_remote_copy(
                src_ref=buf.at[0], dst_ref=buf.at[offset],
                send_sem=all_sent.at[k], recv_sem=all_got.at[k],
                device_id=device(offset), device_id_type=MESH).start()

    def wait_for(ref, sem):
        pltpu.make_async_copy(ref, ref, sem).wait()

    for copy in small:
        copy.wait()

    def flags(x, carry):
        value = solid_ref[x].astype(jnp.float32)
        mask_x[x + 1] = value
        flag_out[2, pl.ds(x, 1), :] = value[by - 1:by]
        flag_out[3, pl.ds(x, 1), :] = value[0:1]
        return carry

    lax.fori_loop(0, bx, flags, 0)
    flag_out[0] = mask_x[bx]
    flag_out[1] = mask_x[1]
    flag_out[4] = mask_x[bx]
    flag_out[5] = mask_x[1]
    flag_out[6] = mask_x[bx]
    flag_out[7] = mask_x[1]
    send(SINGLE, flag_out, flag_in, flag_sent, flag_got)

    cell_x = lax.broadcasted_iota(jnp.int32, (bx, nz), 0)
    cell_lane = lax.broadcasted_iota(jnp.int32, (bx, nz), 1)
    numbers = map_ref[...].astype(jnp.float32)
    row = jnp.zeros((bx, nz), jnp.float32)
    for y in range(by):
        row = row + jnp.where(cell_lane == bx * y + cell_x, numbers[:, y:y + 1] + 1.0, 0.0)
    tiles[0] = jnp.sum(row, 0, keepdims=True)
    send_all(tiles, 0)

    def joined(buf, pair):
        return buf[2 * pair] + pltpu.roll(buf[2 * pair + 1], nz // 2, 1)

    def hot(number):
        number = number - 1.0
        high = jnp.floor(number * (1.0 / nz))
        low = number - high * nz
        rows = theta_ref.shape[0]
        high_eq = lax.broadcasted_iota(jnp.int32, (rows, nz), 0).astype(jnp.float32) == high
        low_eq = lax.broadcasted_iota(jnp.int32, (nz, nz), 0).astype(jnp.float32) == low
        return jnp.where(high_eq, 1.0, 0.0), jnp.where(low_eq, 1.0, 0.0)

    def split(value):
        one = value.astype(jnp.bfloat16)
        rest = value - one.astype(jnp.float32)
        two = rest.astype(jnp.bfloat16)
        three = (rest - two.astype(jnp.float32)).astype(jnp.bfloat16)
        return jnp.concatenate([one, two, three], 0)

    def add_up(value):
        third = value.shape[0] // 3
        return value[:third] + value[third:2 * third] + value[2 * third:]

    high, low = hot(tiles[0])
    picked = lax.dot_general(split(theta_ref[...]), low.astype(jnp.bfloat16), (((1,), (0,)), ((), ())),
                             preferred_element_type=jnp.float32)
    temperature = jnp.sum(add_up(picked) * high, 0, keepdims=True)

    def lay_plate(x, carry):
        chosen = jnp.where(lane == bx * sub + x, temperature, 0.0)
        total = jnp.sum(chosen, 1, keepdims=True)
        plate[x] = jnp.where(lane == 0, 0.25 * total, 0.0)
        return carry

    lax.fori_loop(0, bx, lay_plate, 0)

    def pack_rows(r, which, values, x, base):
        for k, i in enumerate(Y_UP):
            msg_out[r, base + k, pl.ds(x, 1), :] = values(which(i))[by - 1:by]
        for k, i in enumerate(Y_DOWN):
            msg_out[r, base + 6 + k, pl.ds(x, 1), :] = values(which(i))[0:1]

    def pack_planes(r, which, last, first):
        for k, i in enumerate(X_UP):
            msg_out[r, k] = last(which(i))
        for k, i in enumerate(X_DOWN):
            msg_out[r, 6 + k] = first(which(i))
        msg_out[r, 12] = last(which(7))
        msg_out[r, 13] = first(which(8))
        msg_out[r, 14] = last(which(9))
        msg_out[r, 15] = first(which(10))

    def send_group(r, group):
        send(GROUPS[group][0], msg_out.at[r], msg_in.at[r], msg_sent.at[r], msg_got.at[r, group])

    def wait_group(r, group):
        _, first, count = GROUPS[group]
        wait_for(msg_in.at[r, pl.ds(first, count)], msg_got.at[r, group])

    def unpack_far(r, which, pop, rim, extra=None):
        def arrived(slot, i, side):
            value = msg_in[r, slot]
            return value if extra is None else value + extra(which(i), side)

        for k, i in enumerate(X_UP):
            pop[which(i), 0] = arrived(k, i, 0)
        for k, i in enumerate(X_DOWN):
            pop[which(i), bx + 1] = arrived(6 + k, i, 1)
        rim[which(7), 0:1, :] = msg_in[r, 12, by - 1:by, :]
        rim[which(8), bx + 1:bx + 2, :] = msg_in[r, 13, 0:1, :]
        rim[which(9), 0:1, :] = msg_in[r, 14, 0:1, :]
        rim[which(10), bx + 1:bx + 2, :] = msg_in[r, 15, by - 1:by, :]

    def unpack_inner(r, which, rim, extra=None):
        for side, rows_of, base in ((2, Y_UP, 16), (3, Y_DOWN, 22)):
            for k, i in enumerate(rows_of):
                value = msg_in[r, base + k]
                if extra is not None:
                    value = value + extra(which(i), side)
                rim[which(i), 2:bx, :] = value[1:bx - 1]

    def unpack_edge(r, which, rim, extra=None):
        for side, rows_of, base in ((2, Y_UP, 28), (3, Y_DOWN, 34)):
            for k, i in enumerate(rows_of):
                value = msg_in[r, base + k]
                if extra is not None:
                    value = value + extra(which(i), side)
                rim[which(i), 1:2, :] = value[0:1]
                rim[which(i), bx:bx + 1, :] = value[bx - 1:bx]

    def turn(value, edge, step_y, step_z):
        if step_y == 1:
            value = jnp.where(sub == 0, edge, pltpu.roll(value, 1, 0))
        elif step_y == -1:
            value = jnp.where(sub == by - 1, edge, pltpu.roll(value, by - 1, 0))
        if step_z == 1:
            value = pltpu.roll(value, 1, 1)
        elif step_z == -1:
            value = pltpu.roll(value, nz - 1, 1)
        return value

    def pull(pop, rim, source, i, x):
        step_x, step_y, step_z = VELOCITY[i]
        edge = rim[source, pl.ds(x + 1 - step_x, 1), :] if step_y else None
        return turn(pop[source, x + 1 - step_x], edge, step_y, step_z)

    wait_for(flag_in, flag_got)
    mask_x[0] = flag_in[0]
    mask_x[bx + 1] = flag_in[1]
    mask_lo[1:bx + 1, :] = flag_in[2]
    mask_hi[1:bx + 1, :] = flag_in[3]
    mask_lo[0:1, :] = flag_in[4, by - 1:by, :]
    mask_hi[bx + 1:bx + 2, :] = flag_in[5, 0:1, :]
    mask_hi[0:1, :] = flag_in[6, 0:1, :]
    mask_lo[bx + 1:bx + 2, :] = flag_in[7, by - 1:by, :]

    def fill_table(x, carry):
        for i in range(1, 19):
            step_x, step_y, step_z = VELOCITY[i]
            edge = None
            if step_y:
                edge = (mask_lo if step_y == 1 else mask_hi)[pl.ds(x + 1 - step_x, 1), :]
            value = turn(mask_x[x + 1 - step_x], edge, step_y, step_z)
            if step_z:
                value = jnp.where(lane == (0 if step_z == 1 else nz - 1), 1.0, value)
            table[i, x] = value
        return carry

    lax.fori_loop(0, bx, fill_table, 0)

    def moments_of(s):
        def pairs(i):
            return s[i] + s[i + 1], s[i] - s[i + 1]

        p = {}
        m = {}
        for i in range(1, 19, 2):
            p[i], m[i] = pairs(i)
        density = s[0] + ((p[1] + p[3]) + (p[5] + p[7])) + ((p[9] + p[11]) + (p[13] + p[15])) + p[17]
        speed_x = (m[1] + m[7]) + (m[9] + m[11]) + m[13]
        speed_y = (m[3] + m[7]) + (m[15] + m[17]) - m[9]
        speed_z = (m[5] + m[11]) + (m[15] - m[17]) - m[13]
        temper = (s[19] + s[20]) + (s[21] + s[22]) + (s[23] + s[24]) + s[25]
        return density, speed_x, speed_y, speed_z, temper

    def along(c, a, b, d):
        total = None
        for step, value in zip(c, (a, b, d)):
            if step == 0:
                continue
            if total is None:
                total = value if step == 1 else -value
            else:
                total = total + value if step == 1 else total - value
        return total

    def collide(s):
        density, ux, uy, uz, temper = moments_of(s)
        vz = uz + LIFT * (temper - MEAN_TEMP)
        base = density - 1.5 * (ux * ux + uy * uy + vz * vz)
        post = [None] * 26
        post[0] = (1.0 - OMEGA) * s[0] + (OMEGA * WEIGHTS[0]) * base
        for i in range(1, 19, 2):
            cv = along(VELOCITY[i], ux, uy, vz)
            even = base + (4.5 * cv) * cv
            odd = 3.0 * cv
            weight = OMEGA * WEIGHTS[i]
            post[i] = (1.0 - OMEGA) * s[i] + weight * (even + odd)
            post[i + 1] = (1.0 - OMEGA) * s[i + 1] + weight * (even - odd)
        post[19] = (1.0 - OMEGA) * s[19] + (OMEGA * WEIGHTS[19]) * temper
        share = (OMEGA * WEIGHTS[20]) * temper
        for i, u in ((20, ux), (22, uy), (24, uz)):
            odd = (4.0 * u) * share
            post[i] = (1.0 - OMEGA) * s[i] + (share + odd)
            post[i + 1] = (1.0 - OMEGA) * s[i + 1] + (share - odd)
        return post, (ux, uy, uz, temper)

    def keep(pop, r, which, values, x, base):
        for i in range(26):
            pop[i, x + 1] = values[i]
        pack_rows(r, which, lambda j: values[j], x, base)

    def ship_edges(pop, r, which):
        pack_planes(r, which, lambda j: pop[j, bx], lambda j: pop[j, 1])
        send_group(r, 0)
        send_group(r, 2)

    def remember(k, x, values):
        for part in range(4):
            moments[k, part, x] = values[part]

    inner_pairs = (bx - 4) // 2
    pairs_x = bx // 2

    def place(it):
        inner = it < inner_pairs
        away = pairs_x - 1 - it
        return (jnp.where(inner, 2 + 2 * it, away),
                jnp.where(inner, 3 + 2 * it, bx - 1 - away))

    def whole_step(work, carry, pop, r, which):
        carry = work(0, bx - 1, carry, 28)
        ship_edges(pop, r, which)
        carry = lax.fori_loop(
            0, pairs_x - 1, lambda it, c: work(1 + 2 * it, 2 + 2 * it, c, 16), carry)
        send_group(r, 1)
        return carry

    def fed_step(work, carry, old, rim, r, which, new=None, between=None):
        def pair(it, total):
            @pl.when(it == 0)
            def _():
                wait_group(r, 1)
                unpack_inner(r, which, rim)

            @pl.when(it == inner_pairs)
            def _():
                wait_group(r, 2)
                unpack_edge(r, which, rim)

            @pl.when(it == pairs_x - 1)
            def _():
                if new is not None:
                    send_group(r + 1, 1)
                if between is not None:
                    between()
                wait_group(r, 0)
                unpack_far(r, which, old, rim)

            first, second = place(it)
            return work(first, second, total, jnp.where(it == pairs_x - 1, 28, 16))

        carry = lax.fori_loop(0, pairs_x, pair, carry)
        if new is not None:
            ship_edges(new, r + 1, which)
        return carry

    def propagated(pop, rim, x):
        result = [pop[0, x + 1]] + [None] * 25
        result[19] = pop[19, x + 1]
        for i in range(1, 26):
            if i == 19:
                continue
            solid = table[i if i < 19 else i - 19, x] > 0.5
            back = pop[OPPOSITE[i], x + 1]
            if i == 24:
                back = jnp.where(lane == 0, -back, back)
            elif i == 25:
                back = jnp.where(lane == nz - 1, -back, back)
            result[i] = jnp.where(solid, back, pull(pop, rim, i, i, x))
        result[RISING] = result[RISING] + plate[x]
        return result

    wait_for(tiles.at[pl.ds(1, n - 1)], all_got.at[0])

    def fill_hot(pair, carry):
        high, low = hot(joined(tiles, pair))
        high_hot[pair] = high
        low_hot[pl.ds(pl.multiple_of(pair * nz, nz), nz), :] = low.T.astype(jnp.bfloat16)
        return carry

    lax.fori_loop(0, n // 2, fill_hot, 0)


    own.wait()
    wait_for(start.at[:, pl.ds(0, (n_st - 1) * planes)], check_got)

    def begin(first, second, carry, base):
        done = [collide([start[i, x] for i in range(26)]) for x in (first, second)]
        for x, (post, values) in zip((first, second), done):
            keep(pops.at[0], 0, same, post, x, base)
            remember(0, x, values)
        return carry

    whole_step(begin, 0, pops.at[0], 0, same)

    adj_copy.wait()

    def adj_rows(x, carry):
        pack_rows(ROUND_ADJ, opposite, lambda j: adj[j, x], x, 16)
        return carry

    lax.fori_loop(1, bx - 1, adj_rows, 0)
    for x in (0, bx - 1):
        pack_rows(ROUND_ADJ, opposite, lambda j, x=x: adj[j, x], x, 28)
    pack_planes(ROUND_ADJ, opposite, lambda j: adj[j, bx - 1], lambda j: adj[j, 0])
    for group in range(3):
        send_group(ROUND_ADJ, group)

    def forward(k, carry):
        now = lax.rem(k, 2)
        old, new, rim = pops.at[1 - now], pops.at[now], rims.at[1 - now]

        def advance(first, second, carry, base):
            done = [collide(propagated(old, rim, x)) for x in (first, second)]
            for x, (post, values) in zip((first, second), done):
                keep(new, k, same, post, x, base)
                remember(k, x, values)
            return carry

        return fed_step(advance, carry, old, rim, k - 1, same, new)

    lax.fori_loop(1, STEPS, forward, 0)

    last, rim = pops.at[(STEPS - 1) % 2], rims.at[(STEPS - 1) % 2]

    def finish(first, second, total, base):
        return finish_plane(second, finish_plane(first, total))

    def finish_plane(x, total):
        _, _, _, uz, temper = moments_of(propagated(last, rim, x))
        fluid = 1.0 - mask_x[x + 1]
        warm = fluid * temper
        rise = fluid * uz
        seed[0, x] = warm
        seed[1, x] = rise
        seed_out[4, pl.ds(x, 1), :] = warm[by - 1:by]
        seed_out[5, pl.ds(x, 1), :] = rise[by - 1:by]
        seed_out[6, pl.ds(x, 1), :] = warm[0:1]
        seed_out[7, pl.ds(x, 1), :] = rise[0:1]
        return total + warm * uz

    flux = fed_step(finish, jnp.zeros((by, nz), jnp.float32), last, rim, STEPS - 1, same)
    heat[0] = jnp.sum(flux, 0, keepdims=True)
    send_all(heat, 1)
    seed_out[0] = seed[0, bx - 1]
    seed_out[1] = seed[1, bx - 1]
    seed_out[2] = seed[0, 0]
    seed_out[3] = seed[1, 0]
    send(FACES, seed_out, seed_in, seed_sent, seed_got)
    for group in range(3):
        wait_group(ROUND_ADJ, group)
    wait_for(seed_in, seed_got)
    wait_for(heat.at[pl.ds(1, n - 1)], all_got.at[1])
    heat_sum = jnp.sum(jnp.sum(heat[...], 0), 1, keepdims=True)
    nusselt = 1.0 + heat_sum / (KAPPA * (bx * n_gx * by * n_st))
    nu[...] = jnp.broadcast_to(nusselt, nu.shape)
    gain = jnp.broadcast_to(nusselt - 1.0, (by, nz))

    def seeded(j, warm, rise):
        if j >= 19:
            return gain * rise
        if VELOCITY[j][2] == 0:
            return jnp.zeros((by, nz), jnp.float32)
        return gain * warm if VELOCITY[j][2] == 1 else -(gain * warm)

    def bed_of(value, x):
        return jnp.where(lane == bx * sub + x, 0.25 * value[:, 0:1], 0.0)

    def seed_adjoint(x, total):
        warm = seed[0, x]
        rise = seed[1, x]
        for j in range(26):
            value = adj[j, x] + seeded(j, warm, rise)
            pops[0, j, x + 1] = value
            if j == RISING:
                total = total + bed_of(value, x)
        return total

    total = lax.fori_loop(0, bx, seed_adjoint, jnp.zeros((by, nz), jnp.float32))

    def arrived_seed(j, side):
        return seeded(j, seed_in[2 * side], seed_in[2 * side + 1])

    unpack_far(ROUND_ADJ, opposite, pops.at[0], rims.at[0], arrived_seed)
    unpack_inner(ROUND_ADJ, opposite, rims.at[0], arrived_seed)
    unpack_edge(ROUND_ADJ, opposite, rims.at[0], arrived_seed)

    def pulled_back(pop, rim, x):
        fluid = 1.0 - mask_x[x + 1]
        above = jnp.where(lane == 0, 0.0, fluid)
        below = jnp.where(lane == nz - 1, 0.0, fluid)
        mu = [None] * 26
        mu[0] = pop[0, x + 1]
        mu[19] = pop[19, x + 1]
        for i in range(1, 26):
            if i == 19:
                continue
            step_z = VELOCITY[i][2]
            share = fluid if step_z == 0 else (above if step_z == 1 else below)
            bounce = table[i if i < 19 else i - 19, x]
            if i == 24:
                bounce = jnp.where(lane == 0, -1.0, bounce)
            elif i == 25:
                bounce = jnp.where(lane == nz - 1, -1.0, bounce)
            mu[OPPOSITE[i]] = share * pull(pop, rim, OPPOSITE[i], i, x) + bounce * pop[i, x + 1]
        return mu

    def collide_back(mu, k, x):
        ux = moments[k, 0, x]
        uy = moments[k, 1, x]
        uz = moments[k, 2, x]
        temper = moments[k, 3, x]
        vz = uz + LIFT * (temper - MEAN_TEMP)
        even = {}
        odd = {}
        for i in range(1, 19, 2):
            even[i] = mu[i] + mu[i + 1]
            odd[i] = mu[i] - mu[i + 1]
        axis = OMEGA * WEIGHTS[1]
        diag = OMEGA * WEIGHTS[7]
        xy = diag * (even[7] + even[9])
        xz = diag * (even[11] + even[13])
        yz = diag * (even[15] + even[17])
        ex, ey, ez = axis * even[1], axis * even[3], axis * even[5]
        zero = (OMEGA * WEIGHTS[0]) * mu[0] + ((ex + ey) + (ez + xy)) + (xz + yz)
        sxx = ex + (xy + xz)
        syy = ey + (xy + yz)
        szz = ez + (xz + yz)
        sxy = diag * (even[7] - even[9])
        sxz = diag * (even[11] - even[13])
        syz = diag * (even[15] - even[17])
        one_x = axis * odd[1] + diag * ((odd[7] + odd[9]) + (odd[11] + odd[13]))
        one_y = axis * odd[3] + diag * ((odd[7] - odd[9]) + (odd[15] + odd[17]))
        one_z = axis * odd[5] + diag * ((odd[11] - odd[13]) + (odd[15] - odd[17]))
        bar_x = 3.0 * (one_x - zero * ux) + 9.0 * (sxx * ux + sxy * uy + sxz * vz)
        bar_y = 3.0 * (one_y - zero * uy) + 9.0 * (sxy * ux + syy * uy + syz * vz)
        bar_z = 3.0 * (one_z - zero * vz) + 9.0 * (sxz * ux + syz * uy + szz * vz)
        share = OMEGA * WEIGHTS[20]
        hx = (4.0 * share) * (mu[20] - mu[21])
        hy = (4.0 * share) * (mu[22] - mu[23])
        hz = (4.0 * share) * (mu[24] - mu[25])
        warm = (OMEGA * WEIGHTS[19]) * mu[19] + share * (
            ((mu[20] + mu[21]) + (mu[22] + mu[23])) + (mu[24] + mu[25]))
        bar_t = warm + (hx * ux + hy * uy + hz * uz) + LIFT * bar_z
        bar_x = bar_x + temper * hx
        bar_y = bar_y + temper * hy
        bar_z = bar_z + temper * hz
        lam = [None] * 26
        lam[0] = (1.0 - OMEGA) * mu[0] + zero
        for i in range(1, 19, 2):
            cb = along(VELOCITY[i], bar_x, bar_y, bar_z)
            lam[i] = (1.0 - OMEGA) * mu[i] + (zero + cb)
            lam[i + 1] = (1.0 - OMEGA) * mu[i + 1] + (zero - cb)
        for i in range(19, 26):
            lam[i] = (1.0 - OMEGA) * mu[i] + bar_t
        return lam

    def backward(step, total, fed=True):
        now = lax.rem(step, 2)
        old, new, rim = pops.at[now], pops.at[1 - now], rims.at[now]
        k = STEPS - 1 - step
        r = ROUND_ADJ + step

        def retreat(first, second, total, base):
            done = [collide_back(pulled_back(old, rim, x), k, x) for x in (first, second)]
            for x, values in zip((first, second), done):
                keep(new, r + 1, opposite, values, x, base)
                total = total + bed_of(values[RISING], x)
            return total

        if fed:
            return fed_step(retreat, total, old, rim, r, opposite, new)
        return whole_step(retreat, total, new, r + 1, opposite)

    total = backward(0, total, False)
    total = lax.fori_loop(1, STEPS - 1, backward, total)

    grads[0] = jnp.sum(total, 0, keepdims=True)
    send_all(grads, 2)

    def update_tiles():
        wait_for(grads.at[pl.ds(1, n - 1)], all_got.at[2])
        rows = theta_ref.shape[0]
        pairs = n // 2
        part = 16 if pairs % 16 == 0 else pairs

        def gather_tiles(chunk, total):
            weighted = [split(high_hot[chunk * part + p] * joined(grads, chunk * part + p))
                        for p in range(part)]
            low = low_hot[pl.ds(pl.multiple_of(chunk * (part * nz), nz), part * nz), :]
            return total + jnp.dot(jnp.concatenate(weighted, 1), low,
                                   preferred_element_type=jnp.float32)

        tile_grad = add_up(lax.fori_loop(0, pairs // part, gather_tiles,
                                            jnp.zeros((3 * rows, nz), jnp.float32)))
        first = BETA_ONE * first_ref[...] + (1.0 - BETA_ONE) * tile_grad
        second = BETA_TWO * second_ref[...] + (1.0 - BETA_TWO) * tile_grad * tile_grad
        first_hat = first / (1.0 - BETA_ONE**ADAM_STEP)
        second_hat = second / (1.0 - BETA_TWO**ADAM_STEP)
        first_new[...] = first
        second_new[...] = second
        theta_new[...] = theta_ref[...] - LEARN_RATE * first_hat / (jnp.sqrt(second_hat) + ADAM_EPS)

    old, rim = pops.at[(STEPS - 1) % 2], rims.at[(STEPS - 1) % 2]

    def end(first, second, carry, base):
        done = [collide_back(pulled_back(old, rim, x), 0, x) for x in (first, second)]
        for x, values in zip((first, second), done):
            for i in range(26):
                lam[i, x] = values[i]
        return carry

    fed_step(end, 0, old, rim, ROUND_ADJ + STEPS - 1, opposite, between=update_tiles)

    wait_for(start.at[:, pl.ds(0, (n_st - 1) * planes)], check_sent)
    wait_for(flag_out, flag_sent)
    wait_for(seed_out, seed_sent)
    for r in range(ROUNDS):
        wait_for(msg_out.at[r], msg_sent.at[r])
    wait_for(tiles.at[pl.ds(1, n - 1)], all_sent.at[0])
    wait_for(heat.at[pl.ds(1, n - 1)], all_sent.at[1])
    wait_for(grads.at[pl.ds(1, n - 1)], all_sent.at[2])


def deliver(lam, theta_new, first_new, second_new, nu, lam_out, theta_out, first_out, second_out, nu_out,
            scalar, sem):
    scalar[...] = nu[0:1, 0:1]
    pairs = ((lam, lam_out), (theta_new, theta_out), (first_new, first_out),
             (second_new, second_out), (scalar, nu_out))
    copies = [pltpu.make_async_copy(source, into, sem.at[k]) for k, (source, into) in enumerate(pairs)]
    for copy in copies:
        copy.start()
    for copy in copies:
        copy.wait()


def body(n_gx, n_st, checkpoint, adjoint_in, solid_mask, tile_map, theta, first_moment, second_moment):
    bx, by, nz = solid_mask.shape
    planes = checkpoint.shape[1]
    n = n_gx * n_st
    rows = theta.shape[0] // nz
    f32 = jnp.float32
    wide = 16
    vmem = pl.BlockSpec(memory_space=pltpu.VMEM)
    hbm = pl.BlockSpec(memory_space=pltpu.HBM)
    dma = pltpu.SemaphoreType.DMA
    small = jax.ShapeDtypeStruct((rows, nz), f32)
    shapes = (jax.ShapeDtypeStruct((26, bx, by, nz), f32), small, small, small,
              jax.ShapeDtypeStruct((1, 1), f32))
    results = pl.pallas_call(
        functools.partial(kernel, n_gx, n_st, planes),
        out_shape=tuple(pltpu.VMEM(value.shape, f32) for value in shapes[:4]) + (
            pltpu.VMEM((by, nz), f32),),
        in_specs=[hbm] * 7,
        out_specs=(vmem,) * 5,
        scratch_shapes=[
            pltpu.VMEM((bx, by, nz), jnp.int32),
            pltpu.VMEM((bx, by), jnp.int32),
            pltpu.VMEM((rows, nz), f32),
            pltpu.VMEM((rows, nz), f32),
            pltpu.VMEM((rows, nz), f32),
            pltpu.VMEM((26, bx, by, nz), f32),
            pltpu.VMEM((26, bx, by, nz), f32),
            pltpu.VMEM((2, 26, bx + 2, by, nz), f32),
            pltpu.VMEM((2, 26, wide, nz), f32),
            pltpu.VMEM((STEPS, 4, bx, by, nz), f32),
            pltpu.VMEM((19, bx, by, nz), f32),
            pltpu.VMEM((bx, by, nz), f32),
            pltpu.VMEM((ROUNDS, 40, by, nz), f32),
            pltpu.VMEM((ROUNDS, 40, by, nz), f32),
            pltpu.VMEM((8, by, nz), f32),
            pltpu.VMEM((8, by, nz), f32),
            pltpu.VMEM((8, by, nz), f32),
            pltpu.VMEM((8, by, nz), f32),
            pltpu.VMEM((2, bx, by, nz), f32),
            pltpu.VMEM((bx + 2, by, nz), f32),
            pltpu.VMEM((wide, nz), f32),
            pltpu.VMEM((wide, nz), f32),
            pltpu.VMEM((n, 1, nz), f32),
            pltpu.VMEM((n, 1, nz), f32),
            pltpu.VMEM((n, 1, nz), f32),
            pltpu.VMEM((n // 2 * nz, nz), jnp.bfloat16),
            pltpu.VMEM((n // 2, rows, nz), f32),
            dma((ROUNDS,)),
            dma((ROUNDS, 3)),
            dma,
            dma,
            dma,
            dma,
            dma((3,)),
            dma((3,)),
            dma,
            dma,
            dma,
            dma,
            dma((5,)),
        ],
        compiler_params=pltpu.CompilerParams(
            collective_id=0, has_side_effects=True, vmem_limit_bytes=40 * 1024 * 1024),
        name="window",
    )(*(pltpu.with_memory_space_constraint(value, pltpu.HBM) for value in (
        checkpoint, adjoint_in, solid_mask, tile_map, theta.reshape(rows, nz),
        first_moment.reshape(rows, nz), second_moment.reshape(rows, nz))))
    adjoint_out, theta_new, first_new, second_new, nusselt = pl.pallas_call(
        deliver,
        out_shape=shapes,
        in_specs=[vmem] * 5,
        out_specs=(hbm,) * 5,
        scratch_shapes=[pltpu.VMEM((1, 1), f32), dma((5,))],
        name="deliver",
    )(*(pltpu.with_memory_space_constraint(value, pltpu.VMEM) for value in results))
    flat = theta.shape
    return (adjoint_out, theta_new.reshape(flat), first_new.reshape(flat),
            second_new.reshape(flat), nusselt.reshape(()))


def solution(mesh):
    return jax.shard_map(
        functools.partial(body, mesh.shape["gx"], mesh.shape["st"]),
        mesh=mesh,
        in_specs=(
            P(None, ("gx", "st"), None, None),
            P(None, "gx", "st", None),
            P("gx", "st", None),
            P("gx", "st"),
            P(),
            P(),
            P(),
        ),
        out_specs=(P(None, "gx", "st", None), P(), P(), P(), P()),
        check_vma=False,
    )
```

```python
import functools

import jax
import jax.numpy as jnp
import numpy as np
from jax import lax
from jax.experimental import pallas as pl
from jax.experimental.pallas import tpu as pltpu
from jax.sharding import PartitionSpec as P

STEPS = 4
ADAM_STEP = 100

VELOCITY = [
    (0, 0, 0), (1, 0, 0), (-1, 0, 0), (0, 1, 0), (0, -1, 0), (0, 0, 1), (0, 0, -1),
    (1, 1, 0), (-1, -1, 0), (1, -1, 0), (-1, 1, 0), (1, 0, 1), (-1, 0, -1), (1, 0, -1),
    (-1, 0, 1), (0, 1, 1), (0, -1, -1), (0, 1, -1), (0, -1, 1),
    (0, 0, 0), (1, 0, 0), (-1, 0, 0), (0, 1, 0), (0, -1, 0), (0, 0, 1), (0, 0, -1),
]
WEIGHTS = [1.0 / 3.0] + [1.0 / 18.0] * 6 + [1.0 / 36.0] * 12 + [0.25] + [0.125] * 6
OPPOSITE = [0, 2, 1, 4, 3, 6, 5, 8, 7, 10, 9, 12, 11, 14, 13, 16, 15, 18, 17,
            19, 21, 20, 23, 22, 25, 24]
OMEGA = 1.25
LIFT = 0.8 * 0.001
MEAN_TEMP = 0.5
KAPPA = 0.075
RISING = 24
LEARN_RATE = 0.05
BETA_ONE = 0.9
BETA_TWO = 0.99
ADAM_EPS = 1e-08
MESH = pl.DeviceIdType.MESH

X_UP = [i for i in range(26) if VELOCITY[i][0] == 1]
X_DOWN = [i for i in range(26) if VELOCITY[i][0] == -1]
Y_UP = [i for i in range(26) if VELOCITY[i][1] == 1]
Y_DOWN = [i for i in range(26) if VELOCITY[i][1] == -1]
FAR = [(1, 0, 0, 6), (-1, 0, 6, 6), (1, 1, 12, 1), (-1, -1, 13, 1), (1, -1, 14, 1), (-1, 1, 15, 1)]
INNER = [(0, 1, 16, 6), (0, -1, 22, 6)]
EDGE = [(0, 1, 28, 6), (0, -1, 34, 6)]
GROUPS = [(FAR, 0, 16), (INNER, 16, 12), (EDGE, 28, 12)]
SINGLE = [(1, 0, 0, 1), (-1, 0, 1, 1), (0, 1, 2, 1), (0, -1, 3, 1),
          (1, 1, 4, 1), (-1, -1, 5, 1), (1, -1, 6, 1), (-1, 1, 7, 1)]
FACES = [(1, 0, 0, 2), (-1, 0, 2, 2), (0, 1, 4, 2), (0, -1, 6, 2)]
ROUND_ADJ = STEPS
ROUNDS = 2 * STEPS


def same(i):
    return i


def opposite(i):
    return OPPOSITE[i]


def kernel(n_gx, n_st, planes,
           check_ref, adj_ref, solid_hbm, map_hbm, theta_hbm, first_hbm, second_hbm,
           lam, theta_new, first_new, second_new, nu,
           solid_ref, map_ref, theta_ref, first_ref, second_ref, start, adj, pops, rims, moments, table, plate,
           msg_out, msg_in, flag_out, flag_in, seed_out, seed_in, seed,
           mask_x, mask_lo, mask_hi, tiles, heat, grads, low_hot, high_hot,
           msg_sent, msg_got, flag_sent, flag_got, seed_sent, seed_got,
           all_sent, all_got, check_sent, check_got, own_sem, adj_sem, small_sem):
    bx, by, nz = solid_ref.shape
    gx = lax.axis_index("gx")
    st = lax.axis_index("st")
    n = n_gx * n_st
    me = gx * n_st + st
    sub = lax.broadcasted_iota(jnp.int32, (by, nz), 0)
    lane = lax.broadcasted_iota(jnp.int32, (by, nz), 1)

    own = pltpu.make_async_copy(
        check_ref.at[:, :, pl.ds(pl.multiple_of(st * by, by), by), :],
        start.at[:, pl.ds(st * planes, planes)], own_sem)
    own.start()
    adj_copy = pltpu.make_async_copy(adj_ref, adj, adj_sem)
    adj_copy.start()
    small = [pltpu.make_async_copy(source, into, small_sem.at[k]) for k, (source, into) in enumerate(
        ((solid_hbm, solid_ref), (map_hbm, map_ref), (theta_hbm, theta_ref),
         (first_hbm, first_ref), (second_hbm, second_ref)))]
    for copy in small:
        copy.start()

    def device(offset):
        other = lax.rem(me + offset, n)
        return (other // n_st, lax.rem(other, n_st))

    barrier = pltpu.get_barrier_semaphore()

    @pl.loop(1, n)
    def _(offset):
        pl.semaphore_signal(barrier, inc=1, device_id=device(offset), device_id_type=MESH)

    pl.semaphore_wait(barrier, n - 1)

    def check_copy(step):
        other = lax.rem(st + step, n_st)
        return pltpu.make_async_remote_copy(
            src_ref=check_ref.at[:, :, pl.ds(pl.multiple_of(other * by, by), by), :],
            dst_ref=start.at[:, pl.ds(st * planes, planes)],
            send_sem=check_sent, recv_sem=check_got,
            device_id=(gx, other), device_id_type=MESH)

    for step in sorted(range(1, n_st), key=lambda hop: -min(hop, n_st - hop)):
        check_copy(step).start()

    def send(messages, out, into, sent, got):
        for dx, dy, first, count in messages:
            pltpu.make_async_remote_copy(
                src_ref=out.at[pl.ds(first, count)], dst_ref=into.at[pl.ds(first, count)],
                send_sem=sent, recv_sem=got,
                device_id=(lax.rem(gx + dx + n_gx, n_gx), lax.rem(st + dy + n_st, n_st)),
                device_id_type=MESH).start()

    def send_all(buf, k):
        @pl.loop(1, n)
        def _(offset):
            pltpu.make_async_remote_copy(
                src_ref=buf.at[0], dst_ref=buf.at[offset],
                send_sem=all_sent.at[k], recv_sem=all_got.at[k],
                device_id=device(offset), device_id_type=MESH).start()

    def wait_for(ref, sem):
        pltpu.make_async_copy(ref, ref, sem).wait()

    for copy in small:
        copy.wait()

    def flags(x, carry):
        value = solid_ref[x].astype(jnp.float32)
        mask_x[x + 1] = value
        flag_out[2, pl.ds(x, 1), :] = value[by - 1:by]
        flag_out[3, pl.ds(x, 1), :] = value[0:1]
        return carry

    lax.fori_loop(0, bx, flags, 0)
    flag_out[0] = mask_x[bx]
    flag_out[1] = mask_x[1]
    flag_out[4] = mask_x[bx]
    flag_out[5] = mask_x[1]
    flag_out[6] = mask_x[bx]
    flag_out[7] = mask_x[1]
    send(SINGLE, flag_out, flag_in, flag_sent, flag_got)

    cell_x = lax.broadcasted_iota(jnp.int32, (bx, nz), 0)
    cell_lane = lax.broadcasted_iota(jnp.int32, (bx, nz), 1)
    numbers = map_ref[...].astype(jnp.float32)
    row = jnp.zeros((bx, nz), jnp.float32)
    for y in range(by):
        row = row + jnp.where(cell_lane == bx * y + cell_x, numbers[:, y:y + 1] + 1.0, 0.0)
    tiles[0] = jnp.sum(row, 0, keepdims=True)
    send_all(tiles, 0)

    def joined(buf, pair):
        return buf[2 * pair] + pltpu.roll(buf[2 * pair + 1], nz // 2, 1)

    def hot(number):
        number = number - 1.0
        high = jnp.floor(number * (1.0 / nz))
        low = number - high * nz
        rows = theta_ref.shape[0]
        high_eq = lax.broadcasted_iota(jnp.int32, (rows, nz), 0).astype(jnp.float32) == high
        low_eq = lax.broadcasted_iota(jnp.int32, (nz, nz), 0).astype(jnp.float32) == low
        return jnp.where(high_eq, 1.0, 0.0), jnp.where(low_eq, 1.0, 0.0)

    def split(value):
        one = value.astype(jnp.bfloat16)
        rest = value - one.astype(jnp.float32)
        two = rest.astype(jnp.bfloat16)
        three = (rest - two.astype(jnp.float32)).astype(jnp.bfloat16)
        return jnp.concatenate([one, two, three], 0)

    def add_up(value):
        third = value.shape[0] // 3
        return value[:third] + value[third:2 * third] + value[2 * third:]

    high, low = hot(tiles[0])
    picked = lax.dot_general(split(theta_ref[...]), low.astype(jnp.bfloat16), (((1,), (0,)), ((), ())),
                             preferred_element_type=jnp.float32)
    temperature = jnp.sum(add_up(picked) * high, 0, keepdims=True)

    def lay_plate(x, carry):
        chosen = jnp.where(lane == bx * sub + x, temperature, 0.0)
        total = jnp.sum(chosen, 1, keepdims=True)
        plate[x] = jnp.where(lane == 0, 0.25 * total, 0.0)
        return carry

    lax.fori_loop(0, bx, lay_plate, 0)

    def pack_rows(r, which, values, x, base):
        for k, i in enumerate(Y_UP):
            msg_out[r, base + k, pl.ds(x, 1), :] = values(which(i))[by - 1:by]
        for k, i in enumerate(Y_DOWN):
            msg_out[r, base + 6 + k, pl.ds(x, 1), :] = values(which(i))[0:1]

    def pack_planes(r, which, last, first):
        for k, i in enumerate(X_UP):
            msg_out[r, k] = last(which(i))
        for k, i in enumerate(X_DOWN):
            msg_out[r, 6 + k] = first(which(i))
        msg_out[r, 12] = last(which(7))
        msg_out[r, 13] = first(which(8))
        msg_out[r, 14] = last(which(9))
        msg_out[r, 15] = first(which(10))

    def send_group(r, group):
        send(GROUPS[group][0], msg_out.at[r], msg_in.at[r], msg_sent.at[r], msg_got.at[r, group])

    def wait_group(r, group):
        _, first, count = GROUPS[group]
        wait_for(msg_in.at[r, pl.ds(first, count)], msg_got.at[r, group])

    def unpack_far(r, which, pop, rim, extra=None):
        def arrived(slot, i, side):
            value = msg_in[r, slot]
            return value if extra is None else value + extra(which(i), side)

        for k, i in enumerate(X_UP):
            pop[which(i), 0] = arrived(k, i, 0)
        for k, i in enumerate(X_DOWN):
            pop[which(i), bx + 1] = arrived(6 + k, i, 1)
        rim[which(7), 0:1, :] = msg_in[r, 12, by - 1:by, :]
        rim[which(8), bx + 1:bx + 2, :] = msg_in[r, 13, 0:1, :]
        rim[which(9), 0:1, :] = msg_in[r, 14, 0:1, :]
        rim[which(10), bx + 1:bx + 2, :] = msg_in[r, 15, by - 1:by, :]

    def unpack_inner(r, which, rim, extra=None):
        for side, rows_of, base in ((2, Y_UP, 16), (3, Y_DOWN, 22)):
            for k, i in enumerate(rows_of):
                value = msg_in[r, base + k]
                if extra is not None:
                    value = value + extra(which(i), side)
                rim[which(i), 2:bx, :] = value[1:bx - 1]

    def unpack_edge(r, which, rim, extra=None):
        for side, rows_of, base in ((2, Y_UP, 28), (3, Y_DOWN, 34)):
            for k, i in enumerate(rows_of):
                value = msg_in[r, base + k]
                if extra is not None:
                    value = value + extra(which(i), side)
                rim[which(i), 1:2, :] = value[0:1]
                rim[which(i), bx:bx + 1, :] = value[bx - 1:bx]

    def turn(value, edge, step_y, step_z):
        if step_y == 1:
            value = jnp.where(sub == 0, edge, pltpu.roll(value, 1, 0))
        elif step_y == -1:
            value = jnp.where(sub == by - 1, edge, pltpu.roll(value, by - 1, 0))
        if step_z == 1:
            value = pltpu.roll(value, 1, 1)
        elif step_z == -1:
            value = pltpu.roll(value, nz - 1, 1)
        return value

    def pull(pop, rim, source, i, x):
        step_x, step_y, step_z = VELOCITY[i]
        edge = rim[source, pl.ds(x + 1 - step_x, 1), :] if step_y else None
        return turn(pop[source, x + 1 - step_x], edge, step_y, step_z)

    wait_for(flag_in, flag_got)
    mask_x[0] = flag_in[0]
    mask_x[bx + 1] = flag_in[1]
    mask_lo[1:bx + 1, :] = flag_in[2]
    mask_hi[1:bx + 1, :] = flag_in[3]
    mask_lo[0:1, :] = flag_in[4, by - 1:by, :]
    mask_hi[bx + 1:bx + 2, :] = flag_in[5, 0:1, :]
    mask_hi[0:1, :] = flag_in[6, 0:1, :]
    mask_lo[bx + 1:bx + 2, :] = flag_in[7, by - 1:by, :]

    def fill_table(x, carry):
        for i in range(1, 19):
            step_x, step_y, step_z = VELOCITY[i]
            edge = None
            if step_y:
                edge = (mask_lo if step_y == 1 else mask_hi)[pl.ds(x + 1 - step_x, 1), :]
            value = turn(mask_x[x + 1 - step_x], edge, step_y, step_z)
            if step_z:
                value = jnp.where(lane == (0 if step_z == 1 else nz - 1), 1.0, value)
            table[i, x] = value
        return carry

    lax.fori_loop(0, bx, fill_table, 0)

    def moments_of(s):
        def pairs(i):
            return s[i] + s[i + 1], s[i] - s[i + 1]

        p = {}
        m = {}
        for i in range(1, 19, 2):
            p[i], m[i] = pairs(i)
        density = s[0] + ((p[1] + p[3]) + (p[5] + p[7])) + ((p[9] + p[11]) + (p[13] + p[15])) + p[17]
        speed_x = (m[1] + m[7]) + (m[9] + m[11]) + m[13]
        speed_y = (m[3] + m[7]) + (m[15] + m[17]) - m[9]
        speed_z = (m[5] + m[11]) + (m[15] - m[17]) - m[13]
        temper = (s[19] + s[20]) + (s[21] + s[22]) + (s[23] + s[24]) + s[25]
        return density, speed_x, speed_y, speed_z, temper

    def along(c, a, b, d):
        total = None
        for step, value in zip(c, (a, b, d)):
            if step == 0:
                continue
            if total is None:
                total = value if step == 1 else -value
            else:
                total = total + value if step == 1 else total - value
        return total

    def collide(s):
        density, ux, uy, uz, temper = moments_of(s)
        vz = uz + LIFT * (temper - MEAN_TEMP)
        base = density - 1.5 * (ux * ux + uy * uy + vz * vz)
        post = [None] * 26
        post[0] = (1.0 - OMEGA) * s[0] + (OMEGA * WEIGHTS[0]) * base
        for i in range(1, 19, 2):
            cv = along(VELOCITY[i], ux, uy, vz)
            even = base + (4.5 * cv) * cv
            odd = 3.0 * cv
            weight = OMEGA * WEIGHTS[i]
            post[i] = (1.0 - OMEGA) * s[i] + weight * (even + odd)
            post[i + 1] = (1.0 - OMEGA) * s[i + 1] + weight * (even - odd)
        post[19] = (1.0 - OMEGA) * s[19] + (OMEGA * WEIGHTS[19]) * temper
        share = (OMEGA * WEIGHTS[20]) * temper
        for i, u in ((20, ux), (22, uy), (24, uz)):
            odd = (4.0 * u) * share
            post[i] = (1.0 - OMEGA) * s[i] + (share + odd)
            post[i + 1] = (1.0 - OMEGA) * s[i + 1] + (share - odd)
        return post, (ux, uy, uz, temper)

    def keep(pop, r, which, values, x, base):
        for i in range(26):
            pop[i, x + 1] = values[i]
        pack_rows(r, which, lambda j: values[j], x, base)

    def ship_edges(pop, r, which):
        pack_planes(r, which, lambda j: pop[j, bx], lambda j: pop[j, 1])
        send_group(r, 0)
        send_group(r, 2)

    def remember(k, x, values):
        for part in range(4):
            moments[k, part, x] = values[part]

    inner_pairs = (bx - 4) // 2
    pairs_x = bx // 2

    def place(it):
        inner = it < inner_pairs
        away = pairs_x - 1 - it
        return (jnp.where(inner, 2 + 2 * it, away),
                jnp.where(inner, 3 + 2 * it, bx - 1 - away))

    def whole_step(work, carry, pop, r, which):
        carry = work(0, bx - 1, carry, 28)
        ship_edges(pop, r, which)
        carry = lax.fori_loop(
            0, pairs_x - 1, lambda it, c: work(1 + 2 * it, 2 + 2 * it, c, 16), carry)
        send_group(r, 1)
        return carry

    def fed_step(work, carry, old, rim, r, which, new=None, between=None):
        def pair(it, total):
            @pl.when(it == 0)
            def _():
                wait_group(r, 1)
                unpack_inner(r, which, rim)

            @pl.when(it == inner_pairs)
            def _():
                wait_group(r, 2)
                unpack_edge(r, which, rim)

            @pl.when(it == pairs_x - 1)
            def _():
                if new is not None:
                    send_group(r + 1, 1)
                if between is not None:
                    between()
                wait_group(r, 0)
                unpack_far(r, which, old, rim)

            first, second = place(it)
            return work(first, second, total, jnp.where(it == pairs_x - 1, 28, 16))

        carry = lax.fori_loop(0, pairs_x, pair, carry)
        if new is not None:
            ship_edges(new, r + 1, which)
        return carry

    def propagated(pop, rim, x):
        result = [pop[0, x + 1]] + [None] * 25
        result[19] = pop[19, x + 1]
        for i in range(1, 26):
            if i == 19:
                continue
            solid = table[i if i < 19 else i - 19, x] > 0.5
            back = pop[OPPOSITE[i], x + 1]
            if i == 24:
                back = jnp.where(lane == 0, -back, back)
            elif i == 25:
                back = jnp.where(lane == nz - 1, -back, back)
            result[i] = jnp.where(solid, back, pull(pop, rim, i, i, x))
        result[RISING] = result[RISING] + plate[x]
        return result

    wait_for(tiles.at[pl.ds(1, n - 1)], all_got.at[0])

    def fill_hot(pair, carry):
        high, low = hot(joined(tiles, pair))
        high_hot[pair] = high
        low_hot[pl.ds(pl.multiple_of(pair * nz, nz), nz), :] = low.T.astype(jnp.bfloat16)
        return carry

    lax.fori_loop(0, n // 2, fill_hot, 0)


    own.wait()
    wait_for(start.at[:, pl.ds(0, (n_st - 1) * planes)], check_got)

    def begin(first, second, carry, base):
        done = [collide([start[i, x] for i in range(26)]) for x in (first, second)]
        for x, (post, values) in zip((first, second), done):
            keep(pops.at[0], 0, same, post, x, base)
            remember(0, x, values)
        return carry

    whole_step(begin, 0, pops.at[0], 0, same)

    adj_copy.wait()

    def adj_rows(x, carry):
        pack_rows(ROUND_ADJ, opposite, lambda j: adj[j, x], x, 16)
        return carry

    lax.fori_loop(0, bx, adj_rows, 0)
    pack_planes(ROUND_ADJ, opposite, lambda j: adj[j, bx - 1], lambda j: adj[j, 0])
    for group in range(2):
        send_group(ROUND_ADJ, group)

    def forward(k, carry):
        now = lax.rem(k, 2)
        old, new, rim = pops.at[1 - now], pops.at[now], rims.at[1 - now]

        def advance(first, second, carry, base):
            done = [collide(propagated(old, rim, x)) for x in (first, second)]
            for x, (post, values) in zip((first, second), done):
                keep(new, k, same, post, x, base)
                remember(k, x, values)
            return carry

        return fed_step(advance, carry, old, rim, k - 1, same, new)

    lax.fori_loop(1, STEPS, forward, 0)

    last, rim = pops.at[(STEPS - 1) % 2], rims.at[(STEPS - 1) % 2]

    def finish(first, second, total, base):
        return finish_plane(second, finish_plane(first, total))

    def finish_plane(x, total):
        _, _, _, uz, temper = moments_of(propagated(last, rim, x))
        fluid = 1.0 - mask_x[x + 1]
        warm = fluid * temper
        rise = fluid * uz
        seed[0, x] = warm
        seed[1, x] = rise
        seed_out[4, pl.ds(x, 1), :] = warm[by - 1:by]
        seed_out[5, pl.ds(x, 1), :] = rise[by - 1:by]
        seed_out[6, pl.ds(x, 1), :] = warm[0:1]
        seed_out[7, pl.ds(x, 1), :] = rise[0:1]
        return total + warm * uz

    flux = fed_step(finish, jnp.zeros((by, nz), jnp.float32), last, rim, STEPS - 1, same)
    heat[0] = jnp.sum(flux, 0, keepdims=True)
    send_all(heat, 1)
    seed_out[0] = seed[0, bx - 1]
    seed_out[1] = seed[1, bx - 1]
    seed_out[2] = seed[0, 0]
    seed_out[3] = seed[1, 0]
    send(FACES, seed_out, seed_in, seed_sent, seed_got)
    for group in range(2):
        wait_group(ROUND_ADJ, group)
    wait_for(seed_in, seed_got)
    wait_for(heat.at[pl.ds(1, n - 1)], all_got.at[1])
    heat_sum = jnp.sum(jnp.sum(heat[...], 0), 1, keepdims=True)
    nusselt = 1.0 + heat_sum / (KAPPA * (bx * n_gx * by * n_st))
    nu[...] = jnp.broadcast_to(nusselt, nu.shape)
    gain = jnp.broadcast_to(nusselt - 1.0, (by, nz))

    def seeded(j, warm, rise):
        if j >= 19:
            return gain * rise
        if VELOCITY[j][2] == 0:
            return jnp.zeros((by, nz), jnp.float32)
        return gain * warm if VELOCITY[j][2] == 1 else -(gain * warm)

    def bed_of(value, x):
        return jnp.where(lane == bx * sub + x, 0.25 * value[:, 0:1], 0.0)

    def seed_adjoint(x, total):
        warm = seed[0, x]
        rise = seed[1, x]
        for j in range(26):
            value = adj[j, x] + seeded(j, warm, rise)
            pops[0, j, x + 1] = value
            if j == RISING:
                total = total + bed_of(value, x)
        return total

    total = lax.fori_loop(0, bx, seed_adjoint, jnp.zeros((by, nz), jnp.float32))

    def arrived_seed(j, side):
        return seeded(j, seed_in[2 * side], seed_in[2 * side + 1])

    unpack_far(ROUND_ADJ, opposite, pops.at[0], rims.at[0], arrived_seed)
    for side, rows_of, base in ((2, Y_UP, 16), (3, Y_DOWN, 22)):
        for k, i in enumerate(rows_of):
            j = OPPOSITE[i]
            rims[0, j, 1:bx + 1, :] = msg_in[ROUND_ADJ, base + k] + arrived_seed(j, side)

    def pulled_back(pop, rim, x):
        fluid = 1.0 - mask_x[x + 1]
        above = jnp.where(lane == 0, 0.0, fluid)
        below = jnp.where(lane == nz - 1, 0.0, fluid)
        mu = [None] * 26
        mu[0] = pop[0, x + 1]
        mu[19] = pop[19, x + 1]
        for i in range(1, 26):
            if i == 19:
                continue
            step_z = VELOCITY[i][2]
            share = fluid if step_z == 0 else (above if step_z == 1 else below)
            bounce = table[i if i < 19 else i - 19, x]
            if i == 24:
                bounce = jnp.where(lane == 0, -1.0, bounce)
            elif i == 25:
                bounce = jnp.where(lane == nz - 1, -1.0, bounce)
            mu[OPPOSITE[i]] = share * pull(pop, rim, OPPOSITE[i], i, x) + bounce * pop[i, x + 1]
        return mu

    def collide_back(mu, k, x):
        ux = moments[k, 0, x]
        uy = moments[k, 1, x]
        uz = moments[k, 2, x]
        temper = moments[k, 3, x]
        vz = uz + LIFT * (temper - MEAN_TEMP)
        even = {}
        odd = {}
        for i in range(1, 19, 2):
            even[i] = mu[i] + mu[i + 1]
            odd[i] = mu[i] - mu[i + 1]
        axis = OMEGA * WEIGHTS[1]
        diag = OMEGA * WEIGHTS[7]
        xy = diag * (even[7] + even[9])
        xz = diag * (even[11] + even[13])
        yz = diag * (even[15] + even[17])
        ex, ey, ez = axis * even[1], axis * even[3], axis * even[5]
        zero = (OMEGA * WEIGHTS[0]) * mu[0] + ((ex + ey) + (ez + xy)) + (xz + yz)
        sxx = ex + (xy + xz)
        syy = ey + (xy + yz)
        szz = ez + (xz + yz)
        sxy = diag * (even[7] - even[9])
        sxz = diag * (even[11] - even[13])
        syz = diag * (even[15] - even[17])
        one_x = axis * odd[1] + diag * ((odd[7] + odd[9]) + (odd[11] + odd[13]))
        one_y = axis * odd[3] + diag * ((odd[7] - odd[9]) + (odd[15] + odd[17]))
        one_z = axis * odd[5] + diag * ((odd[11] - odd[13]) + (odd[15] - odd[17]))
        bar_x = 3.0 * (one_x - zero * ux) + 9.0 * (sxx * ux + sxy * uy + sxz * vz)
        bar_y = 3.0 * (one_y - zero * uy) + 9.0 * (sxy * ux + syy * uy + syz * vz)
        bar_z = 3.0 * (one_z - zero * vz) + 9.0 * (sxz * ux + syz * uy + szz * vz)
        share = OMEGA * WEIGHTS[20]
        hx = (4.0 * share) * (mu[20] - mu[21])
        hy = (4.0 * share) * (mu[22] - mu[23])
        hz = (4.0 * share) * (mu[24] - mu[25])
        warm = (OMEGA * WEIGHTS[19]) * mu[19] + share * (
            ((mu[20] + mu[21]) + (mu[22] + mu[23])) + (mu[24] + mu[25]))
        bar_t = warm + (hx * ux + hy * uy + hz * uz) + LIFT * bar_z
        bar_x = bar_x + temper * hx
        bar_y = bar_y + temper * hy
        bar_z = bar_z + temper * hz
        lam = [None] * 26
        lam[0] = (1.0 - OMEGA) * mu[0] + zero
        for i in range(1, 19, 2):
            cb = along(VELOCITY[i], bar_x, bar_y, bar_z)
            lam[i] = (1.0 - OMEGA) * mu[i] + (zero + cb)
            lam[i + 1] = (1.0 - OMEGA) * mu[i + 1] + (zero - cb)
        for i in range(19, 26):
            lam[i] = (1.0 - OMEGA) * mu[i] + bar_t
        return lam

    def backward(step, total, fed=True):
        now = lax.rem(step, 2)
        old, new, rim = pops.at[now], pops.at[1 - now], rims.at[now]
        k = STEPS - 1 - step
        r = ROUND_ADJ + step

        def retreat(first, second, total, base):
            done = [collide_back(pulled_back(old, rim, x), k, x) for x in (first, second)]
            for x, values in zip((first, second), done):
                keep(new, r + 1, opposite, values, x, base)
                total = total + bed_of(values[RISING], x)
            return total

        if fed:
            return fed_step(retreat, total, old, rim, r, opposite, new)
        return whole_step(retreat, total, new, r + 1, opposite)

    total = backward(0, total, False)
    total = lax.fori_loop(1, STEPS - 1, backward, total)

    grads[0] = jnp.sum(total, 0, keepdims=True)
    send_all(grads, 2)

    def update_tiles():
        wait_for(grads.at[pl.ds(1, n - 1)], all_got.at[2])
        rows = theta_ref.shape[0]
        pairs = n // 2
        part = 16 if pairs % 16 == 0 else pairs

        def gather_tiles(chunk, total):
            weighted = [split(high_hot[chunk * part + p] * joined(grads, chunk * part + p))
                        for p in range(part)]
            low = low_hot[pl.ds(pl.multiple_of(chunk * (part * nz), nz), part * nz), :]
            return total + jnp.dot(jnp.concatenate(weighted, 1), low,
                                   preferred_element_type=jnp.float32)

        tile_grad = add_up(lax.fori_loop(0, pairs // part, gather_tiles,
                                            jnp.zeros((3 * rows, nz), jnp.float32)))
        first = BETA_ONE * first_ref[...] + (1.0 - BETA_ONE) * tile_grad
        second = BETA_TWO * second_ref[...] + (1.0 - BETA_TWO) * tile_grad * tile_grad
        first_hat = first / (1.0 - BETA_ONE**ADAM_STEP)
        second_hat = second / (1.0 - BETA_TWO**ADAM_STEP)
        first_new[...] = first
        second_new[...] = second
        theta_new[...] = theta_ref[...] - LEARN_RATE * first_hat / (jnp.sqrt(second_hat) + ADAM_EPS)

    old, rim = pops.at[(STEPS - 1) % 2], rims.at[(STEPS - 1) % 2]

    def end(first, second, carry, base):
        done = [collide_back(pulled_back(old, rim, x), 0, x) for x in (first, second)]
        for x, values in zip((first, second), done):
            for i in range(26):
                lam[i, x] = values[i]
        return carry

    fed_step(end, 0, old, rim, ROUND_ADJ + STEPS - 1, opposite, between=update_tiles)

    wait_for(start.at[:, pl.ds(0, (n_st - 1) * planes)], check_sent)
    wait_for(flag_out, flag_sent)
    wait_for(seed_out, seed_sent)
    for r in range(ROUNDS):
        count = 28 if r == ROUND_ADJ else 40
        wait_for(msg_out.at[r, pl.ds(0, count)], msg_sent.at[r])
    wait_for(tiles.at[pl.ds(1, n - 1)], all_sent.at[0])
    wait_for(heat.at[pl.ds(1, n - 1)], all_sent.at[1])
    wait_for(grads.at[pl.ds(1, n - 1)], all_sent.at[2])


def deliver(lam, theta_new, first_new, second_new, nu, lam_out, theta_out, first_out, second_out, nu_out,
            scalar, sem):
    scalar[...] = nu[0:1, 0:1]
    pairs = ((lam, lam_out), (theta_new, theta_out), (first_new, first_out),
             (second_new, second_out), (scalar, nu_out))
    copies = [pltpu.make_async_copy(source, into, sem.at[k]) for k, (source, into) in enumerate(pairs)]
    for copy in copies:
        copy.start()
    for copy in copies:
        copy.wait()


def body(n_gx, n_st, checkpoint, adjoint_in, solid_mask, tile_map, theta, first_moment, second_moment):
    bx, by, nz = solid_mask.shape
    planes = checkpoint.shape[1]
    n = n_gx * n_st
    rows = theta.shape[0] // nz
    f32 = jnp.float32
    wide = 16
    vmem = pl.BlockSpec(memory_space=pltpu.VMEM)
    hbm = pl.BlockSpec(memory_space=pltpu.HBM)
    dma = pltpu.SemaphoreType.DMA
    small = jax.ShapeDtypeStruct((rows, nz), f32)
    shapes = (jax.ShapeDtypeStruct((26, bx, by, nz), f32), small, small, small,
              jax.ShapeDtypeStruct((1, 1), f32))
    results = pl.pallas_call(
        functools.partial(kernel, n_gx, n_st, planes),
        out_shape=tuple(pltpu.VMEM(value.shape, f32) for value in shapes[:4]) + (
            pltpu.VMEM((by, nz), f32),),
        in_specs=[hbm] * 7,
        out_specs=(vmem,) * 5,
        scratch_shapes=[
            pltpu.VMEM((bx, by, nz), jnp.int32),
            pltpu.VMEM((bx, by), jnp.int32),
            pltpu.VMEM((rows, nz), f32),
            pltpu.VMEM((rows, nz), f32),
            pltpu.VMEM((rows, nz), f32),
            pltpu.VMEM((26, bx, by, nz), f32),
            pltpu.VMEM((26, bx, by, nz), f32),
            pltpu.VMEM((2, 26, bx + 2, by, nz), f32),
            pltpu.VMEM((2, 26, wide, nz), f32),
            pltpu.VMEM((STEPS, 4, bx, by, nz), f32),
            pltpu.VMEM((19, bx, by, nz), f32),
            pltpu.VMEM((bx, by, nz), f32),
            pltpu.VMEM((ROUNDS, 40, by, nz), f32),
            pltpu.VMEM((ROUNDS, 40, by, nz), f32),
            pltpu.VMEM((8, by, nz), f32),
            pltpu.VMEM((8, by, nz), f32),
            pltpu.VMEM((8, by, nz), f32),
            pltpu.VMEM((8, by, nz), f32),
            pltpu.VMEM((2, bx, by, nz), f32),
            pltpu.VMEM((bx + 2, by, nz), f32),
            pltpu.VMEM((wide, nz), f32),
            pltpu.VMEM((wide, nz), f32),
            pltpu.VMEM((n, 1, nz), f32),
            pltpu.VMEM((n, 1, nz), f32),
            pltpu.VMEM((n, 1, nz), f32),
            pltpu.VMEM((n // 2 * nz, nz), jnp.bfloat16),
            pltpu.VMEM((n // 2, rows, nz), f32),
            dma((ROUNDS,)),
            dma((ROUNDS, 3)),
            dma,
            dma,
            dma,
            dma,
            dma((3,)),
            dma((3,)),
            dma,
            dma,
            dma,
            dma,
            dma((5,)),
        ],
        compiler_params=pltpu.CompilerParams(
            collective_id=0, has_side_effects=True, vmem_limit_bytes=40 * 1024 * 1024),
        name="window",
    )(*(pltpu.with_memory_space_constraint(value, pltpu.HBM) for value in (
        checkpoint, adjoint_in, solid_mask, tile_map, theta.reshape(rows, nz),
        first_moment.reshape(rows, nz), second_moment.reshape(rows, nz))))
    adjoint_out, theta_new, first_new, second_new, nusselt = pl.pallas_call(
        deliver,
        out_shape=shapes,
        in_specs=[vmem] * 5,
        out_specs=(hbm,) * 5,
        scratch_shapes=[pltpu.VMEM((1, 1), f32), dma((5,))],
        name="deliver",
    )(*(pltpu.with_memory_space_constraint(value, pltpu.VMEM) for value in results))
    flat = theta.shape
    return (adjoint_out, theta_new.reshape(flat), first_new.reshape(flat),
            second_new.reshape(flat), nusselt.reshape(()))


def solution(mesh):
    return jax.shard_map(
        functools.partial(body, mesh.shape["gx"], mesh.shape["st"]),
        mesh=mesh,
        in_specs=(
            P(None, ("gx", "st"), None, None),
            P(None, "gx", "st", None),
            P("gx", "st", None),
            P("gx", "st"),
            P(),
            P(),
            P(),
        ),
        out_specs=(P(None, "gx", "st", None), P(), P(), P(), P()),
        check_vma=False,
    )
```
